32 devices in a mesh: dp: 16 (over z, y, x), tensor: 2 (over core).
Axes of the slice: x: 2, y: 2, z: 4, core: 2. Of those that a mesh axis runs over, the one named last changes fastest.
Arguments:
- resid: bfloat16 [32768, 768], P(('dp', 'tensor')), may hold values from -6 to 6
- gain_in: float32 [768], replicated, may hold values from 0.5 to 1.5
- w_z: bfloat16 [768, 1536], P('dp', 'tensor'), may hold values from -0.21875 to 0.21875
- w_x: bfloat16 [768, 1536], P('dp', 'tensor'), may hold values from -0.21875 to 0.21875
- w_bc: bfloat16 [768, 256], P('dp'), may hold values from -0.21875 to 0.21875
- w_dt: bfloat16 [768, 24], P('dp', 'tensor'), may hold values from -0.21875 to 0.21875
- conv_x: float32 [4, 1536], P(None, 'tensor'), may hold values from -3 to 3
- bias_x: float32 [1536], P('tensor'), may hold values from -0.5 to 0.5
- conv_bc: float32 [4, 256], replicated, may hold values from -3 to 3
- bias_bc: float32 [256], replicated, may hold values from -0.5 to 0.5
- dt_bias: float32 [24], P('tensor'), may hold values from -6.5 to -2.5
- a_log: float32 [24], P('tensor'), may hold values from 0 to 2.5
- d_skip: float32 [24], P('tensor'), may hold values from 0.5 to 1.5
- gain_out: float32 [1536], P('tensor'), may hold values from 0.5 to 1.5
- w_out: bfloat16 [1536, 768], P('tensor', 'dp'), may hold values from -0.15625 to 0.15625
- cotangent: bfloat16 [32768, 768], P(('dp', 'tensor')), may hold values from -6 to 6
Outputs:
- block_out: bfloat16 [32768, 768], P(('dp', 'tensor'))
- grad_resid: float32 [32768, 768], P(('dp', 'tensor'))
- grad_gain_in: float32 [768], replicated
- grad_w_z: float32 [768, 1536], P('dp', 'tensor')
- grad_w_x: float32 [768, 1536], P('dp', 'tensor')
- grad_w_bc: float32 [768, 256], P('dp')
- grad_w_dt: float32 [768, 24], P('dp', 'tensor')
- grad_conv_x: float32 [4, 1536], P(None, 'tensor')
- grad_bias_x: float32 [1536], P('tensor')
- grad_conv_bc: float32 [4, 256], replicated
- grad_bias_bc: float32 [256], replicated
- grad_dt_bias: float32 [24], P('tensor')
- grad_a_log: float32 [24], P('tensor')
- grad_d_skip: float32 [24], P('tensor')
- grad_gain_out: float32 [1536], P('tensor')
- grad_w_out: float32 [1536, 768], P('tensor', 'dp')
The draws below stay inside these ranges and needn't reach their ends.
All inputs are finite; a program needn't handle non-finite values.
Results may differ from the reference program's by a relative error of at most 0.012.
The reference program's roundings to bfloat16 on the way count: a program that leaves them out, or rounds other values in their place, can miss the bound.
Values may be sent and summed in bfloat16 or wider, within the bound.
No kernel may reach another device: no remote copies, remote signals or barrier semaphores. Data moves between devices by JAX's collectives and lax.ppermute only.
A program may use at most 192 MiB of HBM per device.

```python
import jax
import jax.numpy as jnp
from jax import lax

D = 768
H = 24
NS = 128
KW = 4
GROUP = 256
SEQ_LEN = 2048
E = 1536
TOKENS = 32768


def level_of(key, shape, shards, smallest, high):
    def one(position, blocks):
        draws = jax.random.uniform(jax.random.fold_in(jax.random.fold_in(key, 6), position), (blocks,), jnp.float32, smallest / len(shards), high / len(shards))
        return jnp.repeat(jnp.exp(draws), shape[position] // blocks).reshape((-1,) + (1,) * (len(shape) - position - 1))

    loudness = one(*shards[0])
    for cut in shards[1:]:
        loudness = loudness * one(*cut)
    return loudness


def normal_values(own_key, extent, width, limit, shards=(), held_as=jnp.bfloat16):
    result = width * jax.random.normal(own_key, extent, jnp.float32)
    if shards:
        result = result * level_of(own_key, extent, shards, -0.22, 0.18)
    return jnp.clip(result, -limit, limit).astype(held_as)


def setup_inputs(seed: int = 0) -> dict:
    arg_keys = jax.random.split(jax.random.key(seed), 17)
    resid = normal_values(arg_keys[0], (TOKENS, D), 1.0, 6.0, ((0, 32),))
    gain_in = jnp.clip(1.0 + 0.1 * jax.random.normal(arg_keys[1], (D,), jnp.float32), 0.5, 1.5)
    w_z = normal_values(arg_keys[2], (D, E), D ** -0.5, 0.21875, ((0, 16), (1, 2)))
    w_x = normal_values(arg_keys[3], (D, E), D ** -0.5, 0.21875, ((0, 16), (1, 2)))
    w_bc = normal_values(arg_keys[4], (D, 2 * NS), D ** -0.5, 0.21875, ((0, 16),))
    w_dt = normal_values(arg_keys[5], (D, H), D ** -0.5, 0.21875, ((0, 16), (1, 2)))
    conv_x = normal_values(arg_keys[6], (KW, E), KW ** -0.5, 3.0, ((1, 2),), jnp.float32)
    bias_x = jnp.clip(jax.random.uniform(arg_keys[7], (E,), jnp.float32, -0.5, 0.5) * level_of(arg_keys[7], (E,), ((0, 2),), -0.4, 0.0), -0.5, 0.5)
    conv_bc = normal_values(arg_keys[8], (KW, 2 * NS), KW ** -0.5, 3.0, (), jnp.float32)
    bias_bc = jnp.clip(jax.random.uniform(arg_keys[9], (2 * NS,), jnp.float32, -0.5, 0.5), -0.5, 0.5)
    dt_bias = jnp.clip(-6.5 + 4.0 * jax.random.uniform(arg_keys[10], (H,), jnp.float32) ** level_of(arg_keys[10], (H,), ((0, 2),), -0.2, 0.2), -6.5, -2.5)
    a_log = jnp.clip(2.5 * jax.random.uniform(arg_keys[11], (H,), jnp.float32) ** level_of(arg_keys[11], (H,), ((0, 2),), -0.2, 0.2), 0.0, 2.5)
    d_skip = jnp.clip(0.5 + 1.0 * jax.random.uniform(arg_keys[12], (H,), jnp.float32) ** level_of(arg_keys[12], (H,), ((0, 2),), -0.2, 0.2), 0.5, 1.5)
    gain_out = jnp.clip(1.0 + 0.1 * jax.random.normal(arg_keys[13], (E,), jnp.float32), 0.5, 1.5)
    w_out = normal_values(arg_keys[14], (E, D), E ** -0.5, 0.15625, ((0, 2), (1, 16)))
    cotangent = normal_values(arg_keys[15], (TOKENS, D), 1.0, 6.0, ((0, 32),))
    return dict(resid=resid, gain_in=gain_in, w_z=w_z, w_x=w_x, w_bc=w_bc, w_dt=w_dt, conv_x=conv_x, bias_x=bias_x, conv_bc=conv_bc, bias_bc=bias_bc, dt_bias=dt_bias, a_log=a_log, d_skip=d_skip, gain_out=gain_out, w_out=w_out, cotangent=cotangent)


@jax.custom_vjp
def low(v):
    return lax.optimization_barrier(v.astype(jnp.bfloat16)).astype(jnp.float32)

@jax.custom_vjp
def low_back(v):
    return v

def low_keep(v):
    return (low(v), None)

def low_pass(kept, grad):
    return (grad,)

def back_keep(v):
    return (v, None)

def back_low(kept, grad):
    return (low(grad),)
low.defvjp(low_keep, low_pass)
low_back.defvjp(back_keep, back_low)
highest = lax.Precision.HIGHEST
eps = 1e-05

def conv_silu(values, kernel, offset_bias):
    taps = kernel.shape[0]
    seq_length = values.shape[1]
    padded = jnp.pad(values, ((0, 0), (taps - 1, 0), (0, 0)))
    summed = jnp.zeros_like(values) + offset_bias[None, None, :]
    for offset in range(taps):
        summed = summed + kernel[offset][None, None, :] * padded[:, offset:offset + seq_length, :]
    return jax.nn.silu(summed)

def state_space(values, steps_pos, a_log, b_rows, c_rows, d_skip, block_len):
    seq_length, head_count, head_width = values.shape
    block_count = seq_length // block_len
    rates = (steps_pos * (-jnp.exp(a_log))[None, :]).reshape(block_count, block_len, head_count)
    within = jnp.cumsum(rates, axis=1)
    scaled = (values * steps_pos[:, :, None]).reshape(block_count, block_len, head_count, head_width)
    b_blocks = b_rows.reshape(block_count, block_len, -1)
    c_blocks = c_rows.reshape(block_count, block_len, -1)
    order = jnp.arange(block_len)
    lower_mask = order[:, None] >= order[None, :]
    differences = within[:, :, None, :] - within[:, None, :, :]
    decays = jnp.exp(jnp.where(lower_mask[None, :, :, None], differences, -1e+30))
    intersection = jnp.einsum('ctn,csn->cts', c_blocks, b_blocks, precision=highest)
    inside = jnp.einsum('cts,ctsh,cshp->cthp', intersection, decays, scaled, precision=highest)
    tails = jnp.exp(within[:, -1:, :] - within)
    states = jnp.einsum('csn,csh,cshp->chnp', b_blocks, tails, scaled, precision=highest)
    totals = within[:, -1, :]
    ends = jnp.cumsum(totals, axis=0)
    block_order = jnp.arange(block_count)
    earlier = block_order[:, None] > block_order[None, :]
    spans = ends[:, None, :] - totals[:, None, :] - ends[None, :, :]
    carried = jnp.exp(jnp.where(earlier[:, :, None], spans, -1e+30))
    entering = jnp.einsum('cdh,dhnp->chnp', carried, states, precision=highest)
    outside = jnp.einsum('ctn,cth,chnp->cthp', c_blocks, jnp.exp(within), entering, precision=highest)
    joined = (inside + outside).reshape(seq_length, head_count, head_width)
    return joined + d_skip[None, :, None] * values

def mixer_block(resid, gain_in, w_z, w_x, w_bc, w_dt, conv_x, bias_x, conv_bc, bias_bc, dt_bias, a_log, d_skip, gain_out, w_out):
    seq_length = resid.shape[0]
    head_count = a_log.shape[0]
    inv_rms = lax.rsqrt(lax.optimization_barrier(jnp.mean(resid * resid, axis=1, keepdims=True)) + eps)
    normed = low(resid * inv_rms * gain_in[None, :])
    gate_proj = low_back(low(jnp.dot(normed, w_z, precision=highest)))
    inner_proj = low_back(low(jnp.dot(normed, w_x, precision=highest)))
    shared_proj = low_back(low(jnp.dot(normed, w_bc, precision=highest)))
    step_raw = low_back(jnp.dot(normed, w_dt, precision=highest))
    conv_inner = low(conv_silu(inner_proj[None], conv_x, bias_x)[0])
    conv_shared = low(conv_silu(shared_proj[None], conv_bc, bias_bc)[0])
    steps_pos = jax.nn.softplus(step_raw + dt_bias[None, :])
    values = conv_inner.reshape(seq_length, head_count, -1)
    mixed = state_space(values, steps_pos, a_log, conv_shared[:, :NS], conv_shared[:, NS:], d_skip, GROUP)
    gated = mixed.reshape(seq_length, -1) * jax.nn.silu(gate_proj)
    out_scale = lax.rsqrt(lax.optimization_barrier(jnp.mean(gated * gated, axis=1, keepdims=True)) + eps)
    normed_out = low(gated * out_scale * gain_out[None, :])
    return resid + jnp.dot(normed_out, w_out, precision=highest)

def reference(resid, gain_in, w_z, w_x, w_bc, w_dt, conv_x, bias_x, conv_bc, bias_bc, dt_bias, a_log, d_skip, gain_out, w_out, cotangent):
    params = tuple((item.astype(jnp.float32) for item in (gain_in, w_z, w_x, w_bc, w_dt, conv_x, bias_x, conv_bc, bias_bc, dt_bias, a_log, d_skip, gain_out, w_out)))

    def forward(resid_all, *weights):
        sequences = resid_all.reshape(-1, SEQ_LEN, resid_all.shape[1])

        def one_sequence(seq_rows):
            return mixer_block(seq_rows, *weights)
        return lax.map(jax.checkpoint(one_sequence), sequences).reshape(resid_all.shape)
    output, pullback = jax.vjp(forward, resid.astype(jnp.float32), *params)
    grads = pullback(cotangent.astype(jnp.float32))
    g_resid, g_gain_in, g_w_z, g_w_x, g_w_bc, g_w_dt, g_conv_x, g_bias_x, g_conv_bc, g_bias_bc, g_dt_bias, g_a_log, g_d_skip, g_gain_out, g_w_out = grads
    return (output.astype(jnp.bfloat16), g_resid, g_gain_in, g_w_z, g_w_x, g_w_bc, g_w_dt, g_conv_x, g_bias_x, g_conv_bc, g_bias_bc, g_dt_bias, g_a_log, g_d_skip, g_gain_out, g_w_out)
```

```python
import functools

import jax
import jax.numpy as jnp
from jax import lax
from jax.experimental import pallas as pl
from jax.experimental.pallas import tpu as pltpu
from jax.sharding import PartitionSpec as P

NS = 128
L = 256
SEQ_LEN = 2048
HEAD = 64
LANES = 128
VMEM = 52 * 1024 * 1024

f32 = jnp.float32
bf16 = jnp.bfloat16
highest = lax.Precision.HIGHEST
eps = 1e-05

NN = (((1,), (0,)), ((), ()))
NT = (((1,), (1,)), ((), ()))
TN = (((0,), (0,)), ((), ()))


def mm(a, b, dims=NN, precision=None):
    return lax.dot_general(a, b, dims, precision=precision, preferred_element_type=f32)


def iota(shape, dim):
    return lax.broadcasted_iota(jnp.int32, shape, dim)


def lower_tri():
    return (iota((L, L), 0) >= iota((L, L), 1)).astype(f32)


def upper_tri():
    return (iota((L, L), 0) <= iota((L, L), 1)).astype(f32)


def expander(heads):
    rows = iota((LANES, heads * HEAD), 0)
    cols = iota((LANES, heads * HEAD), 1) // HEAD
    return ((rows % 16 == cols) & (rows < 48)).astype(bf16)


def collector(heads):
    rows = iota((heads * HEAD, LANES), 0) // HEAD
    cols = iota((heads * HEAD, LANES), 1)
    return ((cols % 16 == rows) & (cols < 48)).astype(bf16)


def pack3(q):
    lane = iota(q.shape, 1)
    hi = q.astype(bf16).astype(f32)
    rest = q - hi
    mid = rest.astype(bf16).astype(f32)
    return jnp.where(lane < 16, hi, jnp.where(lane < 32, mid, rest - mid)).astype(bf16)


def head_sums(q, col):
    hi = q.astype(bf16)
    lo = (q - hi.astype(f32)).astype(bf16)
    return mm(hi, col) + mm(lo, col)


def softplus(v):
    return jnp.maximum(v, 0.0) + jnp.log1p(jnp.exp(-jnp.abs(v)))


def fold8(q):
    return jnp.sum(q.reshape(q.shape[0] // 8, 8, q.shape[1]), axis=0)


def scan_terms(step_raw, dtb, rate, expand):
    steps = softplus(step_raw + dtb)
    within = mm(lower_tri(), steps * rate, precision=highest)
    tails = jnp.exp(within[L - 1 : L, :] - within)
    steps_e = mm(pack3(steps), expand)
    grown_e = mm(pack3(jnp.exp(within)), expand)
    tails_e = mm(pack3(tails), expand)
    return steps, within, steps_e, grown_e, tails_e


def forward_kernel(
    place, own, oth, gin, w, conv, bias, dtb, rate, dsk, normed_o, xbc_o, step_o, mixed_o, sin_o,
    state, buf,
):
    c = pl.program_id(0)
    half = pl.num_programs(0) // 2
    width = dsk.shape[1]
    heads = width // HEAD
    cols = width + 2 * NS

    @pl.when(c == 0)
    def _():
        state[...] = jnp.zeros_like(state)
        buf[0:8, :] = jnp.zeros((8, cols), f32)

    mine = (c // half) == place[0]
    r = jnp.where(mine, own[...].astype(f32), oth[...].astype(f32))
    inv = lax.rsqrt(jnp.mean(r * r, axis=1, keepdims=True) + eps)
    normed = (r * inv * gin[...]).astype(bf16)
    normed_o[...] = normed
    proj = mm(normed, w[...])
    xbc = proj[:, :cols].astype(bf16)
    step_raw = proj[:, cols:]
    xbc_o[...] = xbc
    step_o[...] = step_raw
    buf[8:, :] = xbc.astype(f32)
    v = bias[...] + conv[3:4, :] * buf[8 : 8 + L, :]
    for k in range(3):
        v = v + conv[k : k + 1, :] * buf[5 + k : 5 + k + L, :]
    buf[0:8, :] = buf[L : L + 8, :]
    act = (v * jax.nn.sigmoid(v)).astype(bf16)
    x = act[:, :width].astype(f32)
    b = act[:, width : width + NS]
    cc = act[:, width + NS :]

    expand = expander(heads)
    steps, within, steps_e, grown_e, tails_e = scan_terms(step_raw, dtb[...], rate[...], expand)
    within_t = within.T
    scaled = x * steps_e
    scaled_b = scaled.astype(bf16)
    inter = mm(cc, b, NT)
    sin = state[...]
    sin_o[0] = sin
    outside = mm(cc, sin.astype(bf16)) * grown_e
    hl = L // 2
    tri = iota((hl, hl), 0) >= iota((hl, hl), 1)
    left = iota((hl, LANES), 1) < HEAD
    for pair in range(heads // 2):
        x2 = scaled_b[:, pair * LANES : (pair + 1) * LANES]
        tops, bots = [], []
        for h in (2 * pair, 2 * pair + 1):
            wc = within[:, h : h + 1]
            wr = within_t[h : h + 1, :]
            d_tl = jnp.exp(jnp.where(tri, wc[:hl] - wr[:, :hl], -1e30))
            d_bl = jnp.exp(wc[hl:] - wr[:, :hl])
            d_br = jnp.exp(jnp.where(tri, wc[hl:] - wr[:, hl:], -1e30))
            m_tl = (inter[:hl, :hl] * d_tl).astype(bf16)
            m_bl = (inter[hl:, :hl] * d_bl).astype(bf16)
            m_br = (inter[hl:, hl:] * d_br).astype(bf16)
            tops.append(mm(m_tl, x2[:hl]))
            bots.append(mm(m_bl, x2[:hl]) + mm(m_br, x2[hl:]))
        ps = slice(pair * LANES, (pair + 1) * LANES)
        skip = dsk[:, ps] * x[:, ps] + outside[:, ps]
        mixed_o[:hl, ps] = jnp.where(left, tops[0], tops[1]) + skip[:hl]
        mixed_o[hl:, ps] = jnp.where(left, bots[0], bots[1]) + skip[hl:]
    state[...] = sin * grown_e[L - 1 : L, :] + mm(b, (scaled * tails_e).astype(bf16), TN)


def gate_kernel(place, cown, coth, normed, mixed, w, gout, gate_o, gno_o, sums_o):
    c = pl.program_id(0)
    half = pl.num_programs(0) // 2
    width = gout.shape[1]
    mine = (c // half) == place[0]
    cot = jnp.where(mine, cown[...].astype(f32), coth[...].astype(f32)).astype(bf16)
    gate = mm(normed[...], w[:, :width]).astype(bf16)
    gate_o[...] = gate
    gf = gate.astype(f32)
    gated = mixed[...] * (gf * jax.nn.sigmoid(gf))
    gno = mm(cot, w[:, width:])
    gno_o[...] = gno
    squares = jnp.sum(gated * gated, axis=1, keepdims=True)
    products = jnp.sum(gno * gout[...] * gated, axis=1, keepdims=True)
    lane = iota((L, LANES), 1)
    sums_o[...] = jnp.where(lane < 64, squares, products)


def gate_back_kernel(
    place, cown, coth, normed, mixed, gate, gno, sown, soth, w, gout, branch_o, ggate_o, gm_o,
    gw_o, ggo_o, acc_z, acc_o, acc_g,
):
    c = pl.program_id(0)
    last = pl.num_programs(0) - 1
    half = pl.num_programs(0) // 2
    width = gout.shape[1]

    @pl.when(c == 0)
    def _():
        acc_z[...] = jnp.zeros_like(acc_z)
        acc_o[...] = jnp.zeros_like(acc_o)
        acc_g[...] = jnp.zeros_like(acc_g)

    mine = (c // half) == place[0]
    cot = jnp.where(mine, cown[...].astype(f32), coth[...].astype(f32)).astype(bf16)
    sums = sown[...] + soth[...]
    inner_total = 2.0 * width
    scale = lax.rsqrt(sums[:, 0:1] / inner_total + eps)
    coef = scale * scale * scale * (sums[:, 64:65] / inner_total)
    gf = gate[...].astype(f32)
    sig = jax.nn.sigmoid(gf)
    silu = gf * sig
    mix = mixed[...]
    gated = mix * silu
    grad = gno[...]
    normed_out = (gated * scale * gout[...]).astype(bf16)
    branch_o[...] = mm(normed_out, w[:, width:], NT).astype(bf16)
    acc_g[...] += fold8(grad * gated * scale)
    grad_gated = scale * (grad * gout[...]) - gated * coef
    grad_gate = (grad_gated * mix * sig * (1.0 + gf * (1.0 - sig))).astype(bf16)
    ggate_o[...] = grad_gate
    gm_o[...] = (grad_gated * silu).astype(bf16)
    acc_z[...] += mm(normed[...], grad_gate, TN)
    acc_o[...] += mm(cot, normed_out, TN)

    @pl.when(c == last)
    def _():
        gw_o[:, :width] = acc_z[...].astype(bf16)
        gw_o[:, width:] = acc_o[...].astype(bf16)
        ggo_o[...] = acc_g[...]


def scan_back_kernel(
    xbc, xprev, step, mixed, sin_r, gm, normed, conv, bias, dtb, rate, dsk,
    gx_o, gw_o, gconv_o, gskip_o, ghead_o,
    dstate, buf, dvbuf, acc_w, acc_c, acc_s, acc_h,
):
    i = pl.program_id(0)
    last = pl.num_programs(0) - 1
    c = last - i
    width = dsk.shape[1]
    heads = width // HEAD
    cols = width + 2 * NS

    @pl.when(i == 0)
    def _():
        dstate[...] = jnp.zeros_like(dstate)
        dvbuf[...] = jnp.zeros_like(dvbuf)
        acc_w[...] = jnp.zeros_like(acc_w)
        acc_c[...] = jnp.zeros_like(acc_c)
        acc_s[...] = jnp.zeros_like(acc_s)
        acc_h[...] = jnp.zeros_like(acc_h)

    buf[8:, :] = xbc[...].astype(f32)
    before = xprev[...].astype(f32)[8:, :]
    buf[0:8, :] = jnp.where(c == 0, 0.0, before)
    v = bias[...] + conv[3:4, :] * buf[8 : 8 + L, :]
    for k in range(3):
        v = v + conv[k : k + 1, :] * buf[5 + k : 5 + k + L, :]
    sig_v = jax.nn.sigmoid(v)
    act = (v * sig_v).astype(bf16)
    dsilu = sig_v * (1.0 + v * (1.0 - sig_v))
    x = act[:, :width].astype(f32)
    b = act[:, width : width + NS]
    cc = act[:, width + NS :]

    expand = expander(heads)
    collect = collector(heads)
    step_raw = step[...]
    steps, within, steps_e, grown_e, tails_e = scan_terms(step_raw, dtb[...], rate[...], expand)
    within_t = within.T
    scaled = x * steps_e
    scaled_b = scaled.astype(bf16)
    gmb = gm[...]
    gmf = gmb.astype(f32)
    sin = sin_r[0]
    ds = dstate[...]
    ds_b = ds.astype(bf16)
    inter_t = mm(b, cc, NT)
    state_part = mm(b, ds_b) * tails_e
    hl = L // 2
    tri = iota((hl, hl), 0) <= iota((hl, hl), 1)
    left = iota((hl, LANES), 1) < HEAD
    leftw = iota((L, LANES), 1) < HEAD
    dg_tl = jnp.zeros((hl, hl), f32)
    dg_tr = jnp.zeros((hl, hl), f32)
    dg_br = jnp.zeros((hl, hl), f32)
    dscaled = []
    for pair in range(heads // 2):
        ps = slice(pair * LANES, (pair + 1) * LANES)
        x2 = scaled_b[:, ps]
        g2 = gmb[:, ps]
        x2f = x2.astype(f32)
        tops, bots = [], []
        for h in (2 * pair, 2 * pair + 1):
            wc = within[:, h : h + 1]
            wr = within_t[h : h + 1, :]
            d_tl = jnp.exp(jnp.where(tri, wr[:, :hl] - wc[:hl], -1e30))
            d_tr = jnp.exp(wr[:, hl:] - wc[:hl])
            d_br = jnp.exp(jnp.where(tri, wr[:, hl:] - wc[hl:], -1e30))
            m_tl = (inter_t[:hl, :hl] * d_tl).astype(bf16)
            m_tr = (inter_t[:hl, hl:] * d_tr).astype(bf16)
            m_br = (inter_t[hl:, hl:] * d_br).astype(bf16)
            tops.append(mm(m_tl, g2[:hl]) + mm(m_tr, g2[hl:]))
            bots.append(mm(m_br, g2[hl:]))
            sel = leftw if h % 2 == 0 else jnp.logical_not(leftw)
            xm = jnp.where(sel, x2f, 0.0).astype(bf16)
            dg_tl += mm(xm[:hl], g2[:hl], NT) * d_tl
            dg_tr += mm(xm[:hl], g2[hl:], NT) * d_tr
            dg_br += mm(xm[hl:], g2[hl:], NT) * d_br
        dscaled.append(
            jnp.concatenate(
                [jnp.where(left, tops[0], tops[1]), jnp.where(left, bots[0], bots[1])], axis=0
            )
        )
    dscaled = jnp.concatenate(dscaled, axis=1) + state_part
    top = jnp.concatenate([dg_tl, dg_tr], axis=1)
    bot = jnp.concatenate([jnp.zeros((hl, hl), f32), dg_br], axis=1)
    dg = jnp.concatenate([top, bot], axis=0).astype(bf16)
    gm_grown = (gmf * grown_e).astype(bf16)
    dc = mm(dg, b, TN) + mm(gm_grown, sin.astype(bf16), NT)
    db = mm(dg, cc) + mm((scaled * tails_e).astype(bf16), ds_b, NT)
    scaled_f = scaled_b.astype(f32)
    y = mixed[...] - dsk[...] * x
    q = gmf * y - scaled_f * dscaled
    last_grown = grown_e[L - 1 : L, :]
    ends = jnp.sum(scaled_f * state_part, axis=0, keepdims=True) + last_grown * jnp.sum(
        sin * ds, axis=0, keepdims=True
    )
    ends_h = head_sums(jnp.broadcast_to(ends, (8, width)), collect)[0:1, :]
    d_rate = mm(upper_tri(), head_sums(q, collect), precision=highest) + ends_h
    d_steps = d_rate * rate[...] + head_sums(dscaled * x, collect)
    sig_s = jax.nn.sigmoid(step_raw + dtb[...])
    keep = iota((L, LANES), 1) < heads
    d_raw = jnp.where(keep, d_steps * sig_s, 0.0)
    acc_h[0:8, :] += fold8(d_raw)
    acc_h[8:16, :] += fold8(d_rate * steps * rate[...])
    acc_s[...] += fold8(gmf * x)
    dx = dscaled * steps_e + dsk[...] * gmf
    dstate[...] = ds * last_grown + mm(cc, gm_grown, TN)

    dv = jnp.concatenate([dx, db, dc], axis=1) * dsilu
    dvbuf[0:L, :] = dv
    acc_c[4] += fold8(dv)
    for k in range(4):
        acc_c[k] += fold8(dv * buf[5 + k : 5 + k + L, :])
    dxin = conv[3:4, :] * dv
    for k in range(3):
        dxin = dxin + conv[k : k + 1, :] * dvbuf[3 - k : 3 - k + L, :]
    dvbuf[L : L + 8, :] = dvbuf[0:8, :]
    gx_o[:, :cols] = dxin.astype(bf16)
    gx_o[:, cols:] = d_raw.astype(bf16)
    acc_w[...] += mm(normed[...], gx_o[...], TN)

    @pl.when(i == last)
    def _():
        gw_o[...] = acc_w[...].astype(bf16)
        gconv_o[...] = acc_c[...]
        gskip_o[...] = acc_s[...]
        ghead_o[...] = acc_h[...]


def input_back_kernel(place, own, oth, ggate, gx, wz, wx, dn_o, gain_o, acc):
    c = pl.program_id(0)
    half = pl.num_programs(0) // 2

    @pl.when(c == 0)
    def _():
        acc[...] = jnp.zeros_like(acc)

    mine = (c // half) == place[0]
    r = jnp.where(mine, own[...].astype(f32), oth[...].astype(f32))
    inv = lax.rsqrt(jnp.mean(r * r, axis=1, keepdims=True) + eps)
    width = ggate.shape[1]
    dn = mm(ggate[...], wz[:, :width], NT) + mm(gx[...], wx[...], NT)
    dn_o[...] = dn.astype(bf16)
    acc[...] += fold8(dn * r * inv)

    @pl.when(c == pl.num_programs(0) - 1)
    def _():
        gain_o[...] = acc[...]


def finish_kernel(resid, cot, gin, dn_own, dn_oth, br_own, br_oth, out_o, gres_o):
    r = resid[...].astype(f32)
    inv = lax.rsqrt(jnp.mean(r * r, axis=1, keepdims=True) + eps)
    out_o[...] = (r + (br_own[...].astype(f32) + br_oth[...].astype(f32))).astype(bf16)
    u = (dn_own[...].astype(f32) + dn_oth[...].astype(f32)) * gin[...]
    mean = jnp.mean(u * r, axis=1, keepdims=True)
    gres_o[...] = cot[...].astype(f32) + inv * u - r * (inv * inv * inv * mean)


def swap(v, bit, axis):
    size = lax.axis_size(axis)
    return lax.ppermute(v, axis, [(i, i ^ bit) for i in range(size)])


def gather_rows(v, bits, axis):
    me = lax.axis_index(axis)
    rows, cols = v.shape
    held = {0: v}
    for bit in bits:
        for slot in list(held):
            held[slot ^ bit] = swap(held[slot], bit, axis)
    stacked = jnp.stack([held[j] for j in range(len(held))])
    return stacked, me


def in_order(stacked, axis):
    size = lax.axis_size(axis)
    me = lax.axis_index(axis)
    count, rows, cols = stacked.shape
    bit = 1
    while bit < size:
        v = stacked.reshape(size // (2 * bit), 2, bit, rows, cols)
        stacked = jnp.where((me & bit) != 0, v[:, ::-1], v).reshape(size, rows, cols)
        bit *= 2
    return stacked.reshape(size * rows, cols)


def scatter_sum(g, bits, axis):
    size = lax.axis_size(axis)
    me = lax.axis_index(axis)
    rows = g.shape[0] // size
    left = sorted(bits, reverse=True)
    cur = g.reshape([2] * len(left) + [rows, g.shape[1]])
    for bit in bits:
        dim = left.index(bit)
        mine = ((me & bit) != 0).astype(jnp.int32)
        send = lax.dynamic_index_in_dim(cur, 1 - mine, dim, keepdims=False)
        keep = lax.dynamic_index_in_dim(cur, mine, dim, keepdims=False)
        got = swap(send.astype(bf16), bit, axis)
        cur = keep.astype(f32) + got.astype(f32)
        left.pop(dim)
    return cur.astype(f32)


def full(shape):
    zeros = (0,) * len(shape)
    return pl.BlockSpec(shape, lambda c, *_: zeros)


def rows_spec(count, width, index=lambda c: c):
    return pl.BlockSpec((count, width), lambda c, *_: (index(c), 0))


def params():
    return pltpu.CompilerParams(dimension_semantics=("arbitrary",), vmem_limit_bytes=VMEM)


def local(
    resid, gain_in, w_z, w_x, w_bc, w_dt, conv_x, bias_x, conv_bc, bias_bc, dt_bias, a_log, d_skip,
    gain_out, w_out, cotangent,
):
    size = lax.axis_size("dp")
    place = lax.axis_index("tensor")
    heads = a_log.shape[0]
    width = heads * HEAD
    dim = resid.shape[1]
    cols = width + 2 * NS
    half_rows = resid.shape[0]
    tokens = 2 * half_rows
    assert tokens == SEQ_LEN
    chunks = tokens // L
    half = chunks // 2
    shape = jax.ShapeDtypeStruct

    bits = []
    bit = size // 2
    while bit:
        bits.append(bit)
        bit //= 2
    order_a = bits
    order_b = bits[:-2] + bits[-2:][::-1]
    order_c = bits[-2:] + bits[:-2]

    def lanes3(v):
        pad = [(0, 0)] * (v.ndim - 1)
        group = jnp.pad(v, pad + [(0, 16 - heads)])
        return jnp.pad(jnp.concatenate([group] * 3, axis=-1), pad + [(0, LANES - 48)])

    resid_oth = swap(resid, 1, "tensor")
    cot_oth = swap(cotangent, 1, "tensor")
    first = jnp.concatenate([w_x, w_bc, lanes3(w_dt)], axis=1)
    second = jnp.concatenate([w_z, w_out.T], axis=1)

    def gather(v, cuts, orders):
        parts = []
        start = 0
        for stop, order in zip(cuts, orders):
            stacked, _ = gather_rows(v[:, start:stop], order, "dp")
            parts.append(stacked)
            start = stop
        return in_order(jnp.concatenate(parts, axis=2), "dp")

    wx = gather(first, (384, 768, 1152), (order_a, order_b, order_c))
    wz = gather(second, (640, 1280, 1536), (order_a, order_b, order_c))

    conv = jnp.concatenate([conv_x, conv_bc], axis=1)
    bias = jnp.concatenate([bias_x, bias_bc])[None]
    dtb = lanes3(dt_bias[None])
    rate = lanes3(-jnp.exp(a_log)[None])
    dsk = jnp.repeat(d_skip, HEAD)[None]
    gin = gain_in[None]
    gout = gain_out[None]
    place1 = place.astype(jnp.int32)[None]

    half_spec = rows_spec(L, dim, lambda c: c % half)
    wide = rows_spec(L, width)
    normed, xbc, step_raw, mixed, sin = pl.pallas_call(
        forward_kernel,
        grid_spec=pltpu.PrefetchScalarGridSpec(
            num_scalar_prefetch=1,
            grid=(chunks,),
            in_specs=[
                half_spec, half_spec, full((1, dim)), full((dim, cols + LANES)), full((4, cols)),
                full((1, cols)), full((1, LANES)), full((1, LANES)), full((1, width)),
            ],
            out_specs=[
                rows_spec(L, dim), rows_spec(L, cols), rows_spec(L, LANES), wide,
                pl.BlockSpec((1, NS, width), lambda c, *_: (c, 0, 0)),
            ],
            scratch_shapes=[pltpu.VMEM((NS, width), f32), pltpu.VMEM((L + 8, cols), f32)],
        ),
        out_shape=[
            shape((tokens, dim), bf16), shape((tokens, cols), bf16), shape((tokens, LANES), f32),
            shape((tokens, width), f32), shape((chunks, NS, width), f32),
        ],
        compiler_params=params(),
        name="mix_forward",
    )(place1, resid, resid_oth, gin, wx, conv, bias, dtb, rate, dsk)

    gate, gno, sums = pl.pallas_call(
        gate_kernel,
        grid_spec=pltpu.PrefetchScalarGridSpec(
            num_scalar_prefetch=1,
            grid=(chunks,),
            in_specs=[
                half_spec, half_spec, rows_spec(L, dim), wide, full((dim, 2 * width)),
                full((1, width)),
            ],
            out_specs=[wide, wide, rows_spec(L, LANES)],
        ),
        out_shape=[
            shape((tokens, width), bf16), shape((tokens, width), f32), shape((tokens, LANES), f32),
        ],
        compiler_params=params(),
        name="gate_forward",
    )(place1, cotangent, cot_oth, normed, mixed, wz, gout)

    sums_oth = swap(sums, 1, "tensor")
    branch, ggate, gm, gw_zo, g_gout = pl.pallas_call(
        gate_back_kernel,
        grid_spec=pltpu.PrefetchScalarGridSpec(
            num_scalar_prefetch=1,
            grid=(chunks,),
            in_specs=[
                half_spec, half_spec, rows_spec(L, dim), wide, wide, wide, rows_spec(L, LANES),
                rows_spec(L, LANES), full((dim, 2 * width)), full((1, width)),
            ],
            out_specs=[
                rows_spec(L, dim), wide, wide, full((dim, 2 * width)), full((8, width)),
            ],
            scratch_shapes=[
                pltpu.VMEM((dim, width), f32), pltpu.VMEM((dim, width), f32),
                pltpu.VMEM((8, width), f32),
            ],
        ),
        out_shape=[
            shape((tokens, dim), bf16), shape((tokens, width), bf16), shape((tokens, width), bf16),
            shape((dim, 2 * width), bf16), shape((8, width), f32),
        ],
        compiler_params=params(),
        name="gate_backward",
    )(place1, cotangent, cot_oth, normed, mixed, gate, gno, sums, sums_oth, wz, gout)

    rs_a = bits[::-1]
    rs_b = (bits[-2:] + bits[:-2][::-1]) if size > 2 else bits
    grad_w_z = scatter_sum(gw_zo[:, :width], rs_a, "dp")
    grad_w_out = scatter_sum(gw_zo[:, width:], rs_b, "dp").T

    half_of = lambda v, which: lax.dynamic_slice_in_dim(v, which * half_rows, half_rows, 0)
    branch_own = half_of(branch, place)
    branch_oth = swap(half_of(branch, 1 - place), 1, "tensor")

    def back(c):
        return chunks - 1 - c

    rwide = rows_spec(L, width, back)
    gx, gw_x, g_conv, g_skip, g_head = pl.pallas_call(
        scan_back_kernel,
        grid=(chunks,),
        in_specs=[
            rows_spec(L, cols, back),
            rows_spec(16, cols, lambda c: jnp.maximum(back(c) * (L // 16) - 1, 0)),
            rows_spec(L, LANES, back), rwide,
            pl.BlockSpec((1, NS, width), lambda c: (back(c), 0, 0)),
            rwide, rows_spec(L, dim, back), full((4, cols)), full((1, cols)), full((1, LANES)),
            full((1, LANES)), full((1, width)),
        ],
        out_specs=[
            rows_spec(L, cols + LANES, back), full((dim, cols + LANES)), full((5, 8, cols)),
            full((8, width)), full((16, LANES)),
        ],
        scratch_shapes=[
            pltpu.VMEM((NS, width), f32), pltpu.VMEM((L + 8, cols), f32),
            pltpu.VMEM((L + 8, cols), f32), pltpu.VMEM((dim, cols + LANES), f32),
            pltpu.VMEM((5, 8, cols), f32), pltpu.VMEM((8, width), f32),
            pltpu.VMEM((16, LANES), f32),
        ],
        out_shape=[
            shape((tokens, cols + LANES), bf16), shape((dim, cols + LANES), bf16),
            shape((5, 8, cols), f32), shape((8, width), f32), shape((16, LANES), f32),
        ],
        compiler_params=params(),
        name="mix_backward",
    )(xbc, xbc, step_raw, mixed, sin, gm, normed, conv, bias, dtb, rate, dsk)

    grad_w_x = scatter_sum(gw_x[:, :width], rs_a, "dp")
    grad_rest = scatter_sum(gw_x[:, width:], rs_b, "dp")
    grad_w_bc = grad_rest[:, : 2 * NS]
    grad_w_bc = grad_w_bc + swap(grad_w_bc, 1, "tensor")
    grad_w_dt = grad_rest[:, 2 * NS : 2 * NS + heads]

    dn, g_gin = pl.pallas_call(
        input_back_kernel,
        grid_spec=pltpu.PrefetchScalarGridSpec(
            num_scalar_prefetch=1,
            grid=(chunks,),
            in_specs=[
                half_spec, half_spec, wide, rows_spec(L, cols + LANES), full((dim, 2 * width)),
                full((dim, cols + LANES)),
            ],
            out_specs=[rows_spec(L, dim), full((8, dim))],
            scratch_shapes=[pltpu.VMEM((8, dim), f32)],
        ),
        out_shape=[shape((tokens, dim), bf16), shape((8, dim), f32)],
        compiler_params=params(),
        name="input_backward",
    )(place1, resid, resid_oth, ggate, gx, wz, wx)
    dn_own = half_of(dn, place)
    dn_oth = swap(half_of(dn, 1 - place), 1, "tensor")

    dspec = rows_spec(L, dim)
    block_out, grad_resid = pl.pallas_call(
        finish_kernel,
        grid=(half,),
        in_specs=[dspec, dspec, full((1, dim)), dspec, dspec, dspec, dspec],
        out_specs=[dspec, dspec],
        out_shape=[shape((half_rows, dim), bf16), shape((half_rows, dim), f32)],
        compiler_params=params(),
        name="finish",
    )(resid, cotangent, gin, dn_own, dn_oth, branch_own, branch_oth)

    conv_sum = jnp.sum(g_conv, axis=1)
    both = jnp.concatenate([conv_sum[:, width:].reshape(-1), jnp.sum(g_gin, axis=0)])
    both = both + swap(both, 1, "tensor")
    head_sum = jnp.sum(g_head.reshape(2, 8, LANES), axis=1)[:, :heads]
    skip_sum = jnp.sum(g_skip, axis=0).reshape(heads, HEAD).sum(axis=1)
    flat = [
        conv_sum[:, :width].reshape(-1), both, jnp.sum(g_gout, axis=0), head_sum.reshape(-1),
        skip_sum,
    ]
    sizes = [v.shape[0] for v in flat]
    vec = jnp.concatenate(flat)
    for bit in bits:
        vec = vec + swap(vec, bit, "dp")
    out = []
    start = 0
    for count in sizes:
        out.append(vec[start : start + count])
        start += count
    conv_g = out[0].reshape(5, width)
    bc_g = out[1][: 10 * NS].reshape(5, 2 * NS)
    grad_gain_in = out[1][10 * NS :]
    head_g = out[3].reshape(2, heads)
    return (
        block_out, grad_resid, grad_gain_in, grad_w_z, grad_w_x, grad_w_bc, grad_w_dt,
        conv_g[:4], conv_g[4], bc_g[:4], bc_g[4], head_g[0], head_g[1], out[4], out[2],
        grad_w_out,
    )


def solution(mesh):
    in_specs = (
        P(("dp", "tensor"), None),
        P(),
        P("dp", "tensor"),
        P("dp", "tensor"),
        P("dp", None),
        P("dp", "tensor"),
        P(None, "tensor"),
        P("tensor"),
        P(),
        P(),
        P("tensor"),
        P("tensor"),
        P("tensor"),
        P("tensor"),
        P("tensor", "dp"),
        P(("dp", "tensor"), None),
    )
    out_specs = (
        P(("dp", "tensor"), None),
        P(("dp", "tensor"), None),
        P(),
        P("dp", "tensor"),
        P("dp", "tensor"),
        P("dp", None),
        P("dp", "tensor"),
        P(None, "tensor"),
        P("tensor"),
        P(),
        P(),
        P("tensor"),
        P("tensor"),
        P("tensor"),
        P("tensor"),
        P("tensor", "dp"),
    )
    return jax.shard_map(local, mesh=mesh, in_specs=in_specs, out_specs=out_specs, check_vma=False)
```

```python
import functools

import jax
import jax.numpy as jnp
from jax import lax
from jax.experimental import pallas as pl
from jax.experimental.pallas import tpu as pltpu
from jax.sharding import PartitionSpec as P

NS = 128
L = 256
SEQ_LEN = 2048
HEAD = 64
LANES = 128
VMEM = 52 * 1024 * 1024

f32 = jnp.float32
bf16 = jnp.bfloat16
highest = lax.Precision.HIGHEST
eps = 1e-05

NN = (((1,), (0,)), ((), ()))
NT = (((1,), (1,)), ((), ()))
TN = (((0,), (0,)), ((), ()))


def mm(a, b, dims=NN, precision=None):
    return lax.dot_general(a, b, dims, precision=precision, preferred_element_type=f32)


def iota(shape, dim):
    return lax.broadcasted_iota(jnp.int32, shape, dim)


def lower_tri():
    return (iota((L, L), 0) >= iota((L, L), 1)).astype(f32)


def upper_tri():
    return (iota((L, L), 0) <= iota((L, L), 1)).astype(f32)


def expander(heads):
    rows = iota((LANES, heads * HEAD), 0)
    cols = iota((LANES, heads * HEAD), 1) // HEAD
    return ((rows % 16 == cols) & (rows < 48)).astype(bf16)


def collector(heads):
    rows = iota((heads * HEAD, LANES), 0) // HEAD
    cols = iota((heads * HEAD, LANES), 1)
    return ((cols % 16 == rows) & (cols < 48)).astype(bf16)


def pack3(q):
    lane = iota(q.shape, 1)
    hi = q.astype(bf16).astype(f32)
    rest = q - hi
    mid = rest.astype(bf16).astype(f32)
    return jnp.where(lane < 16, hi, jnp.where(lane < 32, mid, rest - mid)).astype(bf16)


def head_sums(q, col):
    hi = q.astype(bf16)
    lo = (q - hi.astype(f32)).astype(bf16)
    return mm(hi, col) + mm(lo, col)


def softplus(v):
    return jnp.maximum(v, 0.0) + jnp.log1p(jnp.exp(-jnp.abs(v)))


def fold8(q):
    return jnp.sum(q.reshape(q.shape[0] // 8, 8, q.shape[1]), axis=0)


def spread(steps, within, expand):
    tails = jnp.exp(within[L - 1 : L, :] - within)
    return (
        mm(pack3(steps), expand),
        mm(pack3(jnp.exp(within)), expand),
        mm(pack3(tails), expand),
    )


def load_rows(info, pieces, places, w, sem, cols=slice(None)):
    copies = []
    for piece, (offset, masks) in zip(pieces, places):
        count = piece.shape[1]
        for k, mask in enumerate(masks):
            slot = 0 if mask is None else (info[1] ^ mask)
            rows = pl.ds(pl.multiple_of(slot * count, 16), count)
            if cols == slice(None):
                src = piece.at[k]
                dst = w.at[rows, pl.ds(offset, piece.shape[2])]
            else:
                src = piece.at[k, :, cols]
                dst = w.at[rows, :]
            copies.append(pltpu.make_async_copy(src, dst, sem.at[len(copies)]))
    for copy in copies:
        copy.start()
    for copy in copies:
        copy.wait()


def store_rows(info, acc, outs, masks):
    at = 0
    for out in outs:
        count = out.shape[1]
        for k in range(out.shape[0]):
            mask = masks[at]
            slot = 0 if mask is None else (info[1] ^ mask)
            rows = pl.ds(pl.multiple_of(slot * count, 16), count)
            out[k] = acc[rows, :].astype(bf16)
            at += 1


def forward_kernel(places, info, own, oth, gin, conv, bias, dtb, rate, dsk, *rest):
    count = len(places)
    pieces = rest[:count]
    (normed_o, xbc_o, act_o, dsilu_o, step_o, within_o, mixed_o, sin_o, state, buf, w, sem) = rest[
        count:
    ]
    c = pl.program_id(0)
    half = pl.num_programs(0) // 2
    width = dsk.shape[1]
    heads = width // HEAD
    cols = width + 2 * NS

    @pl.when(c == 0)
    def _():
        load_rows(info, pieces, places, w, sem)
        state[...] = jnp.zeros_like(state)
        buf[0:8, :] = jnp.zeros((8, cols), f32)

    mine = (c // half) == info[0]
    r = jnp.where(mine, own[...].astype(f32), oth[...].astype(f32))
    inv = lax.rsqrt(jnp.mean(r * r, axis=1, keepdims=True) + eps)
    normed = (r * inv * gin[...]).astype(bf16)
    normed_o[...] = normed
    proj = mm(normed, w[...])
    xbc = proj[:, :cols].astype(bf16)
    step_raw = proj[:, cols:]
    xbc_o[...] = xbc
    step_o[...] = step_raw
    xin = xbc.astype(f32)
    buf[8:, :] = xin
    v = bias[...] + conv[3:4, :] * xin
    for k in range(3):
        v = v + conv[k : k + 1, :] * buf[5 + k : 5 + k + L, :]
    buf[0:8, :] = xin[L - 8 :, :]
    sig = jax.nn.sigmoid(v)
    act = (v * sig).astype(bf16)
    act_o[...] = act
    dsilu_o[...] = (sig * (1.0 + v * (1.0 - sig))).astype(bf16)
    x = act[:, :width].astype(f32)
    b = act[:, width : width + NS]
    cc = act[:, width + NS :]

    expand = expander(heads)
    steps = softplus(step_raw + dtb[...])
    within = mm(lower_tri(), steps * rate[...], precision=highest)
    within_o[...] = within
    steps_e, grown_e, tails_e = spread(steps, within, expand)
    within_t = within.T
    scaled = x * steps_e
    scaled_b = scaled.astype(bf16)
    inter = mm(cc, b, NT)
    sin = state[...]
    sin_o[0] = sin
    outside = mm(cc, sin.astype(bf16)) * grown_e
    state[...] = sin * grown_e[L - 1 : L, :] + mm(b, (scaled * tails_e).astype(bf16), TN)
    hl = L // 2
    tri = iota((hl, hl), 0) >= iota((hl, hl), 1)
    left = iota((hl, LANES), 1) < HEAD
    for pair in range(heads // 2):
        ps = slice(pair * LANES, (pair + 1) * LANES)
        x2 = scaled_b[:, ps]
        tops, bots = [], []
        for h in (2 * pair, 2 * pair + 1):
            wc = within[:, h : h + 1]
            wr = within_t[h : h + 1, :]
            d_tl = jnp.exp(jnp.where(tri, wc[:hl] - wr[:, :hl], -1e30))
            d_bl = jnp.exp(wc[hl:] - wr[:, :hl])
            d_br = jnp.exp(jnp.where(tri, wc[hl:] - wr[:, hl:], -1e30))
            tops.append((inter[:hl, :hl] * d_tl).astype(bf16))
            bots.append(
                jnp.concatenate(
                    [
                        (inter[hl:, :hl] * d_bl).astype(bf16),
                        (inter[hl:, hl:] * d_br).astype(bf16),
                    ],
                    axis=1,
                )
            )
        top = mm(jnp.concatenate(tops, axis=0), x2[:hl])
        bot = mm(jnp.concatenate(bots, axis=0), x2)
        skip = dsk[:, ps] * x[:, ps] + outside[:, ps]
        mixed_o[:hl, ps] = jnp.where(left, top[:hl], top[hl:]) + skip[:hl]
        mixed_o[hl:, ps] = jnp.where(left, bot[:hl], bot[hl:]) + skip[hl:]


def gate_kernel(places, info, cown, coth, normed, mixed, gout, *rest):
    count = len(places)
    pieces = rest[:count]
    gate_o, gno_o, sums_o, w, sem = rest[count:]
    c = pl.program_id(0)
    half = pl.num_programs(0) // 2
    width = gout.shape[1]

    @pl.when(c == 0)
    def _():
        load_rows(info, pieces, places, w, sem)

    mine = (c // half) == info[0]
    cot = jnp.where(mine, cown[...].astype(f32), coth[...].astype(f32)).astype(bf16)
    gate = mm(normed[...], w[:, :width]).astype(bf16)
    gate_o[...] = gate
    gf = gate.astype(f32)
    gated = mixed[...] * (gf * jax.nn.sigmoid(gf))
    gno = mm(cot, w[:, width:])
    gno_o[...] = gno
    squares = jnp.sum(gated * gated, axis=1, keepdims=True)
    products = jnp.sum(gno * gout[...] * gated, axis=1, keepdims=True)
    lane = iota((L, LANES), 1)
    sums = jnp.where(lane < 64, squares, products).T
    sums_o[0:8, :] = sums[0:8]
    sums_o[8:16, :] = sums[64:72]


def gate_back_kernel(
    places, masks, info, cown, coth, normed, mixed, gate, gno, sown, soth, gout, *rest
):
    count = len(places)
    pieces = rest[:count]
    rest = rest[count:]
    parts = len(rest) - 9
    (sent_o, kept_o, ggate_o, gm_o, ggo_o) = rest[:5]
    gw_o = rest[5 : 5 + parts]
    acc, acc_g, w, sem = rest[5 + parts :]
    c = pl.program_id(0)
    last = pl.num_programs(0) - 1
    half = pl.num_programs(0) // 2
    width = gout.shape[1]

    @pl.when(c == 0)
    def _():
        load_rows(info, pieces, places, w, sem, pl.ds(width, width))
        acc[...] = jnp.zeros_like(acc)
        acc_g[...] = jnp.zeros_like(acc_g)

    cot = jnp.where(c < half, coth[...].astype(f32), cown[...].astype(f32)).astype(bf16)
    s = sown[...] + soth[...]
    sums = jnp.concatenate(
        [jnp.broadcast_to(s[0:1], (64, L)), jnp.broadcast_to(s[8:9], (64, L))], axis=0
    ).T
    inner_total = 2.0 * width
    scale = lax.rsqrt(sums[:, 0:1] / inner_total + eps)
    coef = scale * scale * scale * (sums[:, 64:65] / inner_total)
    gf = gate[...].astype(f32)
    sig = jax.nn.sigmoid(gf)
    silu = gf * sig
    mix = mixed[...]
    gated = mix * silu
    grad = gno[...]
    unit = gated * scale
    normed_out = (unit * gout[...]).astype(bf16)
    branch = mm(normed_out, w[...], NT).astype(bf16)

    @pl.when(c < half)
    def _():
        sent_o[...] = branch

    @pl.when(c >= half)
    def _():
        kept_o[...] = branch

    acc_g[...] += fold8(grad * unit)
    grad_gated = scale * (grad * gout[...]) - gated * coef
    grad_gate = (grad_gated * mix * (sig + silu * (1.0 - sig))).astype(bf16)
    ggate_o[...] = grad_gate
    gm_o[...] = (grad_gated * silu).astype(bf16)
    acc[:, :width] += mm(normed[...], grad_gate, TN)
    acc[:, width:] += mm(cot, normed_out, TN)

    @pl.when(c == last)
    def _():
        store_rows(info, acc, gw_o, masks)
        ggo_o[...] = acc_g[...]


def scan_back_kernel(
    masks, info, xbc, act_r, dsilu, step, within_r, mixed, sin_r, gm, normed, conv, dtb, rate, dsk,
    gx_o, gconv_o, gskip_o, ghead_o, *rest,
):
    gw_o = rest[:-6]
    dstate, dvbuf, acc_w, acc_c, acc_s, acc_h = rest[-6:]
    i = pl.program_id(0)
    last = pl.num_programs(0) - 1
    width = dsk.shape[1]
    heads = width // HEAD
    cols = width + 2 * NS

    @pl.when(i == 0)
    def _():
        dstate[...] = jnp.zeros_like(dstate)
        dvbuf[...] = jnp.zeros_like(dvbuf)
        acc_w[...] = jnp.zeros_like(acc_w)
        acc_c[...] = jnp.zeros_like(acc_c)
        acc_s[...] = jnp.zeros_like(acc_s)
        acc_h[...] = jnp.zeros_like(acc_h)

    x = act_r[:, :width].astype(f32)
    b = act_r[:, width : width + NS]
    cc = act_r[:, width + NS :]

    expand = expander(heads)
    collect = collector(heads)
    step_raw = step[...]
    within = within_r[...]
    steps = softplus(step_raw + dtb[...])
    steps_e, grown_e, tails_e = spread(steps, within, expand)
    within_t = within.T
    scaled = x * steps_e
    scaled_b = scaled.astype(bf16)
    gmb = gm[...]
    gmf = gmb.astype(f32)
    sin = sin_r[0]
    ds = dstate[...]
    ds_b = ds.astype(bf16)
    inter_t = mm(b, cc, NT)
    state_part = mm(b, ds_b) * tails_e
    gm_grown = (gmf * grown_e).astype(bf16)
    last_grown = grown_e[L - 1 : L, :]
    dstate[...] = ds * last_grown + mm(cc, gm_grown, TN)
    hl = L // 2
    tri = iota((hl, hl), 0) <= iota((hl, hl), 1)
    left = iota((hl, LANES), 1) < HEAD
    leftw = iota((L, LANES), 1) < HEAD
    dg_tl = jnp.zeros((hl, hl), f32)
    dg_tr = jnp.zeros((hl, hl), f32)
    dg_br = jnp.zeros((hl, hl), f32)
    dscaled = []
    for pair in range(heads // 2):
        ps = slice(pair * LANES, (pair + 1) * LANES)
        x2 = scaled_b[:, ps]
        g2 = gmb[:, ps]
        zero = jnp.zeros_like(x2)
        xe = jnp.where(leftw, x2, zero)
        xo = jnp.where(leftw, zero, x2)
        dm_top = mm(jnp.concatenate([xe[:hl], xo[:hl]], axis=0), g2, NT)
        dm_bot = mm(jnp.concatenate([xe[hl:], xo[hl:]], axis=0), g2[hl:], NT)
        tops, bots = [], []
        for side, h in enumerate((2 * pair, 2 * pair + 1)):
            wc = within[:, h : h + 1]
            wr = within_t[h : h + 1, :]
            d_tl = jnp.exp(jnp.where(tri, wr[:, :hl] - wc[:hl], -1e30))
            d_tr = jnp.exp(wr[:, hl:] - wc[:hl])
            d_br = jnp.exp(jnp.where(tri, wr[:, hl:] - wc[hl:], -1e30))
            tops.append(
                jnp.concatenate(
                    [
                        (inter_t[:hl, :hl] * d_tl).astype(bf16),
                        (inter_t[:hl, hl:] * d_tr).astype(bf16),
                    ],
                    axis=1,
                )
            )
            bots.append((inter_t[hl:, hl:] * d_br).astype(bf16))
            rows = slice(side * hl, (side + 1) * hl)
            dg_tl += dm_top[rows, :hl] * d_tl
            dg_tr += dm_top[rows, hl:] * d_tr
            dg_br += dm_bot[rows] * d_br
        top = mm(jnp.concatenate(tops, axis=0), g2)
        bot = mm(jnp.concatenate(bots, axis=0), g2[hl:])
        dscaled.append(
            jnp.concatenate(
                [jnp.where(left, top[:hl], top[hl:]), jnp.where(left, bot[:hl], bot[hl:])], axis=0
            )
        )
    dscaled = jnp.concatenate(dscaled, axis=1) + state_part
    top = jnp.concatenate([dg_tl, dg_tr], axis=1)
    bot = jnp.concatenate([jnp.zeros((hl, hl), f32), dg_br], axis=1)
    dg = jnp.concatenate([top, bot], axis=0).astype(bf16)
    dc = mm(dg, b, TN) + mm(gm_grown, sin.astype(bf16), NT)
    db = mm(dg, cc) + mm((scaled * tails_e).astype(bf16), ds_b, NT)
    scaled_f = scaled_b.astype(f32)
    y = mixed[...] - dsk[...] * x
    q = gmf * y - scaled_f * dscaled
    ends = jnp.sum(scaled_f * state_part, axis=0, keepdims=True) + last_grown * jnp.sum(
        sin * ds, axis=0, keepdims=True
    )
    ends_h = head_sums(jnp.broadcast_to(ends, (8, width)), collect)[0:1, :]
    d_rate = mm(upper_tri(), head_sums(q, collect), precision=highest) + ends_h
    d_steps = d_rate * rate[...] + head_sums(dscaled * x, collect)
    sig_s = jax.nn.sigmoid(step_raw + dtb[...])
    keep = iota((L, LANES), 1) < heads
    d_raw = jnp.where(keep, d_steps * sig_s, 0.0)
    acc_h[0:8, :] += fold8(d_raw)
    acc_h[8:16, :] += fold8(d_rate * steps * rate[...])
    acc_s[...] += fold8(gmf * x)
    dx = dscaled * steps_e + dsk[...] * gmf

    dv = jnp.concatenate([dx, db, dc], axis=1) * dsilu[...].astype(f32)
    dvbuf[0:L, :] = dv
    xin = xbc[...].astype(f32)
    acc_c[4] += fold8(dv)
    acc_c[3] += fold8(dv * xin)
    dxin = conv[3:4, :] * dv
    for k in range(3):
        ahead = dvbuf[3 - k : 3 - k + L, :]
        acc_c[k] += fold8(ahead * xin)
        dxin = dxin + conv[k : k + 1, :] * ahead
    dvbuf[L : L + 8, :] = dv[0:8, :]
    gx = jnp.concatenate([dxin.astype(bf16), d_raw.astype(bf16)], axis=1)
    gx_o[...] = gx
    acc_w[...] += mm(normed[...], gx, TN)

    @pl.when(i == last)
    def _():
        store_rows(info, acc_w, gw_o, masks)
        gconv_o[...] = acc_c[...]
        gskip_o[...] = acc_s[...]
        ghead_o[...] = acc_h[...]


def input_back_kernel(zplaces, xplaces, info, own, oth, ggate, gx, *rest):
    zcount, xcount = len(zplaces), len(xplaces)
    zpieces = rest[:zcount]
    xpieces = rest[zcount : zcount + xcount]
    sent_o, kept_o, gain_o, wz, wx, zsem, xsem = rest[zcount + xcount :]
    c = pl.program_id(0)
    half = pl.num_programs(0) // 2
    width = ggate.shape[1]

    @pl.when(c == 0)
    def _():
        load_rows(info, zpieces, zplaces, wz, zsem, pl.ds(0, width))
        load_rows(info, xpieces, xplaces, wx, xsem)
        gain_o[...] = jnp.zeros_like(gain_o)

    r = jnp.where(c < half, oth[...].astype(f32), own[...].astype(f32))
    inv = lax.rsqrt(jnp.mean(r * r, axis=1, keepdims=True) + eps)
    dn = mm(ggate[...], wz[...], NT) + mm(gx[...], wx[...], NT)
    dnb = dn.astype(bf16)

    @pl.when(c < half)
    def _():
        sent_o[...] = dnb

    @pl.when(c >= half)
    def _():
        kept_o[...] = dnb

    gain_o[...] += fold8(dn * (r * inv))


def finish_kernel(resid, cot, gin, dn_own, dn_oth, br_own, br_oth, out_o, gres_o):
    r = resid[...].astype(f32)
    inv = lax.rsqrt(jnp.mean(r * r, axis=1, keepdims=True) + eps)
    out_o[...] = (r + (br_own[...].astype(f32) + br_oth[...].astype(f32))).astype(bf16)
    u = (dn_own[...].astype(f32) + dn_oth[...].astype(f32)) * gin[...]
    mean = jnp.mean(u * r, axis=1, keepdims=True)
    gres_o[...] = cot[...].astype(f32) + inv * u - r * (inv * inv * inv * mean)


def swap(v, bit, axis):
    size = lax.axis_size(axis)
    return lax.ppermute(v, axis, [(i, i ^ bit) for i in range(size)])


NEAR = (0, 1, 2, 3)
FAR = (0, 4, 8, 12)


def direct(size, rows):
    return size == 16 and rows % 16 == 0


def gather_whole(v, bits):
    size = lax.axis_size("dp")
    me = lax.axis_index("dp")
    held = v[None]
    for bit in sorted(bits):
        got = swap(held, bit, "dp")
        upper = (me & bit) != 0
        held = jnp.where(
            upper, jnp.concatenate([got, held]), jnp.concatenate([held, got])
        )
    return held.reshape(1, size * v.shape[0], v.shape[1])


def whole_pieces(v, bits):
    return [gather_whole(v, bits)], [(0, (None,))]


def gather_far(v):
    return [swap(v, far, "dp") for far in FAR[1:]]


def gather_near(held):
    pieces = [held] + [swap(held, near, "dp") for near in NEAR[1:]]
    return pieces, [(0, tuple(near ^ far for far in FAR)) for near in NEAR]


def scatter_shapes(size, rows, cols):
    if not direct(size, rows):
        return [jax.ShapeDtypeStruct((1, size * rows, cols), bf16)], (None,)
    masks = tuple(near ^ far for near in NEAR for far in FAR)
    return [jax.ShapeDtypeStruct((4, rows, cols), bf16)] * 4, masks


def scatter_near(pieces):
    return [pieces[0]] + [swap(p, near, "dp") for p, near in zip(pieces[1:], NEAR[1:])]


def scatter_far(total):
    sent = total.astype(bf16)
    return [total[0]] + [swap(sent[k], FAR[k], "dp") for k in range(1, 4)]


def sum_pieces(pieces):
    return sum(p.astype(f32) for p in pieces)


def scatter_whole(g, bits):
    me = lax.axis_index("dp")
    rows = g.shape[0] // lax.axis_size("dp")
    left = sorted(bits, reverse=True)
    cur = g.reshape([2] * len(left) + [rows, g.shape[1]])
    for bit in sorted(bits):
        dim = left.index(bit)
        mine = ((me & bit) != 0).astype(jnp.int32)
        send = lax.dynamic_index_in_dim(cur, 1 - mine, dim, keepdims=False)
        keep = lax.dynamic_index_in_dim(cur, mine, dim, keepdims=False)
        got = swap(send.astype(bf16), bit, "dp")
        cur = keep.astype(f32) + got.astype(f32)
        left.pop(dim)
    return cur.astype(f32)


def full(shape):
    zeros = (0,) * len(shape)
    return pl.BlockSpec(shape, lambda c, *_: zeros)


def rows_spec(count, width, index=lambda c, info: c):
    return pl.BlockSpec((count, width), lambda c, info: (index(c, info), 0))


def call(kernel, name, grid, ins, outs, scratch, info, *args):
    specs = [spec for spec, _ in outs]
    shapes = [item for _, item in outs]
    return pl.pallas_call(
        kernel,
        grid_spec=pltpu.PrefetchScalarGridSpec(
            num_scalar_prefetch=1, grid=(grid,), in_specs=ins, out_specs=specs,
            scratch_shapes=scratch,
        ),
        out_shape=shapes,
        compiler_params=pltpu.CompilerParams(
            dimension_semantics=("arbitrary",), vmem_limit_bytes=VMEM
        ),
        name=name,
    )(info, *args)


def local(
    resid, gain_in, w_z, w_x, w_bc, w_dt, conv_x, bias_x, conv_bc, bias_bc, dt_bias, a_log, d_skip,
    gain_out, w_out, cotangent,
):
    size = lax.axis_size("dp")
    place = lax.axis_index("tensor")
    heads = a_log.shape[0]
    width = heads * HEAD
    dim = resid.shape[1]
    rows = w_z.shape[0]
    cols = width + 2 * NS
    half_rows = resid.shape[0]
    tokens = 2 * half_rows
    assert tokens == SEQ_LEN
    chunks = tokens // L
    half = chunks // 2
    shape = jax.ShapeDtypeStruct
    bits = [1 << k for k in range(size.bit_length() - 1)]

    def lanes3(v):
        pad = [(0, 0)] * (v.ndim - 1)
        group = jnp.pad(v, pad + [(0, 16 - heads)])
        return jnp.pad(jnp.concatenate([group] * 3, axis=-1), pad + [(0, LANES - 48)])

    first = jnp.concatenate([w_x, w_bc, lanes3(w_dt)], axis=1)
    second = jnp.concatenate([w_z, w_out.T], axis=1)
    conv = jnp.concatenate([conv_x, conv_bc], axis=1)
    bias = jnp.concatenate([bias_x, bias_bc])[None]
    dtb = lanes3(dt_bias[None])
    rate = lanes3(-jnp.exp(a_log)[None])
    dsk = jnp.repeat(d_skip, HEAD)[None]
    gin = gain_in[None]
    gout = gain_out[None]
    if direct(size, rows):
        first, got, second, resid_in, cot_in, conv, bias, dtb, rate, dsk, gin, gout = (
            lax.optimization_barrier(
                (
                    first, gather_far(first), second, resid, cotangent, conv, bias, dtb, rate, dsk,
                    gin, gout,
                )
            )
        )
        wx, wx_at = gather_near(jnp.stack([first] + got))
        got = gather_far(second)
        resid_oth = swap(resid_in, 1, "tensor")
        cot_oth = swap(cot_in, 1, "tensor")
        second, resid_oth, cot_oth, wx, got = lax.optimization_barrier(
            (second, resid_oth, cot_oth, wx, got)
        )
        wz, wz_at = gather_near(jnp.stack([second] + got))
    else:
        resid_oth = swap(resid, 1, "tensor")
        cot_oth = swap(cotangent, 1, "tensor")
        wx, wx_at = whole_pieces(first, bits)
        wz, wz_at = whole_pieces(second, bits)

    info = jnp.stack([place, lax.axis_index("dp")]).astype(jnp.int32)
    anywhere = pl.BlockSpec(memory_space=pl.ANY)

    def copies(at):
        return pltpu.SemaphoreType.DMA((sum(len(masks) for _, masks in at),))

    def tok(width, dtype):
        return shape((tokens, width), dtype)

    own_spec = rows_spec(L, dim, lambda c, info: jnp.clip(c - half * info[0], 0, half - 1))
    oth_spec = rows_spec(L, dim, lambda c, info: jnp.clip(c - half * (1 - info[0]), 0, half - 1))
    wide = rows_spec(L, width)
    normed, xbc, act, dsilu, step_raw, within, mixed, sin = call(
        functools.partial(forward_kernel, wx_at),
        "mix_forward",
        chunks,
        [
            own_spec, oth_spec, full((1, dim)), full((4, cols)), full((1, cols)),
            full((1, LANES)), full((1, LANES)), full((1, width)),
        ]
        + [anywhere] * len(wx),
        [
            (rows_spec(L, dim), tok(dim, bf16)),
            (rows_spec(L, cols), tok(cols, bf16)),
            (rows_spec(L, cols), tok(cols, bf16)),
            (rows_spec(L, cols), tok(cols, bf16)),
            (rows_spec(L, LANES), tok(LANES, f32)),
            (rows_spec(L, LANES), tok(LANES, f32)),
            (wide, tok(width, f32)),
            (
                pl.BlockSpec((1, NS, width), lambda c, info: (c, 0, 0)),
                shape((chunks, NS, width), f32),
            ),
        ],
        [
            pltpu.VMEM((NS, width), f32), pltpu.VMEM((L + 8, cols), f32),
            pltpu.VMEM((dim, cols + LANES), bf16), copies(wx_at),
        ],
        info, resid, resid_oth, gin, conv, bias, dtb, rate, dsk, *wx,
    )

    sums_shape = shape((chunks * 16, L), f32)
    gate, gno, sums = call(
        functools.partial(gate_kernel, wz_at),
        "gate_forward",
        chunks,
        [own_spec, oth_spec, rows_spec(L, dim), wide, full((1, width))] + [anywhere] * len(wz),
        [(wide, tok(width, bf16)), (wide, tok(width, f32)), (rows_spec(16, L), sums_shape)],
        [pltpu.VMEM((dim, 2 * width), bf16), copies(wz_at)],
        info, cotangent, cot_oth, normed, mixed, gout, *wz,
    )
    sums_oth = swap(sums, 1, "tensor")

    def turned(c, info):
        return jnp.where(c < half, c + half * (1 - info[0]), c - half + half * info[0])

    gw_shapes, masks = scatter_shapes(size, rows, 2 * width)
    twide = rows_spec(L, width, turned)
    lead = rows_spec(L, dim, lambda c, info: jnp.minimum(c, half - 1))
    trail = rows_spec(L, dim, lambda c, info: jnp.maximum(c - half, 0))
    half_shape = shape((half_rows, dim), bf16)
    branch_sent, branch_own, ggate, gm, g_gout, *gw_zo = call(
        functools.partial(gate_back_kernel, wz_at, masks),
        "gate_backward",
        chunks,
        [
            trail, lead, rows_spec(L, dim, turned), twide, twide, twide,
            rows_spec(16, L, turned), rows_spec(16, L, turned), full((1, width)),
        ]
        + [anywhere] * len(wz),
        [
            (lead, half_shape), (trail, half_shape), (twide, tok(width, bf16)),
            (twide, tok(width, bf16)), (full((8, width)), shape((8, width), f32)),
        ]
        + [(full(item.shape), item) for item in gw_shapes],
        [
            pltpu.VMEM((dim, 2 * width), f32), pltpu.VMEM((8, width), f32),
            pltpu.VMEM((dim, width), bf16), copies(wz_at),
        ],
        info, cotangent, cot_oth, normed, mixed, gate, gno, sums, sums_oth, gout, *wz,
    )
    branch_oth = swap(branch_sent, 1, "tensor")
    sent_zo = scatter_near(gw_zo) if direct(size, rows) else gw_zo

    def back(c, info):
        return chunks - 1 - c

    rwide = rows_spec(L, width, back)
    rcols = rows_spec(L, cols, back)
    rlanes = rows_spec(L, LANES, back)
    gwx_shapes, masks = scatter_shapes(size, rows, cols + LANES)
    gx, g_conv, g_skip, g_head, *gw_x = call(
        functools.partial(scan_back_kernel, masks),
        "mix_backward",
        chunks,
        [
            rcols, rcols, rcols, rlanes, rlanes, rwide,
            pl.BlockSpec((1, NS, width), lambda c, info: (chunks - 1 - c, 0, 0)),
            rwide, rows_spec(L, dim, back), full((4, cols)), full((1, LANES)),
            full((1, LANES)), full((1, width)),
        ],
        [
            (rows_spec(L, cols + LANES, back), tok(cols + LANES, bf16)),
            (full((5, 8, cols)), shape((5, 8, cols), f32)),
            (full((8, width)), shape((8, width), f32)),
            (full((16, LANES)), shape((16, LANES), f32)),
        ]
        + [(full(item.shape), item) for item in gwx_shapes],
        [
            pltpu.VMEM((NS, width), f32), pltpu.VMEM((L + 8, cols), f32),
            pltpu.VMEM((dim, cols + LANES), f32), pltpu.VMEM((5, 8, cols), f32),
            pltpu.VMEM((8, width), f32), pltpu.VMEM((16, LANES), f32),
        ],
        info, xbc, act, dsilu, step_raw, within, mixed, sin, gm, normed, conv, dtb, rate, dsk,
    )

    sent_zo, branch_oth, gx, gw_x = lax.optimization_barrier((sent_zo, branch_oth, gx, gw_x))
    if direct(size, rows):
        far_zo = scatter_far(sum_pieces(sent_zo))
        sent_x = scatter_near(gw_x)

    dn_sent, dn_own, g_gin = call(
        functools.partial(input_back_kernel, wz_at, wx_at),
        "input_backward",
        chunks,
        [trail, lead, twide, rows_spec(L, cols + LANES, turned)]
        + [anywhere] * (len(wz) + len(wx)),
        [(lead, half_shape), (trail, half_shape), (full((8, dim)), shape((8, dim), f32))],
        [
            pltpu.VMEM((dim, width), bf16), pltpu.VMEM((dim, cols + LANES), bf16),
            copies(wz_at), copies(wx_at),
        ],
        info, resid, resid_oth, ggate, gx, *wz, *wx,
    )
    if direct(size, rows):
        far_zo, sent_x, dn_own, dn_sent, g_gin = lax.optimization_barrier(
            (far_zo, sent_x, dn_own, dn_sent, g_gin)
        )
        far_x = scatter_far(sum_pieces(sent_x))
    dn_oth = swap(dn_sent, 1, "tensor")

    conv_sum = jnp.sum(g_conv, axis=1)
    both = jnp.concatenate([conv_sum[:, width:].reshape(-1), jnp.sum(g_gin, axis=0)])
    both = both + swap(both, 1, "tensor")
    head_sum = jnp.sum(g_head.reshape(2, 8, LANES), axis=1)[:, :heads]
    skip_sum = jnp.sum(g_skip, axis=0).reshape(heads, HEAD).sum(axis=1)
    flat = [
        conv_sum[:, :width].reshape(-1), both, jnp.sum(g_gout, axis=0), head_sum.reshape(-1),
        skip_sum,
    ]
    sizes = [v.shape[0] for v in flat]
    vec = jnp.concatenate(flat)
    if direct(size, rows):
        near_vec = [vec] + [swap(vec, near, "dp") for near in NEAR[1:]]

    dspec = rows_spec(L, dim)
    block_out, grad_resid = call(
        lambda info, *refs: finish_kernel(*refs),
        "finish",
        half,
        [dspec, dspec, full((1, dim)), dspec, dspec, dspec, dspec],
        [(dspec, half_shape), (dspec, shape((half_rows, dim), f32))],
        [],
        info, resid, cotangent, gin, dn_own, dn_oth, branch_own, branch_oth,
    )

    if direct(size, rows):
        block_out, grad_resid, near_vec = lax.optimization_barrier(
            (block_out, grad_resid, near_vec)
        )
        vec = sum(near_vec)
        vec = vec + sum(swap(vec, far, "dp") for far in FAR[1:])
        sum_zo = sum_pieces(far_zo)
        sum_x = sum_pieces(far_x)
    else:
        sum_zo = scatter_whole(sent_zo[0][0], bits)
        sum_x = scatter_whole(gw_x[0][0], bits)
        for bit in bits:
            vec = vec + swap(vec, bit, "dp")
    grad_w_z = sum_zo[:, :width]
    grad_w_out = sum_zo[:, width:].T
    grad_w_x = sum_x[:, :width]
    grad_w_bc = sum_x[:, width:cols]
    grad_w_bc = grad_w_bc + swap(grad_w_bc, 1, "tensor")
    grad_w_dt = sum_x[:, cols : cols + heads]
    out = []
    start = 0
    for count in sizes:
        out.append(vec[start : start + count])
        start += count
    conv_g = out[0].reshape(5, width)
    bc_g = out[1][: 10 * NS].reshape(5, 2 * NS)
    grad_gain_in = out[1][10 * NS :]
    head_g = out[3].reshape(2, heads)
    return (
        block_out, grad_resid, grad_gain_in, grad_w_z, grad_w_x, grad_w_bc, grad_w_dt,
        conv_g[:4], conv_g[4], bc_g[:4], bc_g[4], head_g[0], head_g[1], out[4], out[2],
        grad_w_out,
    )


def solution(mesh):
    in_specs = (
        P(("dp", "tensor"), None),
        P(),
        P("dp", "tensor"),
        P("dp", "tensor"),
        P("dp", None),
        P("dp", "tensor"),
        P(None, "tensor"),
        P("tensor"),
        P(),
        P(),
        P("tensor"),
        P("tensor"),
        P("tensor"),
        P("tensor"),
        P("tensor", "dp"),
        P(("dp", "tensor"), None),
    )
    out_specs = (
        P(("dp", "tensor"), None),
        P(("dp", "tensor"), None),
        P(),
        P("dp", "tensor"),
        P("dp", "tensor"),
        P("dp", None),
        P("dp", "tensor"),
        P(None, "tensor"),
        P("tensor"),
        P(),
        P(),
        P("tensor"),
        P("tensor"),
        P("tensor"),
        P("tensor"),
        P("tensor", "dp"),
    )
    return jax.shard_map(local, mesh=mesh, in_specs=in_specs, out_specs=out_specs, check_vma=False)
```

```python
import functools

import jax
import jax.numpy as jnp
from jax import lax
from jax.experimental import pallas as pl
from jax.experimental.pallas import tpu as pltpu
from jax.sharding import PartitionSpec as P

NS = 128
L = 256
R = 512
SEQ_LEN = 2048
HEAD = 64
LANES = 128
MIB = 1024 * 1024

f32 = jnp.float32
bf16 = jnp.bfloat16
highest = lax.Precision.HIGHEST
eps = 1e-05

NN = (((1,), (0,)), ((), ()))
NT = (((1,), (1,)), ((), ()))
TN = (((0,), (0,)), ((), ()))


def mm(a, b, dims=NN, precision=None):
    return lax.dot_general(a, b, dims, precision=precision, preferred_element_type=f32)


def iota(shape, dim):
    return lax.broadcasted_iota(jnp.int32, shape, dim)


def lower_tri():
    return (iota((L, L), 0) >= iota((L, L), 1)).astype(bf16)


def upper_tri():
    return (iota((L, L), 0) <= iota((L, L), 1)).astype(bf16)


def expander(heads):
    rows = iota((LANES, heads * HEAD), 0)
    cols = iota((LANES, heads * HEAD), 1) // HEAD
    return ((rows % 16 == cols) & (rows < 48)).astype(bf16)


def collector(heads):
    rows = iota((heads * HEAD, LANES), 0) // HEAD
    cols = iota((heads * HEAD, LANES), 1)
    return ((cols % 16 == rows) & (cols < 48)).astype(bf16)


def split3(q):
    hi = q.astype(bf16).astype(f32)
    rest = q - hi
    mid = rest.astype(bf16).astype(f32)
    return hi, mid, rest - mid


def pack3(q):
    lane = iota(q.shape, 1)
    hi, mid, low = split3(q)
    return jnp.where(lane < 16, hi, jnp.where(lane < 32, mid, low)).astype(bf16)


def exact_mm(a, q):
    return sum(mm(a, part.astype(bf16)) for part in split3(q))


def turn(v):
    return v.astype(f32).T.astype(bf16)


def head_sums(q, col):
    hi = q.astype(bf16)
    lo = (q - hi.astype(f32)).astype(bf16)
    return mm(hi, col) + mm(lo, col)


def softplus(v):
    return jnp.maximum(v, 0.0) + jnp.log1p(jnp.exp(-jnp.abs(v)))


def sigmoid(v):
    return 0.5 * jnp.tanh(0.5 * v) + 0.5


def fold8(q):
    return jnp.sum(q.reshape(q.shape[0] // 8, 8, q.shape[1]), axis=0)


def packs(steps, within):
    tails = jnp.exp(within[L - 1 : L, :] - within)
    return pack3(steps), pack3(jnp.exp(within)), pack3(tails)


def load_rows(info, pieces, places, w, sem, cols=slice(None)):
    copies = []
    for piece, (offset, masks) in zip(pieces, places):
        count = piece.shape[1]
        for k, mask in enumerate(masks):
            slot = 0 if mask is None else (info[1] ^ mask)
            rows = pl.ds(pl.multiple_of(slot * count, 16), count)
            if cols == slice(None):
                src = piece.at[k]
                dst = w.at[rows, pl.ds(offset, piece.shape[2])]
            else:
                src = piece.at[k, :, cols]
                dst = w.at[rows, :]
            copies.append(pltpu.make_async_copy(src, dst, sem.at[len(copies)]))
    for copy in copies:
        copy.start()
    for copy in copies:
        copy.wait()


def store_rows(info, acc, outs, masks, count):
    each = len(masks) // len(outs)
    for at, mask in enumerate(masks):
        slot = 0 if mask is None else (info[1] ^ mask)
        rows = pl.ds(pl.multiple_of(slot * count, 16), count)
        start = at % each * count
        outs[at // each][start : start + count, :] = acc[rows, :].astype(bf16)


def row_products(acc, w, width):
    total = jnp.zeros((acc.shape[0], LANES), f32)
    for at in range(0, width, LANES):
        ps = slice(at, at + LANES)
        total += acc[:, ps] * w[:, ps].astype(f32)
    return total


def forward_kernel(
    places, info, own, oth, gin, conv, bias, dtb, rate, dsk, expand, tri_r, *rest
):
    count = len(places)
    pieces = rest[:count]
    (normed_o, xbc_o, act_o, dsilu_o, step_o, within_o, mixed_o, sin_o, state, buf, w, sem) = rest[
        count:
    ]
    c = pl.program_id(0)
    half = pl.num_programs(0) // 2
    width = dsk.shape[1]
    heads = width // HEAD
    cols = width + 2 * NS

    @pl.when(c == 0)
    def _():
        load_rows(info, pieces, places, w, sem)
        state[...] = jnp.zeros_like(state)
        buf[:, 0:8] = jnp.zeros((cols // LANES, 8, LANES), f32)

    mine = (c // half) == info[0]
    r = jnp.where(mine, own[...].astype(f32), oth[...].astype(f32))
    inv = lax.rsqrt(jnp.mean(r * r, axis=1, keepdims=True) + eps)
    normed = (r * inv * gin[...]).astype(bf16)
    normed_o[...] = normed
    step_raw = mm(normed, w[:, cols:])
    step_o[...] = step_raw
    steps = softplus(step_raw + dtb[...])
    within = exact_mm(tri_r[...], steps * rate[...])
    within_o[...] = within
    p_steps, p_grown, p_tails = packs(steps, within)
    within_t = within.T

    def conv_strip(cs):
        n = cs.start // LANES
        v = bias[:, cs] + conv[3:4, cs] * buf[n, 8 : 8 + L]
        for k in range(3):
            v = v + conv[k : k + 1, cs] * buf[n, 5 + k : 5 + k + L]
        buf[n, 0:8] = buf[n, L : L + 8]
        sig = sigmoid(v)
        value = v * sig
        dsilu_o[:, cs] = (sig + value * (1.0 - sig)).astype(bf16)
        act_o[:, cs] = value.astype(bf16)

    for at in range(cols - 2 * LANES, -1, -2 * LANES):
        ws = slice(at, at + 2 * LANES)
        xb = mm(normed, w[:, ws]).astype(bf16)
        xbc_o[:, ws] = xb
        xf = xb.astype(f32)
        buf[at // LANES, 8:] = xf[:, :LANES]
        buf[at // LANES + 1, 8:] = xf[:, LANES:]
        conv_strip(slice(at, at + LANES))
        conv_strip(slice(at + LANES, at + 2 * LANES))

    b = act_o[:, width : width + NS]
    cc = act_o[:, width + NS :]
    bt = turn(b)
    inter = mm(cc, b, NT)
    hl = L // 2
    tri = iota((hl, hl), 0) >= iota((hl, hl), 1)
    left = iota((L, LANES), 1) < HEAD
    zero = jnp.zeros((L, LANES), bf16)
    for quad in range(heads // 4):
        qs = slice(quad * 2 * LANES, (quad + 1) * 2 * LANES)
        steps_e = mm(p_steps, expand[:, qs])
        grown_e = mm(p_grown, expand[:, qs])
        tails_e = mm(p_tails, expand[:, qs])
        x = act_o[:, qs].astype(f32)
        scaled = x * steps_e
        scaled_b = scaled.astype(bf16)
        sin = state[:, qs]
        sin_o[0, :, qs] = sin
        base = mm(cc, sin.astype(bf16)) * grown_e + dsk[:, qs] * x
        state[:, qs] = sin * grown_e[L - 1 : L, :] + mm(bt, (scaled * tails_e).astype(bf16))
        for side in range(2):
            pair = 2 * quad + side
            ls = slice(side * LANES, (side + 1) * LANES)
            ps = slice(pair * LANES, (pair + 1) * LANES)
            x2 = scaled_b[:, ls]
            xe = jnp.where(left, x2, zero)
            xo = jnp.where(left, zero, x2)
            tops, bots = [], []
            for h in (2 * pair, 2 * pair + 1):
                wc = within[:, h : h + 1]
                wr = within_t[h : h + 1, :]
                d_tl = jnp.exp(jnp.where(tri, wc[:hl] - wr[:, :hl], -1e30))
                d_bl = jnp.exp(wc[hl:] - wr[:, :hl])
                d_br = jnp.exp(jnp.where(tri, wc[hl:] - wr[:, hl:], -1e30))
                tops.append((inter[:hl, :hl] * d_tl).astype(bf16))
                bots.append((inter[hl:, :hl] * d_bl).astype(bf16))
                bots.append((inter[hl:, hl:] * d_br).astype(bf16))
            top = mm(
                jnp.concatenate(tops, axis=1), jnp.concatenate([xe[:hl], xo[:hl]], axis=0)
            )
            bot = mm(jnp.concatenate(bots, axis=1), jnp.concatenate([xe, xo], axis=0))
            mixed_o[:hl, ps] = top + base[:hl, ls]
            mixed_o[hl:, ps] = bot + base[hl:, ls]


def gate_kernel(places, info, cown, coth, normed, mixed, gout, *rest):
    count = len(places)
    pieces = rest[:count]
    gate_o, gno_o, sums_o, w, sem = rest[count:]
    c = pl.program_id(0)
    half = pl.num_programs(0) // 2
    width = gout.shape[1]

    @pl.when(c == 0)
    def _():
        load_rows(info, pieces, places, w, sem)

    mine = (c // half) == info[0]
    cot = jnp.where(mine, cown[...].astype(f32), coth[...].astype(f32)).astype(bf16)
    squares = jnp.zeros((R, LANES), f32)
    products = jnp.zeros((R, LANES), f32)
    for at in range(0, width, 2 * LANES):
        gate = mm(normed[...], w[:, at : at + 2 * LANES]).astype(bf16)
        gno = mm(cot, w[:, width + at : width + at + 2 * LANES])
        gate_o[:, at : at + 2 * LANES] = gate
        gno_o[:, at : at + 2 * LANES] = gno
        for ls in (slice(0, LANES), slice(LANES, 2 * LANES)):
            ps = slice(at + ls.start, at + ls.stop)
            gf = gate[:, ls].astype(f32)
            gated = mixed[:, ps] * (gf * sigmoid(gf))
            squares += gated * gated
            products += gno[:, ls] * gout[:, ps] * gated
    sums_o[0:8, :] = jnp.broadcast_to(jnp.sum(squares.T, axis=0, keepdims=True), (8, R))
    sums_o[8:16, :] = jnp.broadcast_to(jnp.sum(products.T, axis=0, keepdims=True), (8, R))


def gate_back_kernel(
    places, masks, info, cown, coth, normed, mixed, gate, gno, sown, soth, gout, *rest
):
    count = len(places)
    pieces = rest[:count]
    rest = rest[count:]
    parts = len(rest) - 11
    (sent_o, kept_o, ggate_o, gm_o, ggo_o, gain_o) = rest[:6]
    gw_o = rest[6 : 6 + parts]
    acc, acc_g, w, nout, sem = rest[6 + parts :]
    c = pl.program_id(0)
    last = pl.num_programs(0) - 1
    half = pl.num_programs(0) // 2
    width = gout.shape[1]

    @pl.when(c == 0)
    def _():
        load_rows(info, pieces, places, w, sem)
        acc[...] = jnp.zeros_like(acc)
        acc_g[...] = jnp.zeros_like(acc_g)

    cot = jnp.where(c < half, coth[...].astype(f32), cown[...].astype(f32)).astype(bf16)
    inner_total = 2.0 * width
    s = sown[...] + soth[...]
    scale_r = lax.rsqrt(s[0:1] / inner_total + eps)
    coef_r = scale_r * scale_r * scale_r * (s[8:9] / inner_total)
    scale = jnp.broadcast_to(scale_r, (LANES, R)).T
    coef = jnp.broadcast_to(coef_r, (LANES, R)).T
    for at in range(0, width, LANES):
        ps = slice(at, at + LANES)
        gain = gout[:, ps]
        gf = gate[:, ps].astype(f32)
        sig = sigmoid(gf)
        silu = gf * sig
        mix = mixed[:, ps]
        gated = mix * silu
        grad = gno[:, ps]
        unit = gated * scale
        nout[:, ps] = (unit * gain).astype(bf16)
        acc_g[:, ps] += fold8(grad * unit)
        grad_gated = scale * (grad * gain) - gated * coef
        ggate_o[:, ps] = (grad_gated * mix * (sig + silu * (1.0 - sig))).astype(bf16)
        gm_o[:, ps] = (grad_gated * silu).astype(bf16)
    branch = mm(nout[...], w[:, width:], NT).astype(bf16)

    @pl.when(c < half)
    def _():
        sent_o[...] = branch

    @pl.when(c >= half)
    def _():
        kept_o[...] = branch

    acc[:, :width] += mm(normed[...], ggate_o[...], TN)
    acc[:, width:] += mm(cot, nout[...], TN)

    @pl.when(c == last)
    def _():
        store_rows(info, acc, gw_o, masks, acc.shape[0] // len(masks))
        ggo_o[...] = acc_g[...]
        gain_o[...] = row_products(acc, w, width)


def scan_back_kernel(
    masks, places, info, xbc, act_r, dsilu, step, within_r, mixed, sin_r, gm, normed, conv, dtb, rate, dsk,
    expand, collect, tri_r, ggo, gain_z, *rest,
):
    count = len(places)
    pieces = rest[:count]
    gx_o, small_o = rest[count : count + 2]
    gw_o = rest[count + 2 : -8]
    dstate, dvbuf, acc_w, acc_c, acc_s, acc_h, w, sem = rest[-8:]
    i = pl.program_id(0)
    last = pl.num_programs(0) - 1
    width = dsk.shape[1]
    heads = width // HEAD
    cols = width + 2 * NS

    @pl.when(i == 0)
    def _():
        load_rows(info, pieces, places, w, sem)
        dstate[...] = jnp.zeros_like(dstate)
        dvbuf[...] = jnp.zeros_like(dvbuf)
        acc_w[...] = jnp.zeros_like(acc_w)
        acc_c[...] = jnp.zeros_like(acc_c)
        acc_s[...] = jnp.zeros_like(acc_s)
        acc_h[...] = jnp.zeros_like(acc_h)

    def conv_strip(dpost, cs):
        dv = dpost * dsilu[:, cs].astype(f32)
        n = cs.start // LANES
        dvbuf[n, 0:L] = dv
        xin = xbc[:, cs].astype(f32)
        acc_c[4, :, cs] += fold8(dv)
        acc_c[3, :, cs] += fold8(dv * xin)
        dxin = conv[3:4, cs] * dv
        for k in range(3):
            ahead = dvbuf[n, 3 - k : 3 - k + L]
            acc_c[k, :, cs] += fold8(ahead * xin)
            dxin = dxin + conv[k : k + 1, cs] * ahead
        dvbuf[n, L : L + 8] = dv[0:8, :]
        gx_o[:, cs] = dxin.astype(bf16)

    b = act_r[:, width : width + NS]
    cc = act_r[:, width + NS :]
    ct = turn(cc)
    step_raw = step[...]
    within = within_r[...]
    steps = softplus(step_raw + dtb[...])
    p_steps, p_grown, p_tails = packs(steps, within)
    within_t = within.T
    inter_t = mm(b, cc, NT)
    hl = L // 2
    tri = iota((hl, hl), 0) <= iota((hl, hl), 1)
    left = iota((L, LANES), 1) < HEAD
    zero = jnp.zeros((L, LANES), bf16)
    dg_tl = jnp.zeros((hl, hl), f32)
    dg_tr = jnp.zeros((hl, hl), f32)
    dg_br = jnp.zeros((hl, hl), f32)
    dc = jnp.zeros((L, NS), f32)
    db = jnp.zeros((L, NS), f32)
    q_h = jnp.zeros((L, LANES), f32)
    s_h = jnp.zeros((L, LANES), f32)
    ends_h = jnp.zeros((8, LANES), f32)
    for quad in range(heads // 4):
        qs = slice(quad * 2 * LANES, (quad + 1) * 2 * LANES)
        steps_e = mm(p_steps, expand[:, qs])
        grown_e = mm(p_grown, expand[:, qs])
        tails_e = mm(p_tails, expand[:, qs])
        x = act_r[:, qs].astype(f32)
        scaled = x * steps_e
        scaled_b = scaled.astype(bf16)
        scaled_f = scaled_b.astype(f32)
        gmb = gm[:, qs]
        gmf = gmb.astype(f32)
        ds = dstate[:, qs]
        ds_b = ds.astype(bf16)
        sin = sin_r[0, :, qs]
        last_grown = grown_e[L - 1 : L, :]
        gm_grown = (gmf * grown_e).astype(bf16)
        dc += mm(gm_grown, sin.astype(bf16), NT)
        db += mm((scaled * tails_e).astype(bf16), ds_b, NT)
        dstate[:, qs] = ds * last_grown + mm(ct, gm_grown)
        state_part = mm(b, ds_b) * tails_e
        ends = jnp.sum(scaled_f * state_part, axis=0, keepdims=True) + last_grown * jnp.sum(
            sin * ds, axis=0, keepdims=True
        )
        collect_q = collect[qs, :]
        ends_h += head_sums(jnp.broadcast_to(ends, (8, 2 * LANES)), collect_q)
        his, los, prods = [], [], []
        for side in range(2):
            pair = 2 * quad + side
            ls = slice(side * LANES, (side + 1) * LANES)
            ps = slice(pair * LANES, (pair + 1) * LANES)
            x2 = scaled_b[:, ls]
            g2 = gmb[:, ls]
            ge = jnp.where(left, g2, zero)
            go = jnp.where(left, zero, g2)
            g_both = jnp.concatenate([ge, go], axis=0)
            g_bot = jnp.concatenate([ge[hl:], go[hl:]], axis=0)
            dm_top = mm(x2[:hl], g_both, NT)
            dm_bot = mm(x2[hl:], g_bot, NT)
            tops, bots = [], []
            for k, h in enumerate((2 * pair, 2 * pair + 1)):
                wc = within[:, h : h + 1]
                wr = within_t[h : h + 1, :]
                d_tl = jnp.exp(jnp.where(tri, wr[:, :hl] - wc[:hl], -1e30))
                d_tr = jnp.exp(wr[:, hl:] - wc[:hl])
                d_br = jnp.exp(jnp.where(tri, wr[:, hl:] - wc[hl:], -1e30))
                tops.append((inter_t[:hl, :hl] * d_tl).astype(bf16))
                tops.append((inter_t[:hl, hl:] * d_tr).astype(bf16))
                bots.append((inter_t[hl:, hl:] * d_br).astype(bf16))
                dg_tl += dm_top[:, k * L : k * L + hl] * d_tl
                dg_tr += dm_top[:, k * L + hl : (k + 1) * L] * d_tr
                dg_br += dm_bot[:, k * hl : (k + 1) * hl] * d_br
            top = mm(jnp.concatenate(tops, axis=1), g_both)
            bot = mm(jnp.concatenate(bots, axis=1), g_bot)
            dscaled = jnp.concatenate([top, bot], axis=0) + state_part[:, ls]
            xs = x[:, ls]
            gs = gmf[:, ls]
            y = mixed[:, ps] - dsk[:, ps] * xs
            q = gs * y - scaled_f[:, ls] * dscaled
            hi = q.astype(bf16)
            his.append(hi)
            los.append((q - hi.astype(f32)).astype(bf16))
            prods.append((dscaled * xs).astype(bf16))
            acc_s[:, ps] += fold8(gs * xs)
            conv_strip(dscaled * steps_e[:, ls] + dsk[:, ps] * gs, ps)
        q_h += mm(jnp.concatenate(his, axis=1), collect_q)
        q_h += mm(jnp.concatenate(los, axis=1), collect_q)
        s_h += mm(jnp.concatenate(prods, axis=1), collect_q)
    top = jnp.concatenate([dg_tl, dg_tr], axis=1)
    bot = jnp.concatenate([jnp.zeros((hl, hl), f32), dg_br], axis=1)
    dg = jnp.concatenate([top, bot], axis=0)
    dc += mm(dg.T.astype(bf16), b)
    db += mm(dg.astype(bf16), cc)
    conv_strip(db, slice(width, width + NS))
    conv_strip(dc, slice(width + NS, cols))
    d_rate = exact_mm(tri_r[...], q_h) + ends_h[0:1, :]
    d_steps = d_rate * rate[...] + s_h
    sig_s = sigmoid(step_raw + dtb[...])
    keep = iota((L, LANES), 1) < heads
    d_raw = jnp.where(keep, d_steps * sig_s, 0.0)
    acc_h[0:8, :] += fold8(d_raw)
    acc_h[8:16, :] += fold8(d_rate * steps * rate[...])
    gx_o[:, cols:] = d_raw.astype(bf16)
    acc_w[...] += mm(normed[...], gx_o[...], TN)

    @pl.when(i == last)
    def _():
        store_rows(info, acc_w, gw_o, masks, acc_w.shape[0] // len(masks))
        small_o[...] = jnp.zeros_like(small_o)
        for k in range(5):
            small_o[k : k + 1, :cols] = jnp.sum(acc_c[k], axis=0, keepdims=True)
        for k in range(2):
            head = acc_h[8 * k : 8 * k + 8, :]
            small_o[k : k + 1, cols:] = jnp.sum(head, axis=0, keepdims=True)
        small_o[5:6, :width] = jnp.sum(acc_s[...], axis=0, keepdims=True)
        small_o[6:7, :width] = jnp.sum(ggo[...], axis=0, keepdims=True)
        gains = row_products(acc_w, w, cols + LANES) + gain_z[...]
        small_o[7:8, : acc_w.shape[0]] = jnp.sum(gains.T, axis=0, keepdims=True)
        if len(gw_o) > 1:
            small = small_o[...]
            hi = small.astype(bf16).astype(f32)
            parts = jnp.concatenate([hi, small - hi], axis=0).astype(bf16)
            for out in gw_o:
                out[out.shape[0] - 16 :, :] = parts


def input_back_kernel(zplaces, xplaces, info, ggate, gx, *rest):
    zcount, xcount = len(zplaces), len(xplaces)
    zpieces = rest[:zcount]
    xpieces = rest[zcount : zcount + xcount]
    sent_o, kept_o, wz, wx, dnb, zsem, xsem = rest[zcount + xcount :]
    c = pl.program_id(0)
    half = pl.num_programs(0) // 2
    width = ggate.shape[1]

    @pl.when(c == 0)
    def _():
        load_rows(info, zpieces, zplaces, wz, zsem, pl.ds(0, width))
        load_rows(info, xpieces, xplaces, wx, xsem)

    dim = dnb.shape[1]
    for at in range(0, dim, 2 * LANES):
        ds = slice(at, at + 2 * LANES)
        dn = mm(ggate[...], wz[ds, :], NT) + mm(gx[...], wx[ds, :], NT)
        dnb[:, ds] = dn.astype(bf16)

    @pl.when(c < half)
    def _():
        sent_o[...] = dnb[...]

    @pl.when(c >= half)
    def _():
        kept_o[...] = dnb[...]


def finish_kernel(resid, cot, gin, dn_own, dn_oth, br_own, br_oth, out_o, gres_o):
    r = resid[...].astype(f32)
    inv = lax.rsqrt(jnp.mean(r * r, axis=1, keepdims=True) + eps)
    out_o[...] = (r + (br_own[...].astype(f32) + br_oth[...].astype(f32))).astype(bf16)
    u = (dn_own[...].astype(f32) + dn_oth[...].astype(f32)) * gin[...]
    mean = jnp.mean(u * r, axis=1, keepdims=True)
    gres_o[...] = cot[...].astype(f32) + inv * u - r * (inv * inv * inv * mean)


def swap(v, bit, axis):
    size = lax.axis_size(axis)
    return lax.ppermute(v, axis, [(i, i ^ bit) for i in range(size)])


NEAR = (0, 1, 2, 3)
FAR = (0, 4, 8, 12)


def direct(size, rows):
    return size == 16 and rows % 16 == 0


def gather_whole(v, bits):
    size = lax.axis_size("dp")
    me = lax.axis_index("dp")
    held = v[None]
    for bit in sorted(bits):
        got = swap(held, bit, "dp")
        upper = (me & bit) != 0
        held = jnp.where(
            upper, jnp.concatenate([got, held]), jnp.concatenate([held, got])
        )
    return held.reshape(1, size * v.shape[0], v.shape[1])


def whole_pieces(v, bits):
    return [gather_whole(v, bits)], [(0, (None,))]


def gather_far(v):
    return [swap(v, far, "dp") for far in FAR[1:]]


def gather_near(held):
    pieces = [held] + [swap(held, near, "dp") for near in NEAR[1:]]
    return pieces, [(0, tuple(near ^ far for far in FAR)) for near in NEAR]


def scatter_shapes(size, rows, cols, extra=0):
    if not direct(size, rows):
        return [jax.ShapeDtypeStruct((size * rows, cols), bf16)], (None,)
    masks = tuple(near ^ far for near in NEAR for far in FAR)
    return [jax.ShapeDtypeStruct((4 * rows + extra, cols), bf16)] * 4, masks


def both_parts(v):
    return v[-16:-8] + v[-8:]


def scatter_near(pieces):
    return [pieces[0]] + [swap(p, near, "dp") for p, near in zip(pieces[1:], NEAR[1:])]


def scatter_far(total, rows, extra=None):
    blocks = [total[k * rows : (k + 1) * rows] for k in range(4)]
    if extra is not None:
        hi = extra.astype(bf16).astype(f32)
        parts = jnp.concatenate([hi, (extra - hi).astype(bf16).astype(f32)])
        blocks = [jnp.concatenate([block, parts]) for block in blocks]
    sent = [swap(block.astype(bf16), far, "dp") for block, far in zip(blocks[1:], FAR[1:])]
    return blocks[:1] + sent


def sum_pieces(pieces):
    return sum(p.astype(f32) for p in pieces)


def scatter_whole(g, bits):
    me = lax.axis_index("dp")
    rows = g.shape[0] // lax.axis_size("dp")
    left = sorted(bits, reverse=True)
    cur = g.reshape([2] * len(left) + [rows, g.shape[1]])
    for bit in sorted(bits):
        dim = left.index(bit)
        mine = ((me & bit) != 0).astype(jnp.int32)
        send = lax.dynamic_index_in_dim(cur, 1 - mine, dim, keepdims=False)
        keep = lax.dynamic_index_in_dim(cur, mine, dim, keepdims=False)
        got = swap(send.astype(bf16), bit, "dp")
        cur = keep.astype(f32) + got.astype(f32)
        left.pop(dim)
    return cur.astype(f32)


def full(shape):
    zeros = (0,) * len(shape)
    return pl.BlockSpec(shape, lambda c, *_: zeros)


def rows_spec(count, width, index=lambda c, info: c):
    return pl.BlockSpec((count, width), lambda c, info: (index(c, info), 0))


def call(kernel, name, vmem, grid, ins, outs, scratch, info, *args, **more):
    specs = [spec for spec, _ in outs]
    shapes = [item for _, item in outs]
    return pl.pallas_call(
        kernel,
        grid_spec=pltpu.PrefetchScalarGridSpec(
            num_scalar_prefetch=1, grid=(grid,), in_specs=ins, out_specs=specs,
            scratch_shapes=scratch,
        ),
        out_shape=shapes,
        compiler_params=pltpu.CompilerParams(
            dimension_semantics=("arbitrary",), vmem_limit_bytes=vmem * MIB
        ),
        name=name,
        **more,
    )(info, *args)


def local(
    resid, gain_in, w_z, w_x, w_bc, w_dt, conv_x, bias_x, conv_bc, bias_bc, dt_bias, a_log, d_skip,
    gain_out, w_out, cotangent,
):
    size = lax.axis_size("dp")
    place = lax.axis_index("tensor")
    heads = a_log.shape[0]
    width = heads * HEAD
    dim = resid.shape[1]
    rows = w_z.shape[0]
    cols = width + 2 * NS
    half_rows = resid.shape[0]
    tokens = 2 * half_rows
    assert tokens == SEQ_LEN
    chunks = tokens // L
    half = chunks // 2
    shape = jax.ShapeDtypeStruct
    bits = [1 << k for k in range(size.bit_length() - 1)]

    def lanes3(v):
        pad = [(0, 0)] * (v.ndim - 1)
        group = jnp.pad(v, pad + [(0, 16 - heads)])
        return jnp.pad(jnp.concatenate([group] * 3, axis=-1), pad + [(0, LANES - 48)])

    first = jnp.concatenate([w_x, w_bc, lanes3(w_dt)], axis=1)
    second = jnp.concatenate([w_z, w_out.T], axis=1)
    conv = jnp.concatenate([conv_x, conv_bc], axis=1)
    bias = jnp.concatenate([bias_x, bias_bc])[None]
    dtb = lanes3(dt_bias[None])
    rate = lanes3(-jnp.exp(a_log)[None])
    dsk = jnp.repeat(d_skip, HEAD)[None]
    gin = gain_in[None]
    gout = gain_out[None]
    expand = expander(heads)
    if direct(size, rows):
        cut = first.shape[1]
        both = jnp.concatenate([first, second], axis=1)
        both, got, resid_in, cot_in, conv, bias, dtb, rate, dsk, gin, gout, expand = (
            lax.optimization_barrier(
                (
                    both, gather_far(both), resid, cotangent, conv, bias, dtb, rate, dsk, gin,
                    gout, expand,
                )
            )
        )
        held = [both] + got
        wx, wx_at = gather_near(jnp.stack([v[:, :cut] for v in held]))
        resid_oth = swap(resid_in, 1, "tensor")
        cot_oth = swap(cot_in, 1, "tensor")
        held, resid_oth, cot_oth, wx = lax.optimization_barrier((held, resid_oth, cot_oth, wx))
        wz, wz_at = gather_near(jnp.stack([v[:, cut:] for v in held]))
    else:
        resid_oth = swap(resid, 1, "tensor")
        cot_oth = swap(cotangent, 1, "tensor")
        wx, wx_at = whole_pieces(first, bits)
        wz, wz_at = whole_pieces(second, bits)

    info = jnp.stack([place, lax.axis_index("dp")]).astype(jnp.int32)
    anywhere = pl.BlockSpec(memory_space=pl.ANY)

    def copies(at):
        return pltpu.SemaphoreType.DMA((sum(len(masks) for _, masks in at),))

    def tok(width, dtype):
        return shape((tokens, width), dtype)

    own_spec = rows_spec(L, dim, lambda c, info: jnp.clip(c - half * info[0], 0, half - 1))
    oth_spec = rows_spec(L, dim, lambda c, info: jnp.clip(c - half * (1 - info[0]), 0, half - 1))
    wide = rows_spec(L, width)
    normed, xbc, act, dsilu, step_raw, within, mixed, sin = call(
        functools.partial(forward_kernel, wx_at),
        "mix_forward",
        52,
        chunks,
        [
            own_spec, oth_spec, full((1, dim)), full((4, cols)), full((1, cols)),
            full((1, LANES)), full((1, LANES)), full((1, width)), full((LANES, width)),
            full((L, L)),
        ]
        + [anywhere] * len(wx),
        [
            (rows_spec(L, dim), tok(dim, bf16)),
            (rows_spec(L, cols), tok(cols, bf16)),
            (rows_spec(L, cols), tok(cols, bf16)),
            (rows_spec(L, cols), tok(cols, bf16)),
            (rows_spec(L, LANES), tok(LANES, f32)),
            (rows_spec(L, LANES), tok(LANES, f32)),
            (wide, tok(width, f32)),
            (
                pl.BlockSpec((1, NS, width), lambda c, info: (c, 0, 0)),
                shape((chunks, NS, width), f32),
            ),
        ],
        [
            pltpu.VMEM((NS, width), f32), pltpu.VMEM((cols // LANES, L + 8, LANES), f32),
            pltpu.VMEM((dim, cols + LANES), bf16), copies(wx_at),
        ],
        info, resid, resid_oth, gin, conv, bias, dtb, rate, dsk, expand, lower_tri(), *wx,
    )

    steps = tokens // R
    rhalf = steps // 2

    def block(width, index=lambda c, info: c):
        return rows_spec(R, width, index)

    own_r = block(dim, lambda c, info: jnp.clip(c - rhalf * info[0], 0, rhalf - 1))
    oth_r = block(dim, lambda c, info: jnp.clip(c - rhalf * (1 - info[0]), 0, rhalf - 1))
    sums_shape = shape((steps * 16, R), f32)
    gate, gno, sums = call(
        functools.partial(gate_kernel, wz_at),
        "gate_forward",
        52,
        steps,
        [own_r, oth_r, block(dim), block(width), full((1, width))] + [anywhere] * len(wz),
        [
            (block(width), tok(width, bf16)), (block(width), tok(width, f32)),
            (rows_spec(16, R), sums_shape),
        ],
        [pltpu.VMEM((dim, 2 * width), bf16), copies(wz_at)],
        info, cotangent, cot_oth, normed, mixed, gout, *wz,
    )
    sums_oth = swap(sums, 1, "tensor")

    def turned(c, info):
        return jnp.where(c < rhalf, c + rhalf * (1 - info[0]), c - rhalf + rhalf * info[0])

    gw_shapes, masks = scatter_shapes(size, rows, 2 * width)
    twide = block(width, turned)
    lead = block(dim, lambda c, info: jnp.minimum(c, rhalf - 1))
    trail = block(dim, lambda c, info: jnp.maximum(c - rhalf, 0))
    half_shape = shape((half_rows, dim), bf16)
    branch_sent, branch_own, ggate, gm, g_gout, g_gin_z, *gw_zo = call(
        functools.partial(gate_back_kernel, wz_at, masks),
        "gate_backward",
        52,
        steps,
        [
            trail, lead, block(dim, turned), twide, twide, twide,
            rows_spec(16, R, turned), rows_spec(16, R, turned), full((1, width)),
        ]
        + [anywhere] * len(wz),
        [
            (lead, half_shape), (trail, half_shape), (twide, tok(width, bf16)),
            (twide, tok(width, bf16)), (full((8, width)), shape((8, width), f32)),
            (full((dim, LANES)), shape((dim, LANES), f32)),
        ]
        + [(full(item.shape), item) for item in gw_shapes],
        [
            pltpu.VMEM((dim, 2 * width), f32), pltpu.VMEM((8, width), f32),
            pltpu.VMEM((dim, 2 * width), bf16), pltpu.VMEM((R, width), bf16), copies(wz_at),
        ],
        info, cotangent, cot_oth, normed, mixed, gate, gno, sums, sums_oth, gout, *wz,
    )
    branch_oth = swap(branch_sent, 1, "tensor")
    sent_zo = scatter_near(gw_zo) if direct(size, rows) else gw_zo

    def back(c, info):
        return chunks - 1 - c

    rwide = rows_spec(L, width, back)
    rcols = rows_spec(L, cols, back)
    rlanes = rows_spec(L, LANES, back)
    gwx_shapes, masks = scatter_shapes(size, rows, cols + LANES, 16)
    gx, small, *gw_x = call(
        functools.partial(scan_back_kernel, masks, wx_at),
        "mix_backward",
        52,
        chunks,
        [
            rcols, rcols, rcols, rlanes, rlanes, rwide,
            pl.BlockSpec((1, NS, width), lambda c, info: (chunks - 1 - c, 0, 0)),
            rwide, rows_spec(L, dim, back), full((4, cols)), full((1, LANES)),
            full((1, LANES)), full((1, width)), full((LANES, width)), full((width, LANES)),
            full((L, L)), full((8, width)), full((dim, LANES)),
        ]
        + [anywhere] * len(wx),
        [
            (rows_spec(L, cols + LANES, back), tok(cols + LANES, bf16)),
            (full((8, cols + LANES)), shape((8, cols + LANES), f32)),
        ]
        + [(full(item.shape), item) for item in gwx_shapes],
        [
            pltpu.VMEM((NS, width), f32), pltpu.VMEM((cols // LANES, L + 8, LANES), f32),
            pltpu.VMEM((dim, cols + LANES), f32), pltpu.VMEM((5, 8, cols), f32),
            pltpu.VMEM((8, width), f32), pltpu.VMEM((16, LANES), f32),
            pltpu.VMEM((dim, cols + LANES), bf16), copies(wx_at),
        ],
        info, xbc, act, dsilu, step_raw, within, mixed, sin, gm, normed, conv, dtb, rate, dsk,
        expand, collector(heads), upper_tri(), g_gout, g_gin_z, *wx,
    )

    sent_zo, branch_oth, gx, gw_x, small = lax.optimization_barrier(
        (sent_zo, branch_oth, gx, gw_x, small)
    )
    if direct(size, rows):
        sent_x = scatter_near(gw_x)
        far_zo = scatter_far(sum_pieces(sent_zo), rows)

    dn_sent, dn_own = call(
        functools.partial(input_back_kernel, wz_at, wx_at),
        "input_backward",
        32,
        steps,
        [twide, block(cols + LANES, turned)]
        + [anywhere] * (len(wz) + len(wx)),
        [(lead, half_shape), (trail, half_shape)],
        [
            pltpu.VMEM((dim, width), bf16), pltpu.VMEM((dim, cols + LANES), bf16),
            pltpu.VMEM((R, dim), bf16), copies(wz_at), copies(wx_at),
        ],
        info, ggate, gx, *wz, *wx,
    )
    if direct(size, rows):
        sent_x, dn_own, dn_sent = lax.optimization_barrier((sent_x, dn_own, dn_sent))
    dn_oth = swap(dn_sent, 1, "tensor")
    if direct(size, rows):
        total_x = sum_pieces(sent_x)
        far_x = scatter_far(total_x, rows, both_parts(total_x))
        far_zo, dn_oth, dn_own = lax.optimization_barrier((far_zo, dn_oth, dn_own))
        sum_zo = sum_pieces(far_zo)

    dspec = rows_spec(L, dim)
    block_out, grad_resid = call(
        lambda info, *refs: finish_kernel(*refs),
        "finish",
        12,
        half,
        [dspec, dspec, full((1, dim)), dspec, dspec, dspec, dspec],
        [(dspec, half_shape), (dspec, shape((half_rows, dim), f32))],
        [],
        info, resid, cotangent, gin, dn_own, dn_oth, branch_own, branch_oth,
    )

    if direct(size, rows):
        block_out, grad_resid, far_x = lax.optimization_barrier((block_out, grad_resid, far_x))
        sum_x = sum_pieces(far_x)
        small = both_parts(sum_x)
    else:
        sum_zo = scatter_whole(sent_zo[0], bits)
        sum_x = scatter_whole(gw_x[0], bits)
        for bit in bits:
            small = small + swap(small, bit, "dp")
    grad_w_bc = sum_x[:rows, width:cols]
    pair = jnp.concatenate(
        [grad_w_bc.reshape(-1), small[:5, width:cols].reshape(-1), small[7, :dim]]
    )
    pair = pair + swap(pair, 1, "tensor")
    grad_w_bc, bc_g, gain_g = jnp.split(pair, [rows * 2 * NS, (rows + 5) * 2 * NS])
    bc_g = bc_g.reshape(5, 2 * NS)
    return (
        block_out, grad_resid, gain_g / gain_in, sum_zo[:, :width], sum_x[:rows, :width],
        grad_w_bc.reshape(rows, 2 * NS), sum_x[:rows, cols : cols + heads],
        small[:4, :width], small[4, :width], bc_g[:4], bc_g[4], small[0, cols : cols + heads],
        small[1, cols : cols + heads], small[5, :width].reshape(heads, HEAD).sum(axis=1),
        small[6, :width], sum_zo[:, width:].T,
    )


def solution(mesh):
    in_specs = (
        P(("dp", "tensor"), None),
        P(),
        P("dp", "tensor"),
        P("dp", "tensor"),
        P("dp", None),
        P("dp", "tensor"),
        P(None, "tensor"),
        P("tensor"),
        P(),
        P(),
        P("tensor"),
        P("tensor"),
        P("tensor"),
        P("tensor"),
        P("tensor", "dp"),
        P(("dp", "tensor"), None),
    )
    out_specs = (
        P(("dp", "tensor"), None),
        P(("dp", "tensor"), None),
        P(),
        P("dp", "tensor"),
        P("dp", "tensor"),
        P("dp", None),
        P("dp", "tensor"),
        P(None, "tensor"),
        P("tensor"),
        P(),
        P(),
        P("tensor"),
        P("tensor"),
        P("tensor"),
        P("tensor"),
        P("tensor", "dp"),
    )
    return jax.shard_map(local, mesh=mesh, in_specs=in_specs, out_specs=out_specs, check_vma=False)
```

```python
import functools

import jax
import jax.numpy as jnp
from jax import lax
from jax.experimental import pallas as pl
from jax.experimental.pallas import tpu as pltpu
from jax.sharding import PartitionSpec as P

NS = 128
L = 256
R = 512
SEQ_LEN = 2048
HEAD = 64
LANES = 128
MIB = 1024 * 1024

f32 = jnp.float32
bf16 = jnp.bfloat16
highest = lax.Precision.HIGHEST
eps = 1e-05

NN = (((1,), (0,)), ((), ()))
NT = (((1,), (1,)), ((), ()))
TN = (((0,), (0,)), ((), ()))


def mm(a, b, dims=NN, precision=None):
    return lax.dot_general(a, b, dims, precision=precision, preferred_element_type=f32)


def iota(shape, dim):
    return lax.broadcasted_iota(jnp.int32, shape, dim)


def lower_tri():
    return (iota((L, L), 0) >= iota((L, L), 1)).astype(bf16)


def upper_tri():
    return (iota((L, L), 0) <= iota((L, L), 1)).astype(bf16)


def expander(heads):
    rows = iota((LANES, heads * HEAD), 0)
    cols = iota((LANES, heads * HEAD), 1) // HEAD
    return ((rows % 16 == cols) & (rows < 48)).astype(bf16)


def collector(heads):
    rows = iota((heads * HEAD, LANES), 0) // HEAD
    cols = iota((heads * HEAD, LANES), 1)
    return ((cols % 16 == rows) & (cols < 48)).astype(bf16)


def split3(q):
    hi = q.astype(bf16).astype(f32)
    rest = q - hi
    mid = rest.astype(bf16).astype(f32)
    return hi, mid, rest - mid


def pack3(q):
    lane = iota(q.shape, 1)
    hi, mid, low = split3(q)
    return jnp.where(lane < 16, hi, jnp.where(lane < 32, mid, low)).astype(bf16)


def exact_mm(a, q):
    return sum(mm(a, part.astype(bf16)) for part in split3(q))


def turn(v):
    return v.astype(f32).T.astype(bf16)


def head_sums(q, col):
    hi = q.astype(bf16)
    lo = (q - hi.astype(f32)).astype(bf16)
    return mm(hi, col) + mm(lo, col)


def softplus(v):
    return jnp.maximum(v, 0.0) + jnp.log1p(jnp.exp(-jnp.abs(v)))


def sigmoid(v):
    return 0.5 * jnp.tanh(0.5 * v) + 0.5


def fold8(q):
    return jnp.sum(q.reshape(q.shape[0] // 8, 8, q.shape[1]), axis=0)


def packs(steps, within):
    tails = jnp.exp(within[L - 1 : L, :] - within)
    return pack3(steps), pack3(jnp.exp(within)), pack3(tails)


CONV, BIAS, GIN, GOUT, DSK, DTB, RATE = 0, 4, 5, 6, 7, 8, 9


class vector:
    def __init__(self, ref, at, width, count=1):
        self.ref, self.at, self.width, self.count = ref, at, width, count

    def __getitem__(self, key):
        rows, cols = (slice(None), slice(None)) if key is Ellipsis else key
        start, stop, _ = rows.indices(self.count)
        left, right, _ = cols.indices(self.width)
        return self.ref[self.at + start : self.at + stop, left:right]


def load_rows(info, pieces, places, w, sem, cols=slice(None)):
    copies = []
    for piece, (offset, masks) in zip(pieces, places):
        count = piece.shape[1]
        for k, mask in enumerate(masks):
            slot = 0 if mask is None else (info[1] ^ mask)
            rows = pl.ds(pl.multiple_of(slot * count, 16), count)
            if cols == slice(None):
                src = piece.at[k]
                dst = w.at[rows, pl.ds(offset, piece.shape[2])]
            else:
                src = piece.at[k, :, cols]
                dst = w.at[rows, :]
            copies.append(pltpu.make_async_copy(src, dst, sem.at[len(copies)]))
    for copy in copies:
        copy.start()
    for copy in copies:
        copy.wait()


def store_rows(info, acc, outs, masks, count):
    each = len(masks) // len(outs)
    for at, mask in enumerate(masks):
        slot = 0 if mask is None else (info[1] ^ mask)
        rows = pl.ds(pl.multiple_of(slot * count, 16), count)
        start = at % each * count
        outs[at // each][start : start + count, :] = acc[rows, :].astype(bf16)


def row_products(acc, w, width):
    total = jnp.zeros((acc.shape[0], LANES), f32)
    for at in range(0, width, LANES):
        ps = slice(at, at + LANES)
        total += acc[:, ps] * w[:, ps].astype(f32)
    return total


def forward_kernel(
    places, info, own, oth, consts, tri_r, *rest
):
    count = len(places)
    pieces = rest[:count]
    (
        normed_o, xbc_o, act_o, dsilu_o, step_o, within_o, mixed_o, sin_o, state, buf, w, expand,
        sem,
    ) = rest[count:]
    c = pl.program_id(0)
    half = pl.num_programs(0) // 2
    width = expand.shape[1]
    heads = width // HEAD
    cols = width + 2 * NS
    conv, bias = vector(consts, CONV, cols, 4), vector(consts, BIAS, cols)
    gin, dsk = vector(consts, GIN, own.shape[1]), vector(consts, DSK, width)
    dtb, rate = vector(consts, DTB, LANES), vector(consts, RATE, LANES)

    @pl.when(c == 0)
    def _():
        expand[...] = expander(heads)
        load_rows(info, pieces, places, w, sem)
        state[...] = jnp.zeros_like(state)
        buf[:, 0:8] = jnp.zeros((cols // LANES, 8, LANES), f32)

    mine = (c // half) == info[0]
    r = jnp.where(mine, own[...].astype(f32), oth[...].astype(f32))
    inv = lax.rsqrt(jnp.mean(r * r, axis=1, keepdims=True) + eps)
    normed = (r * inv * gin[...]).astype(bf16)
    normed_o[...] = normed
    step_raw = mm(normed, w[:, cols:])
    step_o[...] = step_raw
    steps = softplus(step_raw + dtb[...])
    within = exact_mm(tri_r[...], steps * rate[...])
    within_o[...] = within
    p_steps, p_grown, p_tails = packs(steps, within)
    within_t = within.T

    def conv_strip(cs):
        n = cs.start // LANES
        v = bias[:, cs] + conv[3:4, cs] * buf[n, 8 : 8 + L]
        for k in range(3):
            v = v + conv[k : k + 1, cs] * buf[n, 5 + k : 5 + k + L]
        buf[n, 0:8] = buf[n, L : L + 8]
        sig = sigmoid(v)
        value = v * sig
        dsilu_o[:, cs] = (sig + value * (1.0 - sig)).astype(bf16)
        act_o[:, cs] = value.astype(bf16)

    for at in range(cols - 2 * LANES, -1, -2 * LANES):
        ws = slice(at, at + 2 * LANES)
        xb = mm(normed, w[:, ws]).astype(bf16)
        xbc_o[:, ws] = xb
        xf = xb.astype(f32)
        buf[at // LANES, 8:] = xf[:, :LANES]
        buf[at // LANES + 1, 8:] = xf[:, LANES:]
        conv_strip(slice(at, at + LANES))
        conv_strip(slice(at + LANES, at + 2 * LANES))

    b = act_o[:, width : width + NS]
    cc = act_o[:, width + NS :]
    bt = turn(b)
    inter = mm(cc, b, NT)
    hl = L // 2
    tri = iota((hl, hl), 0) >= iota((hl, hl), 1)
    left = iota((L, LANES), 1) < HEAD
    zero = jnp.zeros((L, LANES), bf16)
    for quad in range(heads // 4):
        qs = slice(quad * 2 * LANES, (quad + 1) * 2 * LANES)
        steps_e = mm(p_steps, expand[:, qs])
        grown_e = mm(p_grown, expand[:, qs])
        tails_e = mm(p_tails, expand[:, qs])
        x = act_o[:, qs].astype(f32)
        scaled = x * steps_e
        scaled_b = scaled.astype(bf16)
        sin = state[:, qs]
        sin_o[0, :, qs] = sin
        base = mm(cc, sin.astype(bf16)) * grown_e + dsk[:, qs] * x
        state[:, qs] = sin * grown_e[L - 1 : L, :] + mm(bt, (scaled * tails_e).astype(bf16))
        for side in range(2):
            pair = 2 * quad + side
            ls = slice(side * LANES, (side + 1) * LANES)
            ps = slice(pair * LANES, (pair + 1) * LANES)
            x2 = scaled_b[:, ls]
            xe = jnp.where(left, x2, zero)
            xo = jnp.where(left, zero, x2)
            tops, bots = [], []
            for h in (2 * pair, 2 * pair + 1):
                wc = within[:, h : h + 1]
                wr = within_t[h : h + 1, :]
                d_tl = jnp.exp(jnp.where(tri, wc[:hl] - wr[:, :hl], -1e30))
                d_bl = jnp.exp(wc[hl:] - wr[:, :hl])
                d_br = jnp.exp(jnp.where(tri, wc[hl:] - wr[:, hl:], -1e30))
                tops.append((inter[:hl, :hl] * d_tl).astype(bf16))
                bots.append((inter[hl:, :hl] * d_bl).astype(bf16))
                bots.append((inter[hl:, hl:] * d_br).astype(bf16))
            top = mm(
                jnp.concatenate(tops, axis=1), jnp.concatenate([xe[:hl], xo[:hl]], axis=0)
            )
            bot = mm(jnp.concatenate(bots, axis=1), jnp.concatenate([xe, xo], axis=0))
            mixed_o[:hl, ps] = top + base[:hl, ls]
            mixed_o[hl:, ps] = bot + base[hl:, ls]


def gate_kernel(places, info, cown, coth, normed, mixed, consts, *rest):
    count = len(places)
    pieces = rest[:count]
    gate_o, gno_o, sums_o, w, sem = rest[count:]
    c = pl.program_id(0)
    half = pl.num_programs(0) // 2
    width = gate_o.shape[1]
    gout = vector(consts, GOUT, width)

    @pl.when(c == 0)
    def _():
        load_rows(info, pieces, places, w, sem)

    mine = (c // half) == info[0]
    cot = jnp.where(mine, cown[...].astype(f32), coth[...].astype(f32)).astype(bf16)
    squares = jnp.zeros((R, LANES), f32)
    products = jnp.zeros((R, LANES), f32)
    for at in range(0, width, 2 * LANES):
        gate = mm(normed[...], w[:, at : at + 2 * LANES]).astype(bf16)
        gno = mm(cot, w[:, width + at : width + at + 2 * LANES])
        gate_o[:, at : at + 2 * LANES] = gate
        gno_o[:, at : at + 2 * LANES] = gno
        for ls in (slice(0, LANES), slice(LANES, 2 * LANES)):
            ps = slice(at + ls.start, at + ls.stop)
            gf = gate[:, ls].astype(f32)
            gated = mixed[:, ps] * (gf * sigmoid(gf))
            squares += gated * gated
            products += gno[:, ls] * gout[:, ps] * gated
    sums_o[0:8, :] = jnp.broadcast_to(jnp.sum(squares.T, axis=0, keepdims=True), (8, R))
    sums_o[8:16, :] = jnp.broadcast_to(jnp.sum(products.T, axis=0, keepdims=True), (8, R))


def gate_back_kernel(
    places, masks, info, cown, coth, normed, mixed, gate, gno, sown, soth, consts, *rest
):
    count = len(places)
    pieces = rest[:count]
    rest = rest[count:]
    parts = len(rest) - 11
    (sent_o, kept_o, ggate_o, gm_o, ggo_o, gain_o) = rest[:6]
    gw_o = rest[6 : 6 + parts]
    acc, acc_g, w, nout, sem = rest[6 + parts :]
    c = pl.program_id(0)
    last = pl.num_programs(0) - 1
    half = pl.num_programs(0) // 2
    width = gm_o.shape[1]
    gout = vector(consts, GOUT, width)

    @pl.when(c == 0)
    def _():
        load_rows(info, pieces, places, w, sem)
        acc[...] = jnp.zeros_like(acc)
        acc_g[...] = jnp.zeros_like(acc_g)

    cot = jnp.where(c < half, coth[...].astype(f32), cown[...].astype(f32)).astype(bf16)
    inner_total = 2.0 * width
    s = sown[...] + soth[...]
    scale_r = lax.rsqrt(s[0:1] / inner_total + eps)
    coef_r = scale_r * scale_r * scale_r * (s[8:9] / inner_total)
    scale = jnp.broadcast_to(scale_r, (LANES, R)).T
    coef = jnp.broadcast_to(coef_r, (LANES, R)).T
    for at in range(0, width, LANES):
        ps = slice(at, at + LANES)
        gain = gout[:, ps]
        gf = gate[:, ps].astype(f32)
        sig = sigmoid(gf)
        silu = gf * sig
        mix = mixed[:, ps]
        gated = mix * silu
        grad = gno[:, ps]
        unit = gated * scale
        nout[:, ps] = (unit * gain).astype(bf16)
        acc_g[:, ps] += fold8(grad * unit)
        grad_gated = scale * (grad * gain) - gated * coef
        ggate_o[:, ps] = (grad_gated * mix * (sig + silu * (1.0 - sig))).astype(bf16)
        gm_o[:, ps] = (grad_gated * silu).astype(bf16)
    branch = mm(nout[...], w[:, width:], NT).astype(bf16)

    @pl.when(c < half)
    def _():
        sent_o[...] = branch

    @pl.when(c >= half)
    def _():
        kept_o[...] = branch

    acc[:, :width] += mm(normed[...], ggate_o[...], TN)
    acc[:, width:] += mm(cot, nout[...], TN)

    @pl.when(c == last)
    def _():
        store_rows(info, acc, gw_o, masks, acc.shape[0] // len(masks))
        ggo_o[...] = acc_g[...]
        gain_o[...] = row_products(acc, w, width)


def scan_back_kernel(
    masks, places, info, xbc, act_r, dsilu, step, within_r, mixed, sin_r, gm, normed, consts,
    tri_r, ggo, gain_z, *rest,
):
    count = len(places)
    pieces = rest[:count]
    gx_o, small_o = rest[count : count + 2]
    gw_o = rest[count + 2 : -10]
    dstate, dvbuf, acc_w, acc_c, acc_s, acc_h, w, expand, collect, sem = rest[-10:]
    i = pl.program_id(0)
    last = pl.num_programs(0) - 1
    width = expand.shape[1]
    heads = width // HEAD
    cols = width + 2 * NS
    conv, dsk = vector(consts, CONV, cols, 4), vector(consts, DSK, width)
    dtb, rate = vector(consts, DTB, LANES), vector(consts, RATE, LANES)

    @pl.when(i == 0)
    def _():
        expand[...] = expander(heads)
        collect[...] = collector(heads)
        load_rows(info, pieces, places, w, sem)
        dstate[...] = jnp.zeros_like(dstate)
        dvbuf[...] = jnp.zeros_like(dvbuf)
        acc_w[...] = jnp.zeros_like(acc_w)
        acc_c[...] = jnp.zeros_like(acc_c)
        acc_s[...] = jnp.zeros_like(acc_s)
        acc_h[...] = jnp.zeros_like(acc_h)

    def conv_strip(dpost, cs):
        dv = dpost * dsilu[:, cs].astype(f32)
        n = cs.start // LANES
        dvbuf[n, 0:L] = dv
        xin = xbc[:, cs].astype(f32)
        acc_c[4, :, cs] += fold8(dv)
        acc_c[3, :, cs] += fold8(dv * xin)
        dxin = conv[3:4, cs] * dv
        for k in range(3):
            ahead = dvbuf[n, 3 - k : 3 - k + L]
            acc_c[k, :, cs] += fold8(ahead * xin)
            dxin = dxin + conv[k : k + 1, cs] * ahead
        dvbuf[n, L : L + 8] = dv[0:8, :]
        gx_o[:, cs] = dxin.astype(bf16)

    b = act_r[:, width : width + NS]
    cc = act_r[:, width + NS :]
    ct = turn(cc)
    step_raw = step[...]
    within = within_r[...]
    steps = softplus(step_raw + dtb[...])
    p_steps, p_grown, p_tails = packs(steps, within)
    within_t = within.T
    inter_t = mm(b, cc, NT)
    hl = L // 2
    tri = iota((hl, hl), 0) <= iota((hl, hl), 1)
    left = iota((L, LANES), 1) < HEAD
    zero = jnp.zeros((L, LANES), bf16)
    dg_tl = jnp.zeros((hl, hl), f32)
    dg_tr = jnp.zeros((hl, hl), f32)
    dg_br = jnp.zeros((hl, hl), f32)
    dc = jnp.zeros((L, NS), f32)
    db = jnp.zeros((L, NS), f32)
    q_h = jnp.zeros((L, LANES), f32)
    s_h = jnp.zeros((L, LANES), f32)
    ends_h = jnp.zeros((8, LANES), f32)
    for quad in range(heads // 4):
        qs = slice(quad * 2 * LANES, (quad + 1) * 2 * LANES)
        steps_e = mm(p_steps, expand[:, qs])
        grown_e = mm(p_grown, expand[:, qs])
        tails_e = mm(p_tails, expand[:, qs])
        x = act_r[:, qs].astype(f32)
        scaled = x * steps_e
        scaled_b = scaled.astype(bf16)
        scaled_f = scaled_b.astype(f32)
        gmb = gm[:, qs]
        gmf = gmb.astype(f32)
        ds = dstate[:, qs]
        ds_b = ds.astype(bf16)
        sin = sin_r[0, :, qs]
        last_grown = grown_e[L - 1 : L, :]
        gm_grown = (gmf * grown_e).astype(bf16)
        dc += mm(gm_grown, sin.astype(bf16), NT)
        db += mm((scaled * tails_e).astype(bf16), ds_b, NT)
        dstate[:, qs] = ds * last_grown + mm(ct, gm_grown)
        state_part = mm(b, ds_b) * tails_e
        ends = jnp.sum(scaled_f * state_part, axis=0, keepdims=True) + last_grown * jnp.sum(
            sin * ds, axis=0, keepdims=True
        )
        collect_q = collect[qs, :]
        ends_h += head_sums(jnp.broadcast_to(ends, (8, 2 * LANES)), collect_q)
        his, los, prods = [], [], []
        for side in range(2):
            pair = 2 * quad + side
            ls = slice(side * LANES, (side + 1) * LANES)
            ps = slice(pair * LANES, (pair + 1) * LANES)
            x2 = scaled_b[:, ls]
            g2 = gmb[:, ls]
            ge = jnp.where(left, g2, zero)
            go = jnp.where(left, zero, g2)
            g_both = jnp.concatenate([ge, go], axis=0)
            g_bot = jnp.concatenate([ge[hl:], go[hl:]], axis=0)
            dm_top = mm(x2[:hl], g_both, NT)
            dm_bot = mm(x2[hl:], g_bot, NT)
            tops, bots = [], []
            for k, h in enumerate((2 * pair, 2 * pair + 1)):
                wc = within[:, h : h + 1]
                wr = within_t[h : h + 1, :]
                d_tl = jnp.exp(jnp.where(tri, wr[:, :hl] - wc[:hl], -1e30))
                d_tr = jnp.exp(wr[:, hl:] - wc[:hl])
                d_br = jnp.exp(jnp.where(tri, wr[:, hl:] - wc[hl:], -1e30))
                tops.append((inter_t[:hl, :hl] * d_tl).astype(bf16))
                tops.append((inter_t[:hl, hl:] * d_tr).astype(bf16))
                bots.append((inter_t[hl:, hl:] * d_br).astype(bf16))
                dg_tl += dm_top[:, k * L : k * L + hl] * d_tl
                dg_tr += dm_top[:, k * L + hl : (k + 1) * L] * d_tr
                dg_br += dm_bot[:, k * hl : (k + 1) * hl] * d_br
            top = mm(jnp.concatenate(tops, axis=1), g_both)
            bot = mm(jnp.concatenate(bots, axis=1), g_bot)
            dscaled = jnp.concatenate([top, bot], axis=0) + state_part[:, ls]
            xs = x[:, ls]
            gs = gmf[:, ls]
            y = mixed[:, ps] - dsk[:, ps] * xs
            q = gs * y - scaled_f[:, ls] * dscaled
            hi = q.astype(bf16)
            his.append(hi)
            los.append((q - hi.astype(f32)).astype(bf16))
            prods.append((dscaled * xs).astype(bf16))
            acc_s[:, ps] += fold8(gs * xs)
            conv_strip(dscaled * steps_e[:, ls] + dsk[:, ps] * gs, ps)
        q_h += mm(jnp.concatenate(his, axis=1), collect_q)
        q_h += mm(jnp.concatenate(los, axis=1), collect_q)
        s_h += mm(jnp.concatenate(prods, axis=1), collect_q)
    top = jnp.concatenate([dg_tl, dg_tr], axis=1)
    bot = jnp.concatenate([jnp.zeros((hl, hl), f32), dg_br], axis=1)
    dg = jnp.concatenate([top, bot], axis=0)
    dc += mm(dg.T.astype(bf16), b)
    db += mm(dg.astype(bf16), cc)
    conv_strip(db, slice(width, width + NS))
    conv_strip(dc, slice(width + NS, cols))
    d_rate = exact_mm(tri_r[...], q_h) + ends_h[0:1, :]
    d_steps = d_rate * rate[...] + s_h
    sig_s = sigmoid(step_raw + dtb[...])
    keep = iota((L, LANES), 1) < heads
    d_raw = jnp.where(keep, d_steps * sig_s, 0.0)
    acc_h[0:8, :] += fold8(d_raw)
    acc_h[8:16, :] += fold8(d_rate * steps * rate[...])
    gx_o[:, cols:] = d_raw.astype(bf16)
    acc_w[...] += mm(normed[...], gx_o[...], TN)

    @pl.when(i == last)
    def _():
        store_rows(info, acc_w, gw_o, masks, acc_w.shape[0] // len(masks))
        small_o[...] = jnp.zeros_like(small_o)
        for k in range(5):
            small_o[k : k + 1, :cols] = jnp.sum(acc_c[k], axis=0, keepdims=True)
        for k in range(2):
            head = acc_h[8 * k : 8 * k + 8, :]
            small_o[k : k + 1, cols:] = jnp.sum(head, axis=0, keepdims=True)
        small_o[5:6, :width] = jnp.sum(acc_s[...], axis=0, keepdims=True)
        small_o[6:7, :width] = jnp.sum(ggo[...], axis=0, keepdims=True)
        gains = row_products(acc_w, w, cols + LANES) + gain_z[...]
        small_o[7:8, : acc_w.shape[0]] = jnp.sum(gains.T, axis=0, keepdims=True)
        if len(gw_o) > 1:
            small = small_o[...]
            hi = small.astype(bf16).astype(f32)
            parts = jnp.concatenate([hi, small - hi], axis=0).astype(bf16)
            for out in gw_o:
                out[out.shape[0] - 16 :, :] = parts


def input_back_kernel(zplaces, xplaces, info, ggate, gx, *rest):
    zcount, xcount = len(zplaces), len(xplaces)
    zpieces = rest[:zcount]
    xpieces = rest[zcount : zcount + xcount]
    sent_o, kept_o, wz, wx, dnb, zsem, xsem = rest[zcount + xcount :]
    c = pl.program_id(0)
    half = pl.num_programs(0) // 2
    width = ggate.shape[1]

    @pl.when(c == 0)
    def _():
        load_rows(info, zpieces, zplaces, wz, zsem, pl.ds(0, width))
        load_rows(info, xpieces, xplaces, wx, xsem)

    dim = dnb.shape[1]
    for at in range(0, dim, 2 * LANES):
        ds = slice(at, at + 2 * LANES)
        dn = mm(ggate[...], wz[ds, :], NT) + mm(gx[...], wx[ds, :], NT)
        dnb[:, ds] = dn.astype(bf16)

    @pl.when(c < half)
    def _():
        sent_o[...] = dnb[...]

    @pl.when(c >= half)
    def _():
        kept_o[...] = dnb[...]


def finish_kernel(resid, cot, consts, dn_own, dn_oth, br_own, br_oth, out_o, gres_o):
    r = resid[...].astype(f32)
    inv = lax.rsqrt(jnp.mean(r * r, axis=1, keepdims=True) + eps)
    out_o[...] = (r + (br_own[...].astype(f32) + br_oth[...].astype(f32))).astype(bf16)
    gin = consts[GIN : GIN + 1, : r.shape[1]]
    u = (dn_own[...].astype(f32) + dn_oth[...].astype(f32)) * gin
    mean = jnp.mean(u * r, axis=1, keepdims=True)
    gres_o[...] = cot[...].astype(f32) + inv * u - r * (inv * inv * inv * mean)


def swap(v, bit, axis):
    size = lax.axis_size(axis)
    return lax.ppermute(v, axis, [(i, i ^ bit) for i in range(size)])


NEAR = (0, 1, 2, 3)
FAR = (0, 4, 8, 12)


def direct(size, rows):
    return size == 16 and rows % 16 == 0


def gather_whole(v, bits):
    size = lax.axis_size("dp")
    me = lax.axis_index("dp")
    held = v[None]
    for bit in sorted(bits):
        got = swap(held, bit, "dp")
        upper = (me & bit) != 0
        held = jnp.where(
            upper, jnp.concatenate([got, held]), jnp.concatenate([held, got])
        )
    return held.reshape(1, size * v.shape[0], v.shape[1])


def whole_pieces(v, bits):
    return [gather_whole(v, bits)], [(0, (None,))]


def gather_far(v):
    return [swap(v, far, "dp") for far in FAR[1:]]


def gather_near(held):
    pieces = [held] + [swap(held, near, "dp") for near in NEAR[1:]]
    return pieces, [(0, tuple(near ^ far for far in FAR)) for near in NEAR]


def scatter_shapes(size, rows, cols, extra=0):
    if not direct(size, rows):
        return [jax.ShapeDtypeStruct((size * rows, cols), bf16)], (None,)
    masks = tuple(near ^ far for near in NEAR for far in FAR)
    return [jax.ShapeDtypeStruct((4 * rows + extra, cols), bf16)] * 4, masks


def both_parts(v):
    return v[-16:-8] + v[-8:]


def scatter_near(pieces):
    return [pieces[0]] + [swap(p, near, "dp") for p, near in zip(pieces[1:], NEAR[1:])]


def scatter_far(total, rows, extra=None):
    blocks = [total[k * rows : (k + 1) * rows] for k in range(4)]
    if extra is not None:
        hi = extra.astype(bf16).astype(f32)
        parts = jnp.concatenate([hi, (extra - hi).astype(bf16).astype(f32)])
        blocks = [jnp.concatenate([block, parts]) for block in blocks]
    sent = [swap(block.astype(bf16), far, "dp") for block, far in zip(blocks[1:], FAR[1:])]
    return blocks[:1] + sent


def sum_pieces(pieces):
    return sum(p.astype(f32) for p in pieces)


def scatter_whole(g, bits):
    me = lax.axis_index("dp")
    rows = g.shape[0] // lax.axis_size("dp")
    left = sorted(bits, reverse=True)
    cur = g.reshape([2] * len(left) + [rows, g.shape[1]])
    for bit in sorted(bits):
        dim = left.index(bit)
        mine = ((me & bit) != 0).astype(jnp.int32)
        send = lax.dynamic_index_in_dim(cur, 1 - mine, dim, keepdims=False)
        keep = lax.dynamic_index_in_dim(cur, mine, dim, keepdims=False)
        got = swap(send.astype(bf16), bit, "dp")
        cur = keep.astype(f32) + got.astype(f32)
        left.pop(dim)
    return cur.astype(f32)


def full(shape):
    zeros = (0,) * len(shape)
    return pl.BlockSpec(shape, lambda c, *_: zeros)


def rows_spec(count, width, index=lambda c, info: c):
    return pl.BlockSpec((count, width), lambda c, info: (index(c, info), 0))


def call(kernel, name, vmem, grid, ins, outs, scratch, info, *args, **more):
    specs = [spec for spec, _ in outs]
    shapes = [item for _, item in outs]
    return pl.pallas_call(
        kernel,
        grid_spec=pltpu.PrefetchScalarGridSpec(
            num_scalar_prefetch=1, grid=(grid,), in_specs=ins, out_specs=specs,
            scratch_shapes=scratch,
        ),
        out_shape=shapes,
        compiler_params=pltpu.CompilerParams(
            dimension_semantics=("arbitrary",), vmem_limit_bytes=vmem * MIB
        ),
        name=name,
        **more,
    )(info, *args)


def local(
    resid, gain_in, w_z, w_x, w_bc, w_dt, conv_x, bias_x, conv_bc, bias_bc, dt_bias, a_log, d_skip,
    gain_out, w_out, cotangent,
):
    size = lax.axis_size("dp")
    place = lax.axis_index("tensor")
    heads = a_log.shape[0]
    width = heads * HEAD
    dim = resid.shape[1]
    rows = w_z.shape[0]
    cols = width + 2 * NS
    half_rows = resid.shape[0]
    tokens = 2 * half_rows
    assert tokens == SEQ_LEN
    chunks = tokens // L
    half = chunks // 2
    shape = jax.ShapeDtypeStruct
    bits = [1 << k for k in range(size.bit_length() - 1)]

    def lanes3(v):
        pad = [(0, 0)] * (v.ndim - 1)
        group = jnp.pad(v, pad + [(0, 16 - heads)])
        return jnp.pad(jnp.concatenate([group] * 3, axis=-1), pad + [(0, LANES - 48)])

    first = jnp.concatenate([w_x, w_bc, lanes3(w_dt)], axis=1)
    second = jnp.concatenate([w_z, w_out.T], axis=1)
    def row(v):
        return jnp.pad(v, ((0, 0), (0, cols - v.shape[1])))

    consts = jnp.concatenate(
        [
            jnp.concatenate([conv_x, conv_bc], axis=1),
            jnp.concatenate([bias_x, bias_bc])[None],
            row(gain_in[None]),
            row(gain_out[None]),
            row(jnp.repeat(d_skip, HEAD)[None]),
            row(lanes3(dt_bias[None])),
            row(lanes3(-jnp.exp(a_log)[None])),
            jnp.zeros((6, cols), f32),
        ]
    )
    if direct(size, rows):
        many = jnp.concatenate([first[:, :width], second], axis=1)
        few = first[:, width:]
        got_many = gather_far(many)
        got_few = [swap(few, near, "dp") for near in NEAR[1:]]
        many, got_many, few, got_few, resid_in, cot_in, consts = lax.optimization_barrier(
            (many, got_many, few, got_few, resid, cotangent, consts)
        )
        held = [many] + got_many
        few = jnp.stack([few] + got_few)
        wx = [few] + [swap(few, far, "dp") for far in FAR[1:]]
        wx_at = [(width, tuple(near ^ far for near in NEAR)) for far in FAR]
        near_x, near_at = gather_near(jnp.stack([v[:, :width] for v in held]))
        wx, wx_at = near_x + wx, near_at + wx_at
        resid_oth = swap(resid_in, 1, "tensor")
        cot_oth = swap(cot_in, 1, "tensor")
        held, resid_oth, cot_oth, wx = lax.optimization_barrier((held, resid_oth, cot_oth, wx))
        wz, wz_at = gather_near(jnp.stack([v[:, width:] for v in held]))
    else:
        resid_oth = swap(resid, 1, "tensor")
        cot_oth = swap(cotangent, 1, "tensor")
        wx, wx_at = whole_pieces(first, bits)
        wz, wz_at = whole_pieces(second, bits)

    info = jnp.stack([place, lax.axis_index("dp")]).astype(jnp.int32)
    anywhere = pl.BlockSpec(memory_space=pltpu.HBM)

    def copies(at):
        return pltpu.SemaphoreType.DMA((sum(len(masks) for _, masks in at),))

    def tok(width, dtype):
        return shape((tokens, width), dtype)

    own_spec = rows_spec(L, dim, lambda c, info: jnp.clip(c - half * info[0], 0, half - 1))
    oth_spec = rows_spec(L, dim, lambda c, info: jnp.clip(c - half * (1 - info[0]), 0, half - 1))
    wide = rows_spec(L, width)
    normed, xbc, act, dsilu, step_raw, within, mixed, sin = call(
        functools.partial(forward_kernel, wx_at),
        "mix_forward",
        52,
        chunks,
        [
            own_spec, oth_spec, full((16, cols)), full((L, L)),
        ]
        + [anywhere] * len(wx),
        [
            (rows_spec(L, dim), tok(dim, bf16)),
            (rows_spec(L, cols), tok(cols, bf16)),
            (rows_spec(L, cols), tok(cols, bf16)),
            (rows_spec(L, cols), tok(cols, bf16)),
            (rows_spec(L, LANES), tok(LANES, f32)),
            (rows_spec(L, LANES), tok(LANES, f32)),
            (wide, tok(width, f32)),
            (
                pl.BlockSpec((1, NS, width), lambda c, info: (c, 0, 0)),
                shape((chunks, NS, width), f32),
            ),
        ],
        [
            pltpu.VMEM((NS, width), f32), pltpu.VMEM((cols // LANES, L + 8, LANES), f32),
            pltpu.VMEM((dim, cols + LANES), bf16), pltpu.VMEM((LANES, width), bf16),
            copies(wx_at),
        ],
        info, resid, resid_oth, consts, lower_tri(), *wx,
    )

    steps = tokens // R
    rhalf = steps // 2

    def block(width, index=lambda c, info: c):
        return rows_spec(R, width, index)

    own_r = block(dim, lambda c, info: jnp.clip(c - rhalf * info[0], 0, rhalf - 1))
    oth_r = block(dim, lambda c, info: jnp.clip(c - rhalf * (1 - info[0]), 0, rhalf - 1))
    sums_shape = shape((steps * 16, R), f32)
    gate, gno, sums = call(
        functools.partial(gate_kernel, wz_at),
        "gate_forward",
        52,
        steps,
        [own_r, oth_r, block(dim), block(width), full((16, cols))] + [anywhere] * len(wz),
        [
            (block(width), tok(width, bf16)), (block(width), tok(width, f32)),
            (rows_spec(16, R), sums_shape),
        ],
        [pltpu.VMEM((dim, 2 * width), bf16), copies(wz_at)],
        info, cotangent, cot_oth, normed, mixed, consts, *wz,
    )
    sums_oth = swap(sums, 1, "tensor")

    def turned(c, info):
        return jnp.where(c < rhalf, c + rhalf * (1 - info[0]), c - rhalf + rhalf * info[0])

    gw_shapes, masks = scatter_shapes(size, rows, 2 * width)
    twide = block(width, turned)
    lead = block(dim, lambda c, info: jnp.minimum(c, rhalf - 1))
    trail = block(dim, lambda c, info: jnp.maximum(c - rhalf, 0))
    half_shape = shape((half_rows, dim), bf16)
    branch_sent, branch_own, ggate, gm, g_gout, g_gin_z, *gw_zo = call(
        functools.partial(gate_back_kernel, wz_at, masks),
        "gate_backward",
        52,
        steps,
        [
            trail, lead, block(dim, turned), twide, twide, twide,
            rows_spec(16, R, turned), rows_spec(16, R, turned), full((16, cols)),
        ]
        + [anywhere] * len(wz),
        [
            (lead, half_shape), (trail, half_shape), (twide, tok(width, bf16)),
            (twide, tok(width, bf16)), (full((8, width)), shape((8, width), f32)),
            (full((dim, LANES)), shape((dim, LANES), f32)),
        ]
        + [(full(item.shape), item) for item in gw_shapes],
        [
            pltpu.VMEM((dim, 2 * width), f32), pltpu.VMEM((8, width), f32),
            pltpu.VMEM((dim, 2 * width), bf16), pltpu.VMEM((R, width), bf16), copies(wz_at),
        ],
        info, cotangent, cot_oth, normed, mixed, gate, gno, sums, sums_oth, consts, *wz,
    )
    branch_oth = swap(branch_sent, 1, "tensor")
    sent_zo = scatter_near(gw_zo) if direct(size, rows) else gw_zo

    def back(c, info):
        return chunks - 1 - c

    rwide = rows_spec(L, width, back)
    rcols = rows_spec(L, cols, back)
    rlanes = rows_spec(L, LANES, back)
    gwx_shapes, masks = scatter_shapes(size, rows, cols + LANES, 16)
    gx, small, *gw_x = call(
        functools.partial(scan_back_kernel, masks, wx_at),
        "mix_backward",
        52,
        chunks,
        [
            rcols, rcols, rcols, rlanes, rlanes, rwide,
            pl.BlockSpec((1, NS, width), lambda c, info: (chunks - 1 - c, 0, 0)),
            rwide, rows_spec(L, dim, back), full((16, cols)),
            full((L, L)), full((8, width)), full((dim, LANES)),
        ]
        + [anywhere] * len(wx),
        [
            (rows_spec(L, cols + LANES, back), tok(cols + LANES, bf16)),
            (full((8, cols + LANES)), shape((8, cols + LANES), f32)),
        ]
        + [(full(item.shape), item) for item in gwx_shapes],
        [
            pltpu.VMEM((NS, width), f32), pltpu.VMEM((cols // LANES, L + 8, LANES), f32),
            pltpu.VMEM((dim, cols + LANES), f32), pltpu.VMEM((5, 8, cols), f32),
            pltpu.VMEM((8, width), f32), pltpu.VMEM((16, LANES), f32),
            pltpu.VMEM((dim, cols + LANES), bf16), pltpu.VMEM((LANES, width), bf16),
            pltpu.VMEM((width, LANES), bf16), copies(wx_at),
        ],
        info, xbc, act, dsilu, step_raw, within, mixed, sin, gm, normed, consts,
        upper_tri(), g_gout, g_gin_z, *wx,
    )

    sent_zo, branch_oth, gx, gw_x, small = lax.optimization_barrier(
        (sent_zo, branch_oth, gx, gw_x, small)
    )
    if direct(size, rows):
        sent_x = scatter_near(gw_x)
        far_zo = scatter_far(sum_pieces(sent_zo), rows)

    dn_sent, dn_own = call(
        functools.partial(input_back_kernel, wz_at, wx_at),
        "input_backward",
        32,
        steps,
        [twide, block(cols + LANES, turned)]
        + [anywhere] * (len(wz) + len(wx)),
        [(lead, half_shape), (trail, half_shape)],
        [
            pltpu.VMEM((dim, width), bf16), pltpu.VMEM((dim, cols + LANES), bf16),
            pltpu.VMEM((R, dim), bf16), copies(wz_at), copies(wx_at),
        ],
        info, ggate, gx, *wz, *wx,
    )
    if direct(size, rows):
        sent_x, dn_own, dn_sent = lax.optimization_barrier((sent_x, dn_own, dn_sent))
    dn_oth = swap(dn_sent, 1, "tensor")
    if direct(size, rows):
        total_x = sum_pieces(sent_x)
        far_x = scatter_far(total_x, rows, both_parts(total_x))
        far_zo, dn_oth, dn_own = lax.optimization_barrier((far_zo, dn_oth, dn_own))
        sum_zo = sum_pieces(far_zo)

    dspec = rows_spec(L, dim)
    block_out, grad_resid = call(
        lambda info, *refs: finish_kernel(*refs),
        "finish",
        12,
        half,
        [dspec, dspec, full((16, cols)), dspec, dspec, dspec, dspec],
        [(dspec, half_shape), (dspec, shape((half_rows, dim), f32))],
        [],
        info, resid, cotangent, consts, dn_own, dn_oth, branch_own, branch_oth,
    )

    if direct(size, rows):
        block_out, grad_resid, far_x = lax.optimization_barrier((block_out, grad_resid, far_x))
        sum_x = sum_pieces(far_x)
        small = both_parts(sum_x)
    else:
        sum_zo = scatter_whole(sent_zo[0], bits)
        sum_x = scatter_whole(gw_x[0], bits)
        for bit in bits:
            small = small + swap(small, bit, "dp")
    grad_w_bc = sum_x[:rows, width:cols]
    pair = jnp.concatenate(
        [grad_w_bc.reshape(-1), small[:5, width:cols].reshape(-1), small[7, :dim]]
    )
    pair = pair + swap(pair, 1, "tensor")
    grad_w_bc, bc_g, gain_g = jnp.split(pair, [rows * 2 * NS, (rows + 5) * 2 * NS])
    bc_g = bc_g.reshape(5, 2 * NS)
    return (
        block_out, grad_resid, gain_g / gain_in, sum_zo[:, :width], sum_x[:rows, :width],
        grad_w_bc.reshape(rows, 2 * NS), sum_x[:rows, cols : cols + heads],
        small[:4, :width], small[4, :width], bc_g[:4], bc_g[4], small[0, cols : cols + heads],
        small[1, cols : cols + heads], small[5, :width].reshape(heads, HEAD).sum(axis=1),
        small[6, :width], sum_zo[:, width:].T,
    )


def solution(mesh):
    in_specs = (
        P(("dp", "tensor"), None),
        P(),
        P("dp", "tensor"),
        P("dp", "tensor"),
        P("dp", None),
        P("dp", "tensor"),
        P(None, "tensor"),
        P("tensor"),
        P(),
        P(),
        P("tensor"),
        P("tensor"),
        P("tensor"),
        P("tensor"),
        P("tensor", "dp"),
        P(("dp", "tensor"), None),
    )
    out_specs = (
        P(("dp", "tensor"), None),
        P(("dp", "tensor"), None),
        P(),
        P("dp", "tensor"),
        P("dp", "tensor"),
        P("dp", None),
        P("dp", "tensor"),
        P(None, "tensor"),
        P("tensor"),
        P(),
        P(),
        P("tensor"),
        P("tensor"),
        P("tensor"),
        P("tensor"),
        P("tensor", "dp"),
    )
    return jax.shard_map(local, mesh=mesh, in_specs=in_specs, out_specs=out_specs, check_vma=False)
```

```python
import functools

import jax
import jax.numpy as jnp
from jax import lax
from jax.experimental import pallas as pl
from jax.experimental.pallas import tpu as pltpu
from jax.sharding import PartitionSpec as P

NS = 128
L = 256
R = 512
SEQ_LEN = 2048
HEAD = 64
LANES = 128
MIB = 1024 * 1024

f32 = jnp.float32
bf16 = jnp.bfloat16
highest = lax.Precision.HIGHEST
eps = 1e-05

NN = (((1,), (0,)), ((), ()))
NT = (((1,), (1,)), ((), ()))
TN = (((0,), (0,)), ((), ()))


def mm(a, b, dims=NN, precision=None):
    return lax.dot_general(a, b, dims, precision=precision, preferred_element_type=f32)


def iota(shape, dim):
    return lax.broadcasted_iota(jnp.int32, shape, dim)


def lower_tri():
    return (iota((L, L), 0) >= iota((L, L), 1)).astype(bf16)


def upper_tri():
    return (iota((L, L), 0) <= iota((L, L), 1)).astype(bf16)


def expander(heads):
    rows = iota((LANES, heads * HEAD), 0)
    cols = iota((LANES, heads * HEAD), 1) // HEAD
    return ((rows % 16 == cols) & (rows < 48)).astype(bf16)


def collector(heads):
    rows = iota((heads * HEAD, LANES), 0) // HEAD
    cols = iota((heads * HEAD, LANES), 1)
    return ((cols % 16 == rows) & (cols < 48)).astype(bf16)


def split3(q):
    hi = q.astype(bf16).astype(f32)
    rest = q - hi
    mid = rest.astype(bf16).astype(f32)
    return hi, mid, rest - mid


def pack3(q):
    lane = iota(q.shape, 1)
    hi, mid, low = split3(q)
    return jnp.where(lane < 16, hi, jnp.where(lane < 32, mid, low)).astype(bf16)


def exact_mm(a, q):
    return sum(mm(a, part.astype(bf16)) for part in split3(q))


def turn(v):
    return v.astype(f32).T.astype(bf16)


def head_sums(q, col):
    hi = q.astype(bf16)
    lo = (q - hi.astype(f32)).astype(bf16)
    return mm(hi, col) + mm(lo, col)


def softplus(v):
    return jnp.maximum(v, 0.0) + jnp.log1p(jnp.exp(-jnp.abs(v)))


def sigmoid(v):
    return 0.5 * jnp.tanh(0.5 * v) + 0.5


def fold8(q):
    return jnp.sum(q.reshape(q.shape[0] // 8, 8, q.shape[1]), axis=0)


def packs(steps, within):
    tails = jnp.exp(within[L - 1 : L, :] - within)
    return pack3(steps), pack3(jnp.exp(within)), pack3(tails)


CONV, BIAS, GIN, GOUT, DSK, DTB, RATE = 0, 4, 5, 6, 7, 8, 9


class vector:
    def __init__(self, ref, at, width, count=1):
        self.ref, self.at, self.width, self.count = ref, at, width, count

    def __getitem__(self, key):
        rows, cols = (slice(None), slice(None)) if key is Ellipsis else key
        start, stop, _ = rows.indices(self.count)
        left, right, _ = cols.indices(self.width)
        return self.ref[self.at + start : self.at + stop, left:right]


def load_rows(info, pieces, places, w, sem, cols=slice(None)):
    copies = []
    for piece, (offset, masks) in zip(pieces, places):
        count = piece.shape[1]
        for k, mask in enumerate(masks):
            slot = 0 if mask is None else (info[1] ^ mask)
            rows = pl.ds(pl.multiple_of(slot * count, 16), count)
            if cols == slice(None):
                src = piece.at[k]
                dst = w.at[rows, pl.ds(offset, piece.shape[2])]
            else:
                src = piece.at[k, :, cols]
                dst = w.at[rows, :]
            copies.append(pltpu.make_async_copy(src, dst, sem.at[len(copies)]))
    for copy in copies:
        copy.start()
    for copy in copies:
        copy.wait()


def store_rows(info, acc, outs, masks, count):
    each = len(masks) // len(outs)
    for at, mask in enumerate(masks):
        slot = 0 if mask is None else (info[1] ^ mask)
        rows = pl.ds(pl.multiple_of(slot * count, 16), count)
        start = at % each * count
        outs[at // each][start : start + count, :] = acc[rows, :].astype(bf16)


def row_products(acc, w, width):
    total = jnp.zeros((acc.shape[0], LANES), f32)
    for at in range(0, width, LANES):
        ps = slice(at, at + LANES)
        total += acc[:, ps] * w[:, ps].astype(f32)
    return total


def forward_kernel(
    places, info, own, oth, consts, tri_r, *rest
):
    count = len(places)
    pieces = rest[:count]
    (
        normed_o, xbc_o, act_o, dsilu_o, step_o, within_o, mixed_o, sin_o, state, buf, w, expand,
        sem,
    ) = rest[count:]
    c = pl.program_id(0)
    half = pl.num_programs(0) // 2
    width = expand.shape[1]
    heads = width // HEAD
    cols = width + 2 * NS
    conv, bias = vector(consts, CONV, cols, 4), vector(consts, BIAS, cols)
    gin, dsk = vector(consts, GIN, own.shape[1]), vector(consts, DSK, width)
    dtb, rate = vector(consts, DTB, LANES), vector(consts, RATE, LANES)

    @pl.when(c == 0)
    def _():
        expand[...] = expander(heads)
        load_rows(info, pieces, places, w, sem)
        state[...] = jnp.zeros_like(state)
        buf[:, 0:8] = jnp.zeros((cols // LANES, 8, LANES), f32)

    mine = (c // half) == info[0]
    r = jnp.where(mine, own[...].astype(f32), oth[...].astype(f32))
    inv = lax.rsqrt(jnp.mean(r * r, axis=1, keepdims=True) + eps)
    normed = (r * inv * gin[...]).astype(bf16)
    normed_o[...] = normed
    step_raw = mm(normed, w[:, cols:])
    step_o[...] = step_raw
    steps = softplus(step_raw + dtb[...])
    within = exact_mm(tri_r[...], steps * rate[...])
    within_o[...] = within
    p_steps, p_grown, p_tails = packs(steps, within)
    within_t = within.T

    def conv_strip(cs):
        n = cs.start // LANES
        v = bias[:, cs] + conv[3:4, cs] * buf[n, 8 : 8 + L]
        for k in range(3):
            v = v + conv[k : k + 1, cs] * buf[n, 5 + k : 5 + k + L]
        buf[n, 0:8] = buf[n, L : L + 8]
        sig = sigmoid(v)
        value = v * sig
        dsilu_o[:, cs] = (sig + value * (1.0 - sig)).astype(bf16)
        act_o[:, cs] = value.astype(bf16)

    for at in range(cols - 2 * LANES, -1, -2 * LANES):
        ws = slice(at, at + 2 * LANES)
        xb = mm(normed, w[:, ws]).astype(bf16)
        xbc_o[:, ws] = xb
        xf = xb.astype(f32)
        buf[at // LANES, 8:] = xf[:, :LANES]
        buf[at // LANES + 1, 8:] = xf[:, LANES:]
        conv_strip(slice(at, at + LANES))
        conv_strip(slice(at + LANES, at + 2 * LANES))

    b = act_o[:, width : width + NS]
    cc = act_o[:, width + NS :]
    bt = turn(b)
    inter = mm(cc, b, NT)
    hl = L // 2
    tri = iota((hl, hl), 0) >= iota((hl, hl), 1)
    left = iota((L, LANES), 1) < HEAD
    zero = jnp.zeros((L, LANES), bf16)
    for quad in range(heads // 4):
        qs = slice(quad * 2 * LANES, (quad + 1) * 2 * LANES)
        steps_e = mm(p_steps, expand[:, qs])
        grown_e = mm(p_grown, expand[:, qs])
        tails_e = mm(p_tails, expand[:, qs])
        x = act_o[:, qs].astype(f32)
        scaled = x * steps_e
        scaled_b = scaled.astype(bf16)
        sin = state[:, qs]
        sin_o[0, :, qs] = sin
        base = mm(cc, sin.astype(bf16)) * grown_e + dsk[:, qs] * x
        state[:, qs] = sin * grown_e[L - 1 : L, :] + mm(bt, (scaled * tails_e).astype(bf16))
        for side in range(2):
            pair = 2 * quad + side
            ls = slice(side * LANES, (side + 1) * LANES)
            ps = slice(pair * LANES, (pair + 1) * LANES)
            x2 = scaled_b[:, ls]
            xe = jnp.where(left, x2, zero)
            xo = jnp.where(left, zero, x2)
            tops, bots = [], []
            for h in (2 * pair, 2 * pair + 1):
                wc = within[:, h : h + 1]
                wr = within_t[h : h + 1, :]
                d_tl = jnp.exp(jnp.where(tri, wc[:hl] - wr[:, :hl], -1e30))
                d_bl = jnp.exp(wc[hl:] - wr[:, :hl])
                d_br = jnp.exp(jnp.where(tri, wc[hl:] - wr[:, hl:], -1e30))
                tops.append((inter[:hl, :hl] * d_tl).astype(bf16))
                bots.append((inter[hl:, :hl] * d_bl).astype(bf16))
                bots.append((inter[hl:, hl:] * d_br).astype(bf16))
            top = mm(
                jnp.concatenate(tops, axis=1), jnp.concatenate([xe[:hl], xo[:hl]], axis=0)
            )
            bot = mm(jnp.concatenate(bots, axis=1), jnp.concatenate([xe, xo], axis=0))
            mixed_o[:hl, ps] = top + base[:hl, ls]
            mixed_o[hl:, ps] = bot + base[hl:, ls]


def gate_kernel(places, info, cown, coth, normed, mixed, consts, *rest):
    count = len(places)
    pieces = rest[:count]
    gate_o, gno_o, sums_o, w, sem = rest[count:]
    c = pl.program_id(0)
    half = pl.num_programs(0) // 2
    width = gate_o.shape[1]
    gout = vector(consts, GOUT, width)

    @pl.when(c == 0)
    def _():
        load_rows(info, pieces, places, w, sem)

    mine = (c // half) == info[0]
    cot = jnp.where(mine, cown[...].astype(f32), coth[...].astype(f32)).astype(bf16)
    squares = jnp.zeros((R, LANES), f32)
    products = jnp.zeros((R, LANES), f32)
    for at in range(0, width, 2 * LANES):
        gate = mm(normed[...], w[:, at : at + 2 * LANES]).astype(bf16)
        gno = mm(cot, w[:, width + at : width + at + 2 * LANES])
        gate_o[:, at : at + 2 * LANES] = gate
        gno_o[:, at : at + 2 * LANES] = gno
        for ls in (slice(0, LANES), slice(LANES, 2 * LANES)):
            ps = slice(at + ls.start, at + ls.stop)
            gf = gate[:, ls].astype(f32)
            gated = mixed[:, ps] * (gf * sigmoid(gf))
            squares += gated * gated
            products += gno[:, ls] * gout[:, ps] * gated
    sums_o[0:8, :] = jnp.broadcast_to(jnp.sum(squares.T, axis=0, keepdims=True), (8, R))
    sums_o[8:16, :] = jnp.broadcast_to(jnp.sum(products.T, axis=0, keepdims=True), (8, R))


def gate_back_kernel(
    places, masks, info, cown, coth, normed, mixed, gate, gno, sown, soth, consts, *rest
):
    count = len(places)
    pieces = rest[:count]
    rest = rest[count:]
    parts = len(rest) - 14
    (sent_o, kept_o, ggate_o, gm_o, ggo_o, gain_o) = rest[:6]
    gw_o = rest[6 : 6 + parts]
    acc, acc_g, w, nout, gates, normed_t, cot_t, sem = rest[6 + parts :]
    c = pl.program_id(0)
    last = pl.num_programs(0) - 1
    half = pl.num_programs(0) // 2
    width = gm_o.shape[1]
    gout = vector(consts, GOUT, width)
    dim = acc.shape[0]

    @pl.when(c == 0)
    def _():
        load_rows(info, pieces, places, w, sem)
        for ref in (acc, acc_g, nout, gates, normed_t, cot_t):
            ref[...] = jnp.zeros_like(ref)

    now = c % 2
    before = 1 - now
    cot = jnp.where(c < half, coth[...].astype(f32), cown[...].astype(f32))
    inner_total = 2.0 * width
    s = sown[...] + soth[...]
    scale_r = lax.rsqrt(s[0:1] / inner_total + eps)
    coef_r = scale_r * scale_r * scale_r * (s[8:9] / inner_total)
    scale = jnp.broadcast_to(scale_r, (LANES, L)).T
    coef = jnp.broadcast_to(coef_r, (LANES, L)).T
    branch = jnp.zeros((L, dim), f32)
    for at in range(0, width, 2 * LANES):
        ws = slice(at, at + 2 * LANES)
        acc[:, ws] += mm(normed_t[before], gates[before, :, ws])
        for ps in (slice(at, at + LANES), slice(at + LANES, at + 2 * LANES)):
            gain = gout[:, ps]
            gf = gate[:, ps].astype(f32)
            sig = jax.nn.sigmoid(gf)
            silu = gf * sig
            mix = mixed[:, ps]
            gated = mix * silu
            grad = gno[:, ps].astype(f32)
            unit = gated * scale
            nout[now, :, ps] = (unit * gain).astype(bf16)
            acc_g[:, ps] += fold8(grad * unit)
            grad_gated = scale * (grad * gain) - gated * coef
            grad_gate = (grad_gated * mix * (sig + silu * (1.0 - sig))).astype(bf16)
            gates[now, :, ps] = grad_gate
            ggate_o[:, ps] = grad_gate
            gm_o[:, ps] = (grad_gated * silu).astype(bf16)
        acc[:, width + at : width + at + 2 * LANES] += mm(cot_t[before], nout[before, :, ws])
        branch += mm(nout[now, :, ws], w[:, width + at : width + at + 2 * LANES], NT)
    normed_t[now] = turn(normed[...])
    cot_t[now] = cot.T.astype(bf16)
    branch_b = branch.astype(bf16)

    @pl.when(c < half)
    def _():
        sent_o[...] = branch_b

    @pl.when(c >= half)
    def _():
        kept_o[...] = branch_b

    @pl.when(c == last)
    def _():
        acc[:, :width] += mm(normed_t[now], gates[now])
        acc[:, width:] += mm(cot_t[now], nout[now])
        store_rows(info, acc, gw_o, masks, acc.shape[0] // len(masks))
        ggo_o[...] = acc_g[...]
        gain_o[...] = row_products(acc, w, width)


def scan_back_kernel(
    masks, places, info, xbc, act_r, dsilu, step, within_r, mixed, sin_r, gm, normed, consts,
    tri_r, ggo, gain_z, *rest,
):
    count = len(places)
    pieces = rest[:count]
    gx_o, small_o = rest[count : count + 2]
    gw_o = rest[count + 2 : -10]
    dstate, dvbuf, acc_w, acc_c, acc_s, acc_h, w, expand, collect, sem = rest[-10:]
    i = pl.program_id(0)
    last = pl.num_programs(0) - 1
    width = expand.shape[1]
    heads = width // HEAD
    cols = width + 2 * NS
    conv, dsk = vector(consts, CONV, cols, 4), vector(consts, DSK, width)
    dtb, rate = vector(consts, DTB, LANES), vector(consts, RATE, LANES)

    @pl.when(i == 0)
    def _():
        expand[...] = expander(heads)
        collect[...] = collector(heads)
        load_rows(info, pieces, places, w, sem)
        dstate[...] = jnp.zeros_like(dstate)
        dvbuf[...] = jnp.zeros_like(dvbuf)
        acc_w[...] = jnp.zeros_like(acc_w)
        acc_c[...] = jnp.zeros_like(acc_c)
        acc_s[...] = jnp.zeros_like(acc_s)
        acc_h[...] = jnp.zeros_like(acc_h)

    def conv_strip(dpost, cs):
        dv = dpost * dsilu[:, cs].astype(f32)
        n = cs.start // LANES
        dvbuf[n, 0:L] = dv
        xin = xbc[:, cs].astype(f32)
        acc_c[4, :, cs] += fold8(dv)
        acc_c[3, :, cs] += fold8(dv * xin)
        dxin = conv[3:4, cs] * dv
        for k in range(3):
            ahead = dvbuf[n, 3 - k : 3 - k + L]
            acc_c[k, :, cs] += fold8(ahead * xin)
            dxin = dxin + conv[k : k + 1, cs] * ahead
        dvbuf[n, L : L + 8] = dv[0:8, :]
        gx_o[:, cs] = dxin.astype(bf16)

    b = act_r[:, width : width + NS]
    cc = act_r[:, width + NS :]
    ct = turn(cc)
    step_raw = step[...]
    within = within_r[...]
    steps = softplus(step_raw + dtb[...])
    p_steps, p_grown, p_tails = packs(steps, within)
    within_t = within.T
    inter_t = mm(b, cc, NT)
    hl = L // 2
    tri = iota((hl, hl), 0) <= iota((hl, hl), 1)
    left = iota((L, LANES), 1) < HEAD
    zero = jnp.zeros((L, LANES), bf16)
    dg_tl = jnp.zeros((hl, hl), f32)
    dg_tr = jnp.zeros((hl, hl), f32)
    dg_br = jnp.zeros((hl, hl), f32)
    dc = jnp.zeros((L, NS), f32)
    db = jnp.zeros((L, NS), f32)
    q_h = jnp.zeros((L, LANES), f32)
    s_h = jnp.zeros((L, LANES), f32)
    ends_h = jnp.zeros((8, LANES), f32)
    for quad in range(heads // 4):
        qs = slice(quad * 2 * LANES, (quad + 1) * 2 * LANES)
        steps_e = mm(p_steps, expand[:, qs])
        grown_e = mm(p_grown, expand[:, qs])
        tails_e = mm(p_tails, expand[:, qs])
        x = act_r[:, qs].astype(f32)
        scaled = x * steps_e
        scaled_b = scaled.astype(bf16)
        scaled_f = scaled_b.astype(f32)
        gmb = gm[:, qs]
        gmf = gmb.astype(f32)
        ds = dstate[:, qs]
        ds_b = ds.astype(bf16)
        sin = sin_r[0, :, qs]
        last_grown = grown_e[L - 1 : L, :]
        gm_grown = (gmf * grown_e).astype(bf16)
        dc += mm(gm_grown, sin.astype(bf16), NT)
        db += mm((scaled * tails_e).astype(bf16), ds_b, NT)
        dstate[:, qs] = ds * last_grown + mm(ct, gm_grown)
        state_part = mm(b, ds_b) * tails_e
        ends = jnp.sum(scaled_f * state_part, axis=0, keepdims=True) + last_grown * jnp.sum(
            sin * ds, axis=0, keepdims=True
        )
        collect_q = collect[qs, :]
        ends_h += head_sums(jnp.broadcast_to(ends, (8, 2 * LANES)), collect_q)
        his, los, prods = [], [], []
        for side in range(2):
            pair = 2 * quad + side
            ls = slice(side * LANES, (side + 1) * LANES)
            ps = slice(pair * LANES, (pair + 1) * LANES)
            x2 = scaled_b[:, ls]
            g2 = gmb[:, ls]
            ge = jnp.where(left, g2, zero)
            go = jnp.where(left, zero, g2)
            g_both = jnp.concatenate([ge, go], axis=0)
            g_bot = jnp.concatenate([ge[hl:], go[hl:]], axis=0)
            dm_top = mm(x2[:hl], g_both, NT)
            dm_bot = mm(x2[hl:], g_bot, NT)
            tops, bots = [], []
            for k, h in enumerate((2 * pair, 2 * pair + 1)):
                wc = within[:, h : h + 1]
                wr = within_t[h : h + 1, :]
                d_tl = jnp.exp(jnp.where(tri, wr[:, :hl] - wc[:hl], -1e30))
                d_tr = jnp.exp(wr[:, hl:] - wc[:hl])
                d_br = jnp.exp(jnp.where(tri, wr[:, hl:] - wc[hl:], -1e30))
                tops.append((inter_t[:hl, :hl] * d_tl).astype(bf16))
                tops.append((inter_t[:hl, hl:] * d_tr).astype(bf16))
                bots.append((inter_t[hl:, hl:] * d_br).astype(bf16))
                dg_tl += dm_top[:, k * L : k * L + hl] * d_tl
                dg_tr += dm_top[:, k * L + hl : (k + 1) * L] * d_tr
                dg_br += dm_bot[:, k * hl : (k + 1) * hl] * d_br
            top = mm(jnp.concatenate(tops, axis=1), g_both)
            bot = mm(jnp.concatenate(bots, axis=1), g_bot)
            dscaled = jnp.concatenate([top, bot], axis=0) + state_part[:, ls]
            xs = x[:, ls]
            gs = gmf[:, ls]
            y = mixed[:, ps] - dsk[:, ps] * xs
            q = gs * y - scaled_f[:, ls] * dscaled
            hi = q.astype(bf16)
            his.append(hi)
            los.append((q - hi.astype(f32)).astype(bf16))
            prods.append((dscaled * xs).astype(bf16))
            acc_s[:, ps] += fold8(gs * xs)
            conv_strip(dscaled * steps_e[:, ls] + dsk[:, ps] * gs, ps)
        q_h += mm(jnp.concatenate(his, axis=1), collect_q)
        q_h += mm(jnp.concatenate(los, axis=1), collect_q)
        s_h += mm(jnp.concatenate(prods, axis=1), collect_q)
    top = jnp.concatenate([dg_tl, dg_tr], axis=1)
    bot = jnp.concatenate([jnp.zeros((hl, hl), f32), dg_br], axis=1)
    dg = jnp.concatenate([top, bot], axis=0)
    dc += mm(dg.T.astype(bf16), b)
    db += mm(dg.astype(bf16), cc)
    conv_strip(db, slice(width, width + NS))
    conv_strip(dc, slice(width + NS, cols))
    d_rate = exact_mm(tri_r[...], q_h) + ends_h[0:1, :]
    d_steps = d_rate * rate[...] + s_h
    sig_s = sigmoid(step_raw + dtb[...])
    keep = iota((L, LANES), 1) < heads
    d_raw = jnp.where(keep, d_steps * sig_s, 0.0)
    acc_h[0:8, :] += fold8(d_raw)
    acc_h[8:16, :] += fold8(d_rate * steps * rate[...])
    gx_o[:, cols:] = d_raw.astype(bf16)
    acc_w[...] += mm(normed[...], gx_o[...], TN)

    @pl.when(i == last)
    def _():
        store_rows(info, acc_w, gw_o, masks, acc_w.shape[0] // len(masks))
        small_o[...] = jnp.zeros_like(small_o)
        for k in range(5):
            small_o[k : k + 1, :cols] = jnp.sum(acc_c[k], axis=0, keepdims=True)
        for k in range(2):
            head = acc_h[8 * k : 8 * k + 8, :]
            small_o[k : k + 1, cols:] = jnp.sum(head, axis=0, keepdims=True)
        small_o[5:6, :width] = jnp.sum(acc_s[...], axis=0, keepdims=True)
        small_o[6:7, :width] = jnp.sum(ggo[...], axis=0, keepdims=True)
        gains = row_products(acc_w, w, cols + LANES) + gain_z[...]
        small_o[7:8, : acc_w.shape[0]] = jnp.sum(gains.T, axis=0, keepdims=True)
        if len(gw_o) > 1:
            small = small_o[...]
            hi = small.astype(bf16).astype(f32)
            parts = jnp.concatenate([hi, small - hi], axis=0).astype(bf16)
            for out in gw_o:
                out[out.shape[0] - 16 :, :] = parts


def input_back_kernel(zplaces, xplaces, info, ggate, gx, *rest):
    zcount, xcount = len(zplaces), len(xplaces)
    zpieces = rest[:zcount]
    xpieces = rest[zcount : zcount + xcount]
    sent_o, kept_o, wz, wx, dnb, zsem, xsem = rest[zcount + xcount :]
    c = pl.program_id(0)
    half = pl.num_programs(0) // 2
    width = ggate.shape[1]

    @pl.when(c == 0)
    def _():
        load_rows(info, zpieces, zplaces, wz, zsem, pl.ds(0, width))
        load_rows(info, xpieces, xplaces, wx, xsem)

    dim = dnb.shape[1]
    for at in range(0, dim, 2 * LANES):
        ds = slice(at, at + 2 * LANES)
        dn = mm(ggate[...], wz[ds, :], NT) + mm(gx[...], wx[ds, :], NT)
        dnb[:, ds] = dn.astype(bf16)

    @pl.when(c < half)
    def _():
        sent_o[...] = dnb[...]

    @pl.when(c >= half)
    def _():
        kept_o[...] = dnb[...]


def finish_kernel(resid, cot, consts, dn_own, dn_oth, br_own, br_oth, out_o, gres_o):
    r = resid[...].astype(f32)
    inv = lax.rsqrt(jnp.mean(r * r, axis=1, keepdims=True) + eps)
    out_o[...] = (r + (br_own[...].astype(f32) + br_oth[...].astype(f32))).astype(bf16)
    gin = consts[GIN : GIN + 1, : r.shape[1]]
    u = (dn_own[...].astype(f32) + dn_oth[...].astype(f32)) * gin
    mean = jnp.mean(u * r, axis=1, keepdims=True)
    gres_o[...] = cot[...].astype(f32) + inv * u - r * (inv * inv * inv * mean)


def swap(v, bit, axis):
    size = lax.axis_size(axis)
    return lax.ppermute(v, axis, [(i, i ^ bit) for i in range(size)])


NEAR = (0, 1, 2, 3)
FAR = (0, 4, 8, 12)


def direct(size, rows):
    return size == 16 and rows % 16 == 0


def gather_whole(v, bits):
    size = lax.axis_size("dp")
    me = lax.axis_index("dp")
    held = v[None]
    for bit in sorted(bits):
        got = swap(held, bit, "dp")
        upper = (me & bit) != 0
        held = jnp.where(
            upper, jnp.concatenate([got, held]), jnp.concatenate([held, got])
        )
    return held.reshape(1, size * v.shape[0], v.shape[1])


def whole_pieces(v, bits):
    return [gather_whole(v, bits)], [(0, (None,))]


def gather_far(v):
    return [swap(v, far, "dp") for far in FAR[1:]]


def gather_near(held):
    pieces = [held] + [swap(held, near, "dp") for near in NEAR[1:]]
    return pieces, [(0, tuple(near ^ far for far in FAR)) for near in NEAR]


def scatter_shapes(size, rows, cols, extra=0):
    if not direct(size, rows):
        return [jax.ShapeDtypeStruct((size * rows, cols), bf16)], (None,)
    masks = tuple(near ^ far for near in NEAR for far in FAR)
    return [jax.ShapeDtypeStruct((4 * rows + extra, cols), bf16)] * 4, masks


def both_parts(v):
    return v[-16:-8] + v[-8:]


def scatter_near(pieces):
    return [pieces[0]] + [swap(p, near, "dp") for p, near in zip(pieces[1:], NEAR[1:])]


def scatter_far(total, rows, extra=None):
    blocks = [total[k * rows : (k + 1) * rows] for k in range(4)]
    if extra is not None:
        hi = extra.astype(bf16).astype(f32)
        parts = jnp.concatenate([hi, (extra - hi).astype(bf16).astype(f32)])
        blocks = [jnp.concatenate([block, parts]) for block in blocks]
    sent = [swap(block.astype(bf16), far, "dp") for block, far in zip(blocks[1:], FAR[1:])]
    return blocks[:1] + sent


def sum_pieces(pieces):
    return sum(p.astype(f32) for p in pieces)


def scatter_whole(g, bits):
    me = lax.axis_index("dp")
    rows = g.shape[0] // lax.axis_size("dp")
    left = sorted(bits, reverse=True)
    cur = g.reshape([2] * len(left) + [rows, g.shape[1]])
    for bit in sorted(bits):
        dim = left.index(bit)
        mine = ((me & bit) != 0).astype(jnp.int32)
        send = lax.dynamic_index_in_dim(cur, 1 - mine, dim, keepdims=False)
        keep = lax.dynamic_index_in_dim(cur, mine, dim, keepdims=False)
        got = swap(send.astype(bf16), bit, "dp")
        cur = keep.astype(f32) + got.astype(f32)
        left.pop(dim)
    return cur.astype(f32)


def full(shape):
    zeros = (0,) * len(shape)
    return pl.BlockSpec(shape, lambda c, *_: zeros)


def rows_spec(count, width, index=lambda c, info: c):
    return pl.BlockSpec((count, width), lambda c, info: (index(c, info), 0))


def call(kernel, name, vmem, grid, ins, outs, scratch, info, *args, **more):
    specs = [spec for spec, _ in outs]
    shapes = [item for _, item in outs]
    return pl.pallas_call(
        kernel,
        grid_spec=pltpu.PrefetchScalarGridSpec(
            num_scalar_prefetch=1, grid=(grid,), in_specs=ins, out_specs=specs,
            scratch_shapes=scratch,
        ),
        out_shape=shapes,
        compiler_params=pltpu.CompilerParams(
            dimension_semantics=("arbitrary",), vmem_limit_bytes=vmem * MIB
        ),
        name=name,
        **more,
    )(info, *args)


def local(
    resid, gain_in, w_z, w_x, w_bc, w_dt, conv_x, bias_x, conv_bc, bias_bc, dt_bias, a_log, d_skip,
    gain_out, w_out, cotangent,
):
    size = lax.axis_size("dp")
    place = lax.axis_index("tensor")
    heads = a_log.shape[0]
    width = heads * HEAD
    dim = resid.shape[1]
    rows = w_z.shape[0]
    cols = width + 2 * NS
    half_rows = resid.shape[0]
    tokens = 2 * half_rows
    assert tokens == SEQ_LEN
    chunks = tokens // L
    half = chunks // 2
    shape = jax.ShapeDtypeStruct
    bits = [1 << k for k in range(size.bit_length() - 1)]

    def lanes3(v):
        pad = [(0, 0)] * (v.ndim - 1)
        group = jnp.pad(v, pad + [(0, 16 - heads)])
        return jnp.pad(jnp.concatenate([group] * 3, axis=-1), pad + [(0, LANES - 48)])

    first = jnp.concatenate([w_x, w_bc, lanes3(w_dt)], axis=1)
    second = jnp.concatenate([w_z, w_out.T], axis=1)
    def row(v):
        return jnp.pad(v, ((0, 0), (0, cols - v.shape[1])))

    consts = jnp.concatenate(
        [
            jnp.concatenate([conv_x, conv_bc], axis=1),
            jnp.concatenate([bias_x, bias_bc])[None],
            row(gain_in[None]),
            row(gain_out[None]),
            row(jnp.repeat(d_skip, HEAD)[None]),
            row(lanes3(dt_bias[None])),
            row(lanes3(-jnp.exp(a_log)[None])),
            jnp.zeros((6, cols), f32),
        ]
    )
    if direct(size, rows):
        many = jnp.concatenate([first[:, :width], second], axis=1)
        few = first[:, width:]
        got_many = gather_far(many)
        got_few = [swap(few, near, "dp") for near in NEAR[1:]]
        many, got_many, few, got_few, resid_in, cot_in, consts = lax.optimization_barrier(
            (many, got_many, few, got_few, resid, cotangent, consts)
        )
        held = [many] + got_many
        few = jnp.stack([few] + got_few)
        wx = [jnp.concatenate([few] + [swap(few, far, "dp") for far in FAR[1:]])]
        wx_at = [(width, tuple(near ^ far for far in FAR for near in NEAR))]
        near_x, near_at = gather_near(jnp.stack([v[:, :width] for v in held]))
        wx, wx_at = near_x + wx, near_at + wx_at
        resid_oth = swap(resid_in, 1, "tensor")
        cot_oth = swap(cot_in, 1, "tensor")
        held, resid_oth, cot_oth, wx = lax.optimization_barrier((held, resid_oth, cot_oth, wx))
        wz, wz_at = gather_near(jnp.stack([v[:, width:] for v in held]))
    else:
        resid_oth = swap(resid, 1, "tensor")
        cot_oth = swap(cotangent, 1, "tensor")
        wx, wx_at = whole_pieces(first, bits)
        wz, wz_at = whole_pieces(second, bits)

    info = jnp.stack([place, lax.axis_index("dp")]).astype(jnp.int32)
    anywhere = pl.BlockSpec(memory_space=pltpu.HBM)

    def copies(at):
        return pltpu.SemaphoreType.DMA((sum(len(masks) for _, masks in at),))

    def tok(width, dtype):
        return shape((tokens, width), dtype)

    own_spec = rows_spec(L, dim, lambda c, info: jnp.clip(c - half * info[0], 0, half - 1))
    oth_spec = rows_spec(L, dim, lambda c, info: jnp.clip(c - half * (1 - info[0]), 0, half - 1))
    wide = rows_spec(L, width)
    normed, xbc, act, dsilu, step_raw, within, mixed, sin = call(
        functools.partial(forward_kernel, wx_at),
        "mix_forward",
        52,
        chunks,
        [
            own_spec, oth_spec, full((16, cols)), full((L, L)),
        ]
        + [anywhere] * len(wx),
        [
            (rows_spec(L, dim), tok(dim, bf16)),
            (rows_spec(L, cols), tok(cols, bf16)),
            (rows_spec(L, cols), tok(cols, bf16)),
            (rows_spec(L, cols), tok(cols, bf16)),
            (rows_spec(L, LANES), tok(LANES, f32)),
            (rows_spec(L, LANES), tok(LANES, f32)),
            (wide, tok(width, f32)),
            (
                pl.BlockSpec((1, NS, width), lambda c, info: (c, 0, 0)),
                shape((chunks, NS, width), f32),
            ),
        ],
        [
            pltpu.VMEM((NS, width), f32), pltpu.VMEM((cols // LANES, L + 8, LANES), f32),
            pltpu.VMEM((dim, cols + LANES), bf16), pltpu.VMEM((LANES, width), bf16),
            copies(wx_at),
        ],
        info, resid, resid_oth, consts, lower_tri(), *wx,
    )

    steps = tokens // R
    rhalf = steps // 2

    def block(width, index=lambda c, info: c):
        return rows_spec(R, width, index)

    own_r = block(dim, lambda c, info: jnp.clip(c - rhalf * info[0], 0, rhalf - 1))
    oth_r = block(dim, lambda c, info: jnp.clip(c - rhalf * (1 - info[0]), 0, rhalf - 1))
    sums_shape = shape((steps * 16, R), f32)
    gate, gno, sums = call(
        functools.partial(gate_kernel, wz_at),
        "gate_forward",
        52,
        steps,
        [own_r, oth_r, block(dim), block(width), full((16, cols))] + [anywhere] * len(wz),
        [
            (block(width), tok(width, bf16)), (block(width), tok(width, f32)),
            (rows_spec(16, R), sums_shape),
        ],
        [pltpu.VMEM((dim, 2 * width), bf16), copies(wz_at)],
        info, cotangent, cot_oth, normed, mixed, consts, *wz,
    )
    sums_oth = swap(sums, 1, "tensor")

    def turned(c, info):
        return jnp.where(c < rhalf, c + rhalf * (1 - info[0]), c - rhalf + rhalf * info[0])

    gw_shapes, masks = scatter_shapes(size, rows, 2 * width)

    def turned_l(c, info):
        return jnp.where(c < half, c + half * (1 - info[0]), c - half + half * info[0])

    twide = rows_spec(L, width, turned_l)
    lead = rows_spec(L, dim, lambda c, info: jnp.minimum(c, half - 1))
    trail = rows_spec(L, dim, lambda c, info: jnp.maximum(c - half, 0))
    sums_spec = pl.BlockSpec(
        (16, L), lambda c, info: (turned_l(c, info) // (R // L), turned_l(c, info) % (R // L))
    )
    half_shape = shape((half_rows, dim), bf16)
    branch_sent, branch_own, ggate, gm, g_gout, g_gin_z, *gw_zo = call(
        functools.partial(gate_back_kernel, wz_at, masks),
        "gate_backward",
        52,
        chunks,
        [
            trail, lead, rows_spec(L, dim, turned_l), twide, twide, twide,
            sums_spec, sums_spec, full((16, cols)),
        ]
        + [anywhere] * len(wz),
        [
            (lead, half_shape), (trail, half_shape), (twide, tok(width, bf16)),
            (twide, tok(width, bf16)), (full((8, width)), shape((8, width), f32)),
            (full((dim, LANES)), shape((dim, LANES), f32)),
        ]
        + [(full(item.shape), item) for item in gw_shapes],
        [
            pltpu.VMEM((dim, 2 * width), f32), pltpu.VMEM((8, width), f32),
            pltpu.VMEM((dim, 2 * width), bf16), pltpu.VMEM((2, L, width), bf16),
            pltpu.VMEM((2, L, width), bf16), pltpu.VMEM((2, dim, L), bf16),
            pltpu.VMEM((2, dim, L), bf16), copies(wz_at),
        ],
        info, cotangent, cot_oth, normed, mixed, gate, gno, sums, sums_oth, consts, *wz,
    )
    branch_oth = swap(branch_sent, 1, "tensor")
    sent_zo = scatter_near(gw_zo) if direct(size, rows) else gw_zo

    def back(c, info):
        return chunks - 1 - c

    rwide = rows_spec(L, width, back)
    rcols = rows_spec(L, cols, back)
    rlanes = rows_spec(L, LANES, back)
    gwx_shapes, masks = scatter_shapes(size, rows, cols + LANES, 16)
    gx, small, *gw_x = call(
        functools.partial(scan_back_kernel, masks, wx_at),
        "mix_backward",
        52,
        chunks,
        [
            rcols, rcols, rcols, rlanes, rlanes, rwide,
            pl.BlockSpec((1, NS, width), lambda c, info: (chunks - 1 - c, 0, 0)),
            rwide, rows_spec(L, dim, back), full((16, cols)),
            full((L, L)), full((8, width)), full((dim, LANES)),
        ]
        + [anywhere] * len(wx),
        [
            (rows_spec(L, cols + LANES, back), tok(cols + LANES, bf16)),
            (full((8, cols + LANES)), shape((8, cols + LANES), f32)),
        ]
        + [(full(item.shape), item) for item in gwx_shapes],
        [
            pltpu.VMEM((NS, width), f32), pltpu.VMEM((cols // LANES, L + 8, LANES), f32),
            pltpu.VMEM((dim, cols + LANES), f32), pltpu.VMEM((5, 8, cols), f32),
            pltpu.VMEM((8, width), f32), pltpu.VMEM((16, LANES), f32),
            pltpu.VMEM((dim, cols + LANES), bf16), pltpu.VMEM((LANES, width), bf16),
            pltpu.VMEM((width, LANES), bf16), copies(wx_at),
        ],
        info, xbc, act, dsilu, step_raw, within, mixed, sin, gm, normed, consts,
        upper_tri(), g_gout, g_gin_z, *wx,
    )

    sent_zo, branch_oth, gx, gw_x, small = lax.optimization_barrier(
        (sent_zo, branch_oth, gx, gw_x, small)
    )
    if direct(size, rows):
        sent_x = scatter_near(gw_x)
        far_zo = scatter_far(sum_pieces(sent_zo), rows)

    lead_r = block(dim, lambda c, info: jnp.minimum(c, rhalf - 1))
    trail_r = block(dim, lambda c, info: jnp.maximum(c - rhalf, 0))
    dn_sent, dn_own = call(
        functools.partial(input_back_kernel, wz_at, wx_at),
        "input_backward",
        32,
        steps,
        [block(width, turned), block(cols + LANES, turned)]
        + [anywhere] * (len(wz) + len(wx)),
        [(lead_r, half_shape), (trail_r, half_shape)],
        [
            pltpu.VMEM((dim, width), bf16), pltpu.VMEM((dim, cols + LANES), bf16),
            pltpu.VMEM((R, dim), bf16), copies(wz_at), copies(wx_at),
        ],
        info, ggate, gx, *wz, *wx,
    )
    if direct(size, rows):
        sent_x, dn_own, dn_sent = lax.optimization_barrier((sent_x, dn_own, dn_sent))
    dn_oth = swap(dn_sent, 1, "tensor")
    if direct(size, rows):
        total_x = sum_pieces(sent_x)
        far_x = scatter_far(total_x, rows, both_parts(total_x))
        far_zo, dn_oth, dn_own = lax.optimization_barrier((far_zo, dn_oth, dn_own))
        sum_zo = sum_pieces(far_zo)

    dspec = rows_spec(L, dim)
    block_out, grad_resid = call(
        lambda info, *refs: finish_kernel(*refs),
        "finish",
        12,
        half,
        [dspec, dspec, full((16, cols)), dspec, dspec, dspec, dspec],
        [(dspec, half_shape), (dspec, shape((half_rows, dim), f32))],
        [],
        info, resid, cotangent, consts, dn_own, dn_oth, branch_own, branch_oth,
    )

    if direct(size, rows):
        block_out, grad_resid, far_x, grad_w_z, grad_w_out = lax.optimization_barrier(
            (block_out, grad_resid, far_x, sum_zo[:, :width], sum_zo[:, width:].T)
        )
        sum_x = sum_pieces(far_x)
        small = both_parts(sum_x)
    else:
        sum_zo = scatter_whole(sent_zo[0], bits)
        grad_w_z, grad_w_out = sum_zo[:, :width], sum_zo[:, width:].T
        sum_x = scatter_whole(gw_x[0], bits)
        for bit in bits:
            small = small + swap(small, bit, "dp")
    grad_w_bc = sum_x[:rows, width:cols]
    pair = jnp.concatenate(
        [grad_w_bc.reshape(-1), small[:5, width:cols].reshape(-1), small[7, :dim]]
    )
    pair = pair + swap(pair, 1, "tensor")
    grad_w_bc, bc_g, gain_g = jnp.split(pair, [rows * 2 * NS, (rows + 5) * 2 * NS])
    bc_g = bc_g.reshape(5, 2 * NS)
    return (
        block_out, grad_resid, gain_g / gain_in, grad_w_z, sum_x[:rows, :width],
        grad_w_bc.reshape(rows, 2 * NS), sum_x[:rows, cols : cols + heads],
        small[:4, :width], small[4, :width], bc_g[:4], bc_g[4], small[0, cols : cols + heads],
        small[1, cols : cols + heads], small[5, :width].reshape(heads, HEAD).sum(axis=1),
        small[6, :width], grad_w_out,
    )


def solution(mesh):
    in_specs = (
        P(("dp", "tensor"), None),
        P(),
        P("dp", "tensor"),
        P("dp", "tensor"),
        P("dp", None),
        P("dp", "tensor"),
        P(None, "tensor"),
        P("tensor"),
        P(),
        P(),
        P("tensor"),
        P("tensor"),
        P("tensor"),
        P("tensor"),
        P("tensor", "dp"),
        P(("dp", "tensor"), None),
    )
    out_specs = (
        P(("dp", "tensor"), None),
        P(("dp", "tensor"), None),
        P(),
        P("dp", "tensor"),
        P("dp", "tensor"),
        P("dp", None),
        P("dp", "tensor"),
        P(None, "tensor"),
        P("tensor"),
        P(),
        P(),
        P("tensor"),
        P("tensor"),
        P("tensor"),
        P("tensor"),
        P("tensor", "dp"),
    )
    return jax.shard_map(local, mesh=mesh, in_specs=in_specs, out_specs=out_specs, check_vma=False)
```

```python
import functools

import jax
import jax.numpy as jnp
from jax import lax
from jax.experimental import pallas as pl
from jax.experimental.pallas import tpu as pltpu
from jax.sharding import PartitionSpec as P

NS = 128
L = 256
R = 512
SEQ_LEN = 2048
HEAD = 64
LANES = 128
MIB = 1024 * 1024

f32 = jnp.float32
bf16 = jnp.bfloat16
highest = lax.Precision.HIGHEST
eps = 1e-05

NN = (((1,), (0,)), ((), ()))
NT = (((1,), (1,)), ((), ()))
TN = (((0,), (0,)), ((), ()))


def mm(a, b, dims=NN, precision=None):
    return lax.dot_general(a, b, dims, precision=precision, preferred_element_type=f32)


def iota(shape, dim):
    return lax.broadcasted_iota(jnp.int32, shape, dim)


def lower_tri():
    return (iota((L, L), 0) >= iota((L, L), 1)).astype(bf16)


def upper_tri():
    return (iota((L, L), 0) <= iota((L, L), 1)).astype(bf16)


def expander(heads):
    rows = iota((LANES, heads * HEAD), 0)
    cols = iota((LANES, heads * HEAD), 1) // HEAD
    return ((rows % 16 == cols) & (rows < 48)).astype(bf16)


def collector(heads):
    rows = iota((heads * HEAD, LANES), 0) // HEAD
    cols = iota((heads * HEAD, LANES), 1)
    return ((cols % 16 == rows) & (cols < 48)).astype(bf16)


def split3(q):
    hi = q.astype(bf16).astype(f32)
    rest = q - hi
    mid = rest.astype(bf16).astype(f32)
    return hi, mid, rest - mid


def pack3(q):
    lane = iota(q.shape, 1)
    hi, mid, low = split3(q)
    return jnp.where(lane < 16, hi, jnp.where(lane < 32, mid, low)).astype(bf16)


def exact_mm(a, q):
    return sum(mm(a, part.astype(bf16)) for part in split3(q))


def turn(v):
    return v.astype(f32).T.astype(bf16)


def head_sums(q, col):
    hi = q.astype(bf16)
    lo = (q - hi.astype(f32)).astype(bf16)
    return mm(hi, col) + mm(lo, col)


def softplus(v):
    return jnp.maximum(v, 0.0) + jnp.log1p(jnp.exp(-jnp.abs(v)))


def sigmoid(v):
    return 0.5 * jnp.tanh(0.5 * v) + 0.5


def fold8(q):
    return jnp.sum(q.reshape(q.shape[0] // 8, 8, q.shape[1]), axis=0)


def packs(steps, within):
    tails = jnp.exp(within[L - 1 : L, :] - within)
    return pack3(steps), pack3(jnp.exp(within)), pack3(tails)


CONV, BIAS, GIN, GOUT, DSK, DTB, RATE = 0, 4, 5, 6, 7, 8, 9


class vector:
    def __init__(self, ref, at, width, count=1):
        self.ref, self.at, self.width, self.count = ref, at, width, count

    def __getitem__(self, key):
        rows, cols = (slice(None), slice(None)) if key is Ellipsis else key
        start, stop, _ = rows.indices(self.count)
        left, right, _ = cols.indices(self.width)
        return self.ref[self.at + start : self.at + stop, left:right]


def load_rows(info, pieces, places, w, sem, cols=slice(None)):
    copies = []
    for piece, (offset, masks) in zip(pieces, places):
        count = piece.shape[1]
        for k, mask in enumerate(masks):
            slot = 0 if mask is None else (info[1] ^ mask)
            rows = pl.ds(pl.multiple_of(slot * count, 16), count)
            if cols == slice(None):
                src = piece.at[k]
                dst = w.at[rows, pl.ds(offset, piece.shape[2])]
            else:
                src = piece.at[k, :, cols]
                dst = w.at[rows, :]
            copies.append(pltpu.make_async_copy(src, dst, sem.at[len(copies)]))
    for copy in copies:
        copy.start()
    for copy in copies:
        copy.wait()


def store_rows(info, acc, outs, masks, count):
    each = len(masks) // len(outs)
    for at, mask in enumerate(masks):
        slot = 0 if mask is None else (info[1] ^ mask)
        rows = pl.ds(pl.multiple_of(slot * count, 16), count)
        start = at % each * count
        outs[at // each][start : start + count, :] = acc[rows, :].astype(bf16)


def row_products(acc, w, width):
    total = jnp.zeros((acc.shape[0], LANES), f32)
    for at in range(0, width, LANES):
        ps = slice(at, at + LANES)
        total += acc[:, ps] * w[:, ps].astype(f32)
    return total


def forward_kernel(
    places, info, own, oth, consts, tri_r, *rest
):
    count = len(places)
    pieces = rest[:count]
    (
        normed_o, xbc_o, act_o, dsilu_o, step_o, within_o, mixed_o, sin_o, state, buf, w, expand,
        sem,
    ) = rest[count:]
    c = pl.program_id(0)
    half = pl.num_programs(0) // 2
    width = expand.shape[1]
    heads = width // HEAD
    cols = width + 2 * NS
    conv, bias = vector(consts, CONV, cols, 4), vector(consts, BIAS, cols)
    gin, dsk = vector(consts, GIN, own.shape[1]), vector(consts, DSK, width)
    dtb, rate = vector(consts, DTB, LANES), vector(consts, RATE, LANES)

    @pl.when(c == 0)
    def _():
        expand[...] = expander(heads)
        load_rows(info, pieces, places, w, sem)
        state[...] = jnp.zeros_like(state)
        buf[:, 0:8] = jnp.zeros((cols // LANES, 8, LANES), f32)

    mine = (c // half) == info[0]
    r = jnp.where(mine, own[...].astype(f32), oth[...].astype(f32))
    inv = lax.rsqrt(jnp.mean(r * r, axis=1, keepdims=True) + eps)
    normed = (r * inv * gin[...]).astype(bf16)
    normed_o[...] = normed
    step_raw = mm(normed, w[:, cols:])
    step_o[...] = step_raw
    steps = softplus(step_raw + dtb[...])
    within = exact_mm(tri_r[...], steps * rate[...])
    within_o[...] = within
    p_steps, p_grown, p_tails = packs(steps, within)
    within_t = within.T

    def conv_strip(cs):
        n = cs.start // LANES
        v = bias[:, cs] + conv[3:4, cs] * buf[n, 8 : 8 + L]
        for k in range(3):
            v = v + conv[k : k + 1, cs] * buf[n, 5 + k : 5 + k + L]
        buf[n, 0:8] = buf[n, L : L + 8]
        sig = sigmoid(v)
        value = v * sig
        dsilu_o[:, cs] = (sig + value * (1.0 - sig)).astype(bf16)
        act_o[:, cs] = value.astype(bf16)

    for at in range(cols - 2 * LANES, -1, -2 * LANES):
        ws = slice(at, at + 2 * LANES)
        xb = mm(normed, w[:, ws]).astype(bf16)
        xbc_o[:, ws] = xb
        xf = xb.astype(f32)
        buf[at // LANES, 8:] = xf[:, :LANES]
        buf[at // LANES + 1, 8:] = xf[:, LANES:]
        conv_strip(slice(at, at + LANES))
        conv_strip(slice(at + LANES, at + 2 * LANES))

    b = act_o[:, width : width + NS]
    cc = act_o[:, width + NS :]
    bt = turn(b)
    inter = mm(cc, b, NT)
    hl = L // 2
    tri = iota((hl, hl), 0) >= iota((hl, hl), 1)
    left = iota((L, LANES), 1) < HEAD
    zero = jnp.zeros((L, LANES), bf16)
    for quad in range(heads // 4):
        qs = slice(quad * 2 * LANES, (quad + 1) * 2 * LANES)
        steps_e = mm(p_steps, expand[:, qs])
        grown_e = mm(p_grown, expand[:, qs])
        tails_e = mm(p_tails, expand[:, qs])
        x = act_o[:, qs].astype(f32)
        scaled = x * steps_e
        scaled_b = scaled.astype(bf16)
        sin = state[:, qs]
        sin_o[0, :, qs] = sin
        base = mm(cc, sin.astype(bf16)) * grown_e + dsk[:, qs] * x
        state[:, qs] = sin * grown_e[L - 1 : L, :] + mm(bt, (scaled * tails_e).astype(bf16))
        for side in range(2):
            pair = 2 * quad + side
            ls = slice(side * LANES, (side + 1) * LANES)
            ps = slice(pair * LANES, (pair + 1) * LANES)
            x2 = scaled_b[:, ls]
            xe = jnp.where(left, x2, zero)
            xo = jnp.where(left, zero, x2)
            tops, bots = [], []
            for h in (2 * pair, 2 * pair + 1):
                wc = within[:, h : h + 1]
                wr = within_t[h : h + 1, :]
                d_tl = jnp.exp(jnp.where(tri, wc[:hl] - wr[:, :hl], -1e30))
                d_bl = jnp.exp(wc[hl:] - wr[:, :hl])
                d_br = jnp.exp(jnp.where(tri, wc[hl:] - wr[:, hl:], -1e30))
                tops.append((inter[:hl, :hl] * d_tl).astype(bf16))
                bots.append((inter[hl:, :hl] * d_bl).astype(bf16))
                bots.append((inter[hl:, hl:] * d_br).astype(bf16))
            top = mm(
                jnp.concatenate(tops, axis=1), jnp.concatenate([xe[:hl], xo[:hl]], axis=0)
            )
            bot = mm(jnp.concatenate(bots, axis=1), jnp.concatenate([xe, xo], axis=0))
            mixed_o[:hl, ps] = top + base[:hl, ls]
            mixed_o[hl:, ps] = bot + base[hl:, ls]


def gate_kernel(places, info, cown, coth, normed, mixed, consts, *rest):
    count = len(places)
    pieces = rest[:count]
    gate_o, gno_o, sums_o, w, sem = rest[count:]
    c = pl.program_id(0)
    half = pl.num_programs(0) // 2
    width = gate_o.shape[1]
    gout = vector(consts, GOUT, width)

    @pl.when(c == 0)
    def _():
        load_rows(info, pieces, places, w, sem)

    mine = (c // half) == info[0]
    cot = jnp.where(mine, cown[...].astype(f32), coth[...].astype(f32)).astype(bf16)
    squares = jnp.zeros((R, LANES), f32)
    products = jnp.zeros((R, LANES), f32)
    for at in range(0, width, 2 * LANES):
        gate = mm(normed[...], w[:, at : at + 2 * LANES]).astype(bf16)
        gno = mm(cot, w[:, width + at : width + at + 2 * LANES])
        gate_o[:, at : at + 2 * LANES] = gate
        gno_o[:, at : at + 2 * LANES] = gno
        for ls in (slice(0, LANES), slice(LANES, 2 * LANES)):
            ps = slice(at + ls.start, at + ls.stop)
            gf = gate[:, ls].astype(f32)
            gated = mixed[:, ps] * (gf * sigmoid(gf))
            squares += gated * gated
            products += gno[:, ls] * gout[:, ps] * gated
    sums_o[0:8, :] = jnp.broadcast_to(jnp.sum(squares.T, axis=0, keepdims=True), (8, R))
    sums_o[8:16, :] = jnp.broadcast_to(jnp.sum(products.T, axis=0, keepdims=True), (8, R))


def gate_back_kernel(
    places, masks, info, cown, coth, normed, mixed, gate, gno, sown, soth, consts, *rest
):
    count = len(places)
    pieces = rest[:count]
    rest = rest[count:]
    parts = len(rest) - 14
    (sent_o, kept_o, ggate_o, gm_o, ggo_o, gain_o) = rest[:6]
    gw_o = rest[6 : 6 + parts]
    acc, acc_g, w, nout, gates, normed_t, cot_t, sem = rest[6 + parts :]
    c = pl.program_id(0)
    last = pl.num_programs(0) - 1
    half = pl.num_programs(0) // 2
    width = gm_o.shape[1]
    gout = vector(consts, GOUT, width)
    dim = acc.shape[0]

    @pl.when(c == 0)
    def _():
        load_rows(info, pieces, places, w, sem)
        for ref in (acc, acc_g, nout, gates, normed_t, cot_t):
            ref[...] = jnp.zeros_like(ref)

    now = c % 2
    before = 1 - now
    cot = jnp.where(c < half, coth[...].astype(f32), cown[...].astype(f32))
    inner_total = 2.0 * width
    s = sown[...] + soth[...]
    scale_r = lax.rsqrt(s[0:1] / inner_total + eps)
    coef_r = scale_r * scale_r * scale_r * (s[8:9] / inner_total)
    scale = jnp.broadcast_to(scale_r, (LANES, L)).T
    coef = jnp.broadcast_to(coef_r, (LANES, L)).T
    branch = jnp.zeros((L, dim), f32)
    for at in range(0, width, 2 * LANES):
        ws = slice(at, at + 2 * LANES)
        acc[:, ws] += mm(normed_t[before], gates[before, :, ws])
        for ps in (slice(at, at + LANES), slice(at + LANES, at + 2 * LANES)):
            gain = gout[:, ps]
            gf = gate[:, ps].astype(f32)
            sig = jax.nn.sigmoid(gf)
            silu = gf * sig
            mix = mixed[:, ps]
            gated = mix * silu
            grad = gno[:, ps].astype(f32)
            unit = gated * scale
            nout[now, :, ps] = (unit * gain).astype(bf16)
            acc_g[:, ps] += fold8(grad * unit)
            grad_gated = scale * (grad * gain) - gated * coef
            grad_gate = (grad_gated * mix * (sig + silu * (1.0 - sig))).astype(bf16)
            gates[now, :, ps] = grad_gate
            ggate_o[:, ps] = grad_gate
            gm_o[:, ps] = (grad_gated * silu).astype(bf16)
        acc[:, width + at : width + at + 2 * LANES] += mm(cot_t[before], nout[before, :, ws])
        branch += mm(nout[now, :, ws], w[:, width + at : width + at + 2 * LANES], NT)
    normed_t[now] = turn(normed[...])
    cot_t[now] = cot.T.astype(bf16)
    branch_b = branch.astype(bf16)

    @pl.when(c < half)
    def _():
        sent_o[...] = branch_b

    @pl.when(c >= half)
    def _():
        kept_o[...] = branch_b

    @pl.when(c == last)
    def _():
        acc[:, :width] += mm(normed_t[now], gates[now])
        acc[:, width:] += mm(cot_t[now], nout[now])
        store_rows(info, acc, gw_o, masks, acc.shape[0] // len(masks))
        ggo_o[...] = acc_g[...]
        gain_o[...] = row_products(acc, w, width)


def scan_back_kernel(
    masks, places, info, xbc, act_r, dsilu, step, within_r, mixed, sin_r, gm, normed, consts,
    tri_r, ggo, gain_z, *rest,
):
    count = len(places)
    pieces = rest[:count]
    gx_o, small_o = rest[count : count + 2]
    gw_o = rest[count + 2 : -10]
    dstate, dvbuf, acc_w, acc_c, acc_s, acc_h, w, expand, collect, sem = rest[-10:]
    i = pl.program_id(0)
    last = pl.num_programs(0) - 1
    width = expand.shape[1]
    heads = width // HEAD
    cols = width + 2 * NS
    conv, dsk = vector(consts, CONV, cols, 4), vector(consts, DSK, width)
    dtb, rate = vector(consts, DTB, LANES), vector(consts, RATE, LANES)

    @pl.when(i == 0)
    def _():
        expand[...] = expander(heads)
        collect[...] = collector(heads)
        load_rows(info, pieces, places, w, sem)
        dstate[...] = jnp.zeros_like(dstate)
        dvbuf[...] = jnp.zeros_like(dvbuf)
        acc_w[...] = jnp.zeros_like(acc_w)
        acc_c[...] = jnp.zeros_like(acc_c)
        acc_s[...] = jnp.zeros_like(acc_s)
        acc_h[...] = jnp.zeros_like(acc_h)

    def conv_strip(dpost, cs):
        dv = dpost * dsilu[:, cs].astype(f32)
        n = cs.start // LANES
        dvbuf[n, 0:L] = dv
        xin = xbc[:, cs].astype(f32)
        acc_c[4, :, cs] += fold8(dv)
        acc_c[3, :, cs] += fold8(dv * xin)
        dxin = conv[3:4, cs] * dv
        for k in range(3):
            ahead = dvbuf[n, 3 - k : 3 - k + L]
            acc_c[k, :, cs] += fold8(ahead * xin)
            dxin = dxin + conv[k : k + 1, cs] * ahead
        dvbuf[n, L : L + 8] = dv[0:8, :]
        gx_o[:, cs] = dxin.astype(bf16)

    b = act_r[:, width : width + NS]
    cc = act_r[:, width + NS :]
    ct = turn(cc)
    step_raw = step[...]
    within = within_r[...]
    steps = softplus(step_raw + dtb[...])
    p_steps, p_grown, p_tails = packs(steps, within)
    within_t = within.T
    inter_t = mm(b, cc, NT)
    hl = L // 2
    tri = iota((hl, hl), 0) <= iota((hl, hl), 1)
    left = iota((L, LANES), 1) < HEAD
    zero = jnp.zeros((L, LANES), bf16)
    dg_tl = jnp.zeros((hl, hl), f32)
    dg_tr = jnp.zeros((hl, hl), f32)
    dg_br = jnp.zeros((hl, hl), f32)
    dc = jnp.zeros((L, NS), f32)
    db = jnp.zeros((L, NS), f32)
    q_h = jnp.zeros((L, LANES), f32)
    s_h = jnp.zeros((L, LANES), f32)
    ends_h = jnp.zeros((8, LANES), f32)
    for quad in range(heads // 4):
        qs = slice(quad * 2 * LANES, (quad + 1) * 2 * LANES)
        steps_e = mm(p_steps, expand[:, qs])
        grown_e = mm(p_grown, expand[:, qs])
        tails_e = mm(p_tails, expand[:, qs])
        x = act_r[:, qs].astype(f32)
        scaled = x * steps_e
        scaled_b = scaled.astype(bf16)
        scaled_f = scaled_b.astype(f32)
        gmb = gm[:, qs]
        gmf = gmb.astype(f32)
        ds = dstate[:, qs]
        ds_b = ds.astype(bf16)
        sin = sin_r[0, :, qs]
        last_grown = grown_e[L - 1 : L, :]
        gm_grown = (gmf * grown_e).astype(bf16)
        dc += mm(gm_grown, sin.astype(bf16), NT)
        db += mm((scaled * tails_e).astype(bf16), ds_b, NT)
        dstate[:, qs] = ds * last_grown + mm(ct, gm_grown)
        state_part = mm(b, ds_b) * tails_e
        ends = jnp.sum(scaled_f * state_part, axis=0, keepdims=True) + last_grown * jnp.sum(
            sin * ds, axis=0, keepdims=True
        )
        collect_q = collect[qs, :]
        ends_h += head_sums(jnp.broadcast_to(ends, (8, 2 * LANES)), collect_q)
        his, los, prods = [], [], []
        for side in range(2):
            pair = 2 * quad + side
            ls = slice(side * LANES, (side + 1) * LANES)
            ps = slice(pair * LANES, (pair + 1) * LANES)
            x2 = scaled_b[:, ls]
            g2 = gmb[:, ls]
            ge = jnp.where(left, g2, zero)
            go = jnp.where(left, zero, g2)
            g_both = jnp.concatenate([ge, go], axis=0)
            g_bot = jnp.concatenate([ge[hl:], go[hl:]], axis=0)
            dm_top = mm(x2[:hl], g_both, NT)
            dm_bot = mm(x2[hl:], g_bot, NT)
            tops, bots = [], []
            for k, h in enumerate((2 * pair, 2 * pair + 1)):
                wc = within[:, h : h + 1]
                wr = within_t[h : h + 1, :]
                d_tl = jnp.exp(jnp.where(tri, wr[:, :hl] - wc[:hl], -1e30))
                d_tr = jnp.exp(wr[:, hl:] - wc[:hl])
                d_br = jnp.exp(jnp.where(tri, wr[:, hl:] - wc[hl:], -1e30))
                tops.append((inter_t[:hl, :hl] * d_tl).astype(bf16))
                tops.append((inter_t[:hl, hl:] * d_tr).astype(bf16))
                bots.append((inter_t[hl:, hl:] * d_br).astype(bf16))
                dg_tl += dm_top[:, k * L : k * L + hl] * d_tl
                dg_tr += dm_top[:, k * L + hl : (k + 1) * L] * d_tr
                dg_br += dm_bot[:, k * hl : (k + 1) * hl] * d_br
            top = mm(jnp.concatenate(tops, axis=1), g_both)
            bot = mm(jnp.concatenate(bots, axis=1), g_bot)
            dscaled = jnp.concatenate([top, bot], axis=0) + state_part[:, ls]
            xs = x[:, ls]
            gs = gmf[:, ls]
            y = mixed[:, ps] - dsk[:, ps] * xs
            q = gs * y - scaled_f[:, ls] * dscaled
            hi = q.astype(bf16)
            his.append(hi)
            los.append((q - hi.astype(f32)).astype(bf16))
            prods.append((dscaled * xs).astype(bf16))
            acc_s[:, ps] += fold8(gs * xs)
            conv_strip(dscaled * steps_e[:, ls] + dsk[:, ps] * gs, ps)
        q_h += mm(jnp.concatenate(his, axis=1), collect_q)
        q_h += mm(jnp.concatenate(los, axis=1), collect_q)
        s_h += mm(jnp.concatenate(prods, axis=1), collect_q)
    top = jnp.concatenate([dg_tl, dg_tr], axis=1)
    bot = jnp.concatenate([jnp.zeros((hl, hl), f32), dg_br], axis=1)
    dg = jnp.concatenate([top, bot], axis=0)
    dc += mm(dg.T.astype(bf16), b)
    db += mm(dg.astype(bf16), cc)
    conv_strip(db, slice(width, width + NS))
    conv_strip(dc, slice(width + NS, cols))
    d_rate = exact_mm(tri_r[...], q_h) + ends_h[0:1, :]
    d_steps = d_rate * rate[...] + s_h
    sig_s = sigmoid(step_raw + dtb[...])
    keep = iota((L, LANES), 1) < heads
    d_raw = jnp.where(keep, d_steps * sig_s, 0.0)
    acc_h[0:8, :] += fold8(d_raw)
    acc_h[8:16, :] += fold8(d_rate * steps * rate[...])
    gx_o[:, cols:] = d_raw.astype(bf16)
    acc_w[...] += mm(normed[...], gx_o[...], TN)

    @pl.when(i == last)
    def _():
        store_rows(info, acc_w, gw_o, masks, acc_w.shape[0] // len(masks))
        small_o[...] = jnp.zeros_like(small_o)
        for k in range(5):
            small_o[k : k + 1, :cols] = jnp.sum(acc_c[k], axis=0, keepdims=True)
        for k in range(2):
            head = acc_h[8 * k : 8 * k + 8, :]
            small_o[k : k + 1, cols:] = jnp.sum(head, axis=0, keepdims=True)
        small_o[5:6, :width] = jnp.sum(acc_s[...], axis=0, keepdims=True)
        small_o[6:7, :width] = jnp.sum(ggo[...], axis=0, keepdims=True)
        gains = row_products(acc_w, w, cols + LANES) + gain_z[...]
        small_o[7:8, : acc_w.shape[0]] = jnp.sum(gains.T, axis=0, keepdims=True)
        if len(gw_o) > 1:
            small = small_o[...]
            hi = small.astype(bf16).astype(f32)
            parts = jnp.concatenate([hi, small - hi], axis=0).astype(bf16)
            for out in gw_o:
                out[out.shape[0] - 16 :, :] = parts


def input_back_kernel(zplaces, xplaces, info, ggate, gx, *rest):
    zcount, xcount = len(zplaces), len(xplaces)
    zpieces = rest[:zcount]
    xpieces = rest[zcount : zcount + xcount]
    sent_o, kept_o, wz, wx, dnb, zsem, xsem = rest[zcount + xcount :]
    c = pl.program_id(0)
    half = pl.num_programs(0) // 2
    width = ggate.shape[1]

    @pl.when(c == 0)
    def _():
        load_rows(info, zpieces, zplaces, wz, zsem, pl.ds(0, width))
        load_rows(info, xpieces, xplaces, wx, xsem)

    dim = dnb.shape[1]
    for at in range(0, dim, 2 * LANES):
        ds = slice(at, at + 2 * LANES)
        dn = mm(ggate[...], wz[ds, :], NT) + mm(gx[...], wx[ds, :], NT)
        dnb[:, ds] = dn.astype(bf16)

    @pl.when(c < half)
    def _():
        sent_o[...] = dnb[...]

    @pl.when(c >= half)
    def _():
        kept_o[...] = dnb[...]


def finish_kernel(resid, cot, consts, dn_own, dn_oth, br_own, br_oth, out_o, gres_o):
    r = resid[...].astype(f32)
    inv = lax.rsqrt(jnp.mean(r * r, axis=1, keepdims=True) + eps)
    out_o[...] = (r + (br_own[...].astype(f32) + br_oth[...].astype(f32))).astype(bf16)
    gin = consts[GIN : GIN + 1, : r.shape[1]]
    u = (dn_own[...].astype(f32) + dn_oth[...].astype(f32)) * gin
    mean = jnp.mean(u * r, axis=1, keepdims=True)
    gres_o[...] = cot[...].astype(f32) + inv * u - r * (inv * inv * inv * mean)


def swap(v, bit, axis):
    size = lax.axis_size(axis)
    return lax.ppermute(v, axis, [(i, i ^ bit) for i in range(size)])


NEAR = (0, 1, 2, 3)
FAR = (0, 4, 8, 12)


def direct(size, rows):
    return size == 16 and rows % 16 == 0


def gather_whole(v, bits):
    size = lax.axis_size("dp")
    me = lax.axis_index("dp")
    held = v[None]
    for bit in sorted(bits):
        got = swap(held, bit, "dp")
        upper = (me & bit) != 0
        held = jnp.where(
            upper, jnp.concatenate([got, held]), jnp.concatenate([held, got])
        )
    return held.reshape(1, size * v.shape[0], v.shape[1])


def whole_pieces(v, bits):
    return [gather_whole(v, bits)], [(0, (None,))]


def gather_far(v):
    return [swap(v, far, "dp") for far in FAR[1:]]


def gather_near(held):
    pieces = [held] + [swap(held, near, "dp") for near in NEAR[1:]]
    return pieces, [(0, tuple(near ^ far for far in FAR)) for near in NEAR]


def scatter_shapes(size, rows, cols, extra=0):
    if not direct(size, rows):
        return [jax.ShapeDtypeStruct((size * rows, cols), bf16)], (None,)
    masks = tuple(near ^ far for near in NEAR for far in FAR)
    return [jax.ShapeDtypeStruct((4 * rows + extra, cols), bf16)] * 4, masks


def both_parts(v):
    return v[-16:-8] + v[-8:]


def scatter_near(pieces):
    return [pieces[0]] + [swap(p, near, "dp") for p, near in zip(pieces[1:], NEAR[1:])]


def scatter_far(total, rows, extra=None):
    blocks = [total[k * rows : (k + 1) * rows] for k in range(4)]
    if extra is not None:
        rounded = extra.astype(bf16).astype(f32)
        blocks = [jnp.concatenate([block, rounded]) for block in blocks]
    sent = [swap(blocks[k].astype(bf16), FAR[k], "dp") for k in (3, 2, 1)]
    return blocks[:1] + sent


def sum_pieces(pieces):
    a, b, c, d = (p.astype(f32) for p in pieces)
    return (a + b) + (c + d)


def scatter_whole(g, bits):
    me = lax.axis_index("dp")
    rows = g.shape[0] // lax.axis_size("dp")
    left = sorted(bits, reverse=True)
    cur = g.reshape([2] * len(left) + [rows, g.shape[1]])
    for bit in sorted(bits):
        dim = left.index(bit)
        mine = ((me & bit) != 0).astype(jnp.int32)
        send = lax.dynamic_index_in_dim(cur, 1 - mine, dim, keepdims=False)
        keep = lax.dynamic_index_in_dim(cur, mine, dim, keepdims=False)
        got = swap(send.astype(bf16), bit, "dp")
        cur = keep.astype(f32) + got.astype(f32)
        left.pop(dim)
    return cur.astype(f32)


def full(shape):
    zeros = (0,) * len(shape)
    return pl.BlockSpec(shape, lambda c, *_: zeros)


def rows_spec(count, width, index=lambda c, info: c):
    return pl.BlockSpec((count, width), lambda c, info: (index(c, info), 0))


def call(kernel, name, vmem, grid, ins, outs, scratch, info, *args, **more):
    specs = [spec for spec, _ in outs]
    shapes = [item for _, item in outs]
    return pl.pallas_call(
        kernel,
        grid_spec=pltpu.PrefetchScalarGridSpec(
            num_scalar_prefetch=1, grid=(grid,), in_specs=ins, out_specs=specs,
            scratch_shapes=scratch,
        ),
        out_shape=shapes,
        compiler_params=pltpu.CompilerParams(
            dimension_semantics=("arbitrary",), vmem_limit_bytes=vmem * MIB
        ),
        name=name,
        **more,
    )(info, *args)


def local(
    resid, gain_in, w_z, w_x, w_bc, w_dt, conv_x, bias_x, conv_bc, bias_bc, dt_bias, a_log, d_skip,
    gain_out, w_out, cotangent,
):
    size = lax.axis_size("dp")
    place = lax.axis_index("tensor")
    heads = a_log.shape[0]
    width = heads * HEAD
    dim = resid.shape[1]
    rows = w_z.shape[0]
    cols = width + 2 * NS
    half_rows = resid.shape[0]
    tokens = 2 * half_rows
    assert tokens == SEQ_LEN
    chunks = tokens // L
    half = chunks // 2
    shape = jax.ShapeDtypeStruct
    bits = [1 << k for k in range(size.bit_length() - 1)]

    def lanes3(v):
        pad = [(0, 0)] * (v.ndim - 1)
        group = jnp.pad(v, pad + [(0, 16 - heads)])
        return jnp.pad(jnp.concatenate([group] * 3, axis=-1), pad + [(0, LANES - 48)])

    first = jnp.concatenate([w_x, w_bc, lanes3(w_dt)], axis=1)
    second = jnp.concatenate([w_z, w_out.T], axis=1)
    def row(v):
        return jnp.pad(v, ((0, 0), (0, cols - v.shape[1])))

    consts = jnp.concatenate(
        [
            jnp.concatenate([conv_x, conv_bc], axis=1),
            jnp.concatenate([bias_x, bias_bc])[None],
            row(gain_in[None]),
            row(gain_out[None]),
            row(jnp.repeat(d_skip, HEAD)[None]),
            row(lanes3(dt_bias[None])),
            row(lanes3(-jnp.exp(a_log)[None])),
            jnp.zeros((6, cols), f32),
        ]
    )
    if direct(size, rows):
        many = jnp.concatenate([first[:, :width], second], axis=1)
        few = first[:, width:]
        got_many = gather_far(many)
        got_few = [swap(few, near, "dp") for near in NEAR[1:]]
        many, got_many, few, got_few, resid_in, cot_in, consts = lax.optimization_barrier(
            (many, got_many, few, got_few, resid, cotangent, consts)
        )
        held = [many] + got_many
        few = jnp.stack([few] + got_few)
        wx = [jnp.concatenate([few] + [swap(few, far, "dp") for far in FAR[1:]])]
        wx_at = [(width, tuple(near ^ far for far in FAR for near in NEAR))]
        near_x, near_at = gather_near(jnp.stack([v[:, :width] for v in held]))
        wx, wx_at = near_x + wx, near_at + wx_at
        resid_oth = swap(resid_in, 1, "tensor")
        cot_oth = swap(cot_in, 1, "tensor")
        held, resid_oth, cot_oth, wx = lax.optimization_barrier((held, resid_oth, cot_oth, wx))
        wz, wz_at = gather_near(jnp.stack([v[:, width:] for v in held]))
    else:
        resid_oth = swap(resid, 1, "tensor")
        cot_oth = swap(cotangent, 1, "tensor")
        wx, wx_at = whole_pieces(first, bits)
        wz, wz_at = whole_pieces(second, bits)

    info = jnp.stack([place, lax.axis_index("dp")]).astype(jnp.int32)
    anywhere = pl.BlockSpec(memory_space=pltpu.HBM)

    def copies(at):
        return pltpu.SemaphoreType.DMA((sum(len(masks) for _, masks in at),))

    def tok(width, dtype):
        return shape((tokens, width), dtype)

    own_spec = rows_spec(L, dim, lambda c, info: jnp.clip(c - half * info[0], 0, half - 1))
    oth_spec = rows_spec(L, dim, lambda c, info: jnp.clip(c - half * (1 - info[0]), 0, half - 1))
    wide = rows_spec(L, width)
    normed, xbc, act, dsilu, step_raw, within, mixed, sin = call(
        functools.partial(forward_kernel, wx_at),
        "mix_forward",
        52,
        chunks,
        [
            own_spec, oth_spec, full((16, cols)), full((L, L)),
        ]
        + [anywhere] * len(wx),
        [
            (rows_spec(L, dim), tok(dim, bf16)),
            (rows_spec(L, cols), tok(cols, bf16)),
            (rows_spec(L, cols), tok(cols, bf16)),
            (rows_spec(L, cols), tok(cols, bf16)),
            (rows_spec(L, LANES), tok(LANES, f32)),
            (rows_spec(L, LANES), tok(LANES, f32)),
            (wide, tok(width, f32)),
            (
                pl.BlockSpec((1, NS, width), lambda c, info: (c, 0, 0)),
                shape((chunks, NS, width), f32),
            ),
        ],
        [
            pltpu.VMEM((NS, width), f32), pltpu.VMEM((cols // LANES, L + 8, LANES), f32),
            pltpu.VMEM((dim, cols + LANES), bf16), pltpu.VMEM((LANES, width), bf16),
            copies(wx_at),
        ],
        info, resid, resid_oth, consts, lower_tri(), *wx,
    )

    steps = tokens // R
    rhalf = steps // 2

    def block(width, index=lambda c, info: c):
        return rows_spec(R, width, index)

    own_r = block(dim, lambda c, info: jnp.clip(c - rhalf * info[0], 0, rhalf - 1))
    oth_r = block(dim, lambda c, info: jnp.clip(c - rhalf * (1 - info[0]), 0, rhalf - 1))
    sums_shape = shape((steps * 16, R), f32)
    gate, gno, sums = call(
        functools.partial(gate_kernel, wz_at),
        "gate_forward",
        52,
        steps,
        [own_r, oth_r, block(dim), block(width), full((16, cols))] + [anywhere] * len(wz),
        [
            (block(width), tok(width, bf16)), (block(width), tok(width, f32)),
            (rows_spec(16, R), sums_shape),
        ],
        [pltpu.VMEM((dim, 2 * width), bf16), copies(wz_at)],
        info, cotangent, cot_oth, normed, mixed, consts, *wz,
    )
    sums_oth = swap(sums, 1, "tensor")

    def turned(c, info):
        return jnp.where(c < rhalf, c + rhalf * (1 - info[0]), c - rhalf + rhalf * info[0])

    gw_shapes, masks = scatter_shapes(size, rows, 2 * width)

    def turned_l(c, info):
        return jnp.where(c < half, c + half * (1 - info[0]), c - half + half * info[0])

    twide = rows_spec(L, width, turned_l)
    lead = rows_spec(L, dim, lambda c, info: jnp.minimum(c, half - 1))
    trail = rows_spec(L, dim, lambda c, info: jnp.maximum(c - half, 0))
    sums_spec = pl.BlockSpec(
        (16, L), lambda c, info: (turned_l(c, info) // (R // L), turned_l(c, info) % (R // L))
    )
    half_shape = shape((half_rows, dim), bf16)
    branch_sent, branch_own, ggate, gm, g_gout, g_gin_z, *gw_zo = call(
        functools.partial(gate_back_kernel, wz_at, masks),
        "gate_backward",
        52,
        chunks,
        [
            trail, lead, rows_spec(L, dim, turned_l), twide, twide, twide,
            sums_spec, sums_spec, full((16, cols)),
        ]
        + [anywhere] * len(wz),
        [
            (lead, half_shape), (trail, half_shape), (twide, tok(width, bf16)),
            (twide, tok(width, bf16)), (full((8, width)), shape((8, width), f32)),
            (full((dim, LANES)), shape((dim, LANES), f32)),
        ]
        + [(full(item.shape), item) for item in gw_shapes],
        [
            pltpu.VMEM((dim, 2 * width), f32), pltpu.VMEM((8, width), f32),
            pltpu.VMEM((dim, 2 * width), bf16), pltpu.VMEM((2, L, width), bf16),
            pltpu.VMEM((2, L, width), bf16), pltpu.VMEM((2, dim, L), bf16),
            pltpu.VMEM((2, dim, L), bf16), copies(wz_at),
        ],
        info, cotangent, cot_oth, normed, mixed, gate, gno, sums, sums_oth, consts, *wz,
    )
    branch_oth = swap(branch_sent, 1, "tensor")
    sent_zo = scatter_near(gw_zo) if direct(size, rows) else gw_zo

    def back(c, info):
        return chunks - 1 - c

    rwide = rows_spec(L, width, back)
    rcols = rows_spec(L, cols, back)
    rlanes = rows_spec(L, LANES, back)
    gwx_shapes, masks = scatter_shapes(size, rows, cols + LANES, 16)
    gx, small, *gw_x = call(
        functools.partial(scan_back_kernel, masks, wx_at),
        "mix_backward",
        52,
        chunks,
        [
            rcols, rcols, rcols, rlanes, rlanes, rwide,
            pl.BlockSpec((1, NS, width), lambda c, info: (chunks - 1 - c, 0, 0)),
            rwide, rows_spec(L, dim, back), full((16, cols)),
            full((L, L)), full((8, width)), full((dim, LANES)),
        ]
        + [anywhere] * len(wx),
        [
            (rows_spec(L, cols + LANES, back), tok(cols + LANES, bf16)),
            (full((8, cols + LANES)), shape((8, cols + LANES), f32)),
        ]
        + [(full(item.shape), item) for item in gwx_shapes],
        [
            pltpu.VMEM((NS, width), f32), pltpu.VMEM((cols // LANES, L + 8, LANES), f32),
            pltpu.VMEM((dim, cols + LANES), f32), pltpu.VMEM((5, 8, cols), f32),
            pltpu.VMEM((8, width), f32), pltpu.VMEM((16, LANES), f32),
            pltpu.VMEM((dim, cols + LANES), bf16), pltpu.VMEM((LANES, width), bf16),
            pltpu.VMEM((width, LANES), bf16), copies(wx_at),
        ],
        info, xbc, act, dsilu, step_raw, within, mixed, sin, gm, normed, consts,
        upper_tri(), g_gout, g_gin_z, *wx,
    )

    sent_zo, branch_oth, gx, gw_x, small = lax.optimization_barrier(
        (sent_zo, branch_oth, gx, gw_x, small)
    )
    if direct(size, rows):
        sent_x = scatter_near(gw_x)
        far_zo = scatter_far(sum_pieces(sent_zo), rows)

    lead_r = block(dim, lambda c, info: jnp.minimum(c, rhalf - 1))
    trail_r = block(dim, lambda c, info: jnp.maximum(c - rhalf, 0))
    dn_sent, dn_own = call(
        functools.partial(input_back_kernel, wz_at, wx_at),
        "input_backward",
        32,
        steps,
        [block(width, turned), block(cols + LANES, turned)]
        + [anywhere] * (len(wz) + len(wx)),
        [(lead_r, half_shape), (trail_r, half_shape)],
        [
            pltpu.VMEM((dim, width), bf16), pltpu.VMEM((dim, cols + LANES), bf16),
            pltpu.VMEM((R, dim), bf16), copies(wz_at), copies(wx_at),
        ],
        info, ggate, gx, *wz, *wx,
    )
    if direct(size, rows):
        sent_x, dn_own, dn_sent = lax.optimization_barrier((sent_x, dn_own, dn_sent))
    dn_oth = swap(dn_sent, 1, "tensor")
    if direct(size, rows):
        total_x = sum_pieces(sent_x)
        far_x = scatter_far(total_x, rows, both_parts(total_x))
        far_zo, dn_oth, dn_own = lax.optimization_barrier((far_zo, dn_oth, dn_own))
        sum_zo = sum_pieces(far_zo)

    dspec = rows_spec(L, dim)
    block_out, grad_resid = call(
        lambda info, *refs: finish_kernel(*refs),
        "finish",
        12,
        half,
        [dspec, dspec, full((16, cols)), dspec, dspec, dspec, dspec],
        [(dspec, half_shape), (dspec, shape((half_rows, dim), f32))],
        [],
        info, resid, cotangent, consts, dn_own, dn_oth, branch_own, branch_oth,
    )

    if direct(size, rows):
        block_out, grad_resid, far_x, grad_w_z, grad_w_out = lax.optimization_barrier(
            (block_out, grad_resid, far_x, sum_zo[:, :width], sum_zo[:, width:].T)
        )
        sum_x = sum_pieces(far_x)
        small = sum_x[rows:]
    else:
        sum_zo = scatter_whole(sent_zo[0], bits)
        grad_w_z, grad_w_out = sum_zo[:, :width], sum_zo[:, width:].T
        sum_x = scatter_whole(gw_x[0], bits)
        for bit in bits:
            small = small + swap(small, bit, "dp")
    grad_w_bc = sum_x[:rows, width:cols]
    pair = jnp.concatenate(
        [grad_w_bc.reshape(-1), small[:5, width:cols].reshape(-1), small[7, :dim]]
    )
    pair = pair + swap(pair, 1, "tensor")
    grad_w_bc, bc_g, gain_g = jnp.split(pair, [rows * 2 * NS, (rows + 5) * 2 * NS])
    bc_g = bc_g.reshape(5, 2 * NS)
    return (
        block_out, grad_resid, gain_g / gain_in, grad_w_z, sum_x[:rows, :width],
        grad_w_bc.reshape(rows, 2 * NS), sum_x[:rows, cols : cols + heads],
        small[:4, :width], small[4, :width], bc_g[:4], bc_g[4], small[0, cols : cols + heads],
        small[1, cols : cols + heads], small[5, :width].reshape(heads, HEAD).sum(axis=1),
        small[6, :width], grad_w_out,
    )


def solution(mesh):
    in_specs = (
        P(("dp", "tensor"), None),
        P(),
        P("dp", "tensor"),
        P("dp", "tensor"),
        P("dp", None),
        P("dp", "tensor"),
        P(None, "tensor"),
        P("tensor"),
        P(),
        P(),
        P("tensor"),
        P("tensor"),
        P("tensor"),
        P("tensor"),
        P("tensor", "dp"),
        P(("dp", "tensor"), None),
    )
    out_specs = (
        P(("dp", "tensor"), None),
        P(("dp", "tensor"), None),
        P(),
        P("dp", "tensor"),
        P("dp", "tensor"),
        P("dp", None),
        P("dp", "tensor"),
        P(None, "tensor"),
        P("tensor"),
        P(),
        P(),
        P("tensor"),
        P("tensor"),
        P("tensor"),
        P("tensor"),
        P("tensor", "dp"),
    )
    return jax.shard_map(local, mesh=mesh, in_specs=in_specs, out_specs=out_specs, check_vma=False)
```
